32 devices in a mesh: dp: 4 (over x, core), fsdp: 8 (over z, y).
Axes of the slice: x: 2, y: 2, z: 4, core: 2. Of those that a mesh axis runs over, the one named last changes fastest.
Arguments:
- inputs: float32 [96, 512, 512], P(('dp', 'fsdp')), may hold values from -6 to 6
- cotangent: float32 [96, 512, 512], P(('dp', 'fsdp')), may hold values from -6 to 6
- segment_ids: int32 [96, 512], P(('dp', 'fsdp')), may hold values from 0 to 24, as said below
- expert_ids: int32 [96, 512, 2], P(('dp', 'fsdp')), may hold values from 0 to 7, as said below
- overflow: int32 [96, 512, 2], P(('dp', 'fsdp')), may hold values from 0 to 1, as said below
- norm1_gain: float32 [512], P(('dp', 'fsdp')), may hold values from 0.5 to 1.5
- router_weight: float32 [512, 8], P(('dp', 'fsdp')), may hold values from -0.1875 to 0.1875
- query_weight: float32 [512, 512], P(('dp', 'fsdp')), may hold values from -0.375 to 0.375
- key_value_weight: float32 [512, 128], P(('dp', 'fsdp')), may hold values from -0.25 to 0.25
- output_weight: float32 [512, 512], P(('dp', 'fsdp')), may hold values from -15 to 15
- norm2_gain: float32 [512], P(('dp', 'fsdp')), may hold values from 0.5 to 1.5
- up_weight: float32 [512, 2048], P(('dp', 'fsdp')), may hold values from -0.25 to 0.25
- up_bias: float32 [2048], P(('dp', 'fsdp')), may hold values from -3 to 3
- down_weight: float32 [2048, 512], P(('dp', 'fsdp')), may hold values from -0.1875 to 0.1875
Outputs:
- layer_output: float32 [96, 512, 512], P(('dp', 'fsdp'))
- input_grad: float32 [96, 512, 512], P(('dp', 'fsdp'))
- norm1_gain_grad: float32 [512], P(('dp', 'fsdp'))
- router_weight_grad: float32 [512, 8], P(('dp', 'fsdp'))
- query_weight_grad: float32 [512, 512], P(('dp', 'fsdp'))
- key_value_weight_grad: float32 [512, 128], P(('dp', 'fsdp'))
- output_weight_grad: float32 [512, 512], P(('dp', 'fsdp'))
- norm2_gain_grad: float32 [512], P(('dp', 'fsdp'))
- up_weight_grad: float32 [512, 2048], P(('dp', 'fsdp'))
- up_bias_grad: float32 [2048], P(('dp', 'fsdp'))
- down_weight_grad: float32 [2048, 512], P(('dp', 'fsdp'))
The draws below stay inside these ranges and needn't reach their ends.
Inputs may be any that keep to these rules, and one draw needn't show every extreme that they name: `segment_ids`: ids start at 0 in each row and rise by one at each sentence boundary; every sentence has 16 to 128 tokens except the last of a row, which may be shorter; the first sentence of each row has exactly 128 tokens; some row reaches the largest id. `expert_ids`: A token's two experts differ; loads lean heavily on two experts chosen by the seed. Within each aligned block of 3 rows, pairs taken in token order (a token's first choice before its second), a pair has overflow 1 exactly when at least 480 earlier pairs of the block name the same expert; in every block some expert fills its 480 slots.
All inputs are finite; a program needn't handle non-finite values.
Results may differ from the reference program's by a relative error of at most 0.012.
The reference program's roundings to bfloat16 on the way count: a program that leaves them out, or rounds other values in their place, can miss the bound.
Values may be sent and summed in bfloat16 or wider, within the bound.
A program may use at most 192 MiB of HBM per device.

```python
import jax
import jax.numpy as jnp
from jax import lax

D = 512
E = 8
TOP = 2
DH = 64
FF = 2048
SENT = 128
ROW = 512
ROWS_DEV = 3
ROWS = 96
CAP = 480


def draw_segment_ids(key, part):
    sub = jax.random.fold_in(key, 11)
    shortest = SENT // 8
    lengths = jax.random.randint(sub, (ROWS, ROW // shortest), shortest, SENT + 1)
    first_row = (jnp.arange(ROWS, dtype=jnp.int32) == 0)[:, None]
    lengths = jnp.where(first_row, jnp.int32(shortest), lengths.astype(jnp.int32))
    lengths = jnp.concatenate([jnp.full((ROWS, 1), SENT, jnp.int32), lengths[:, 1:].astype(jnp.int32)], axis=1)
    ends = jnp.cumsum(lengths, axis=1)
    places = jnp.arange(ROW, dtype=jnp.int32)
    return jnp.sum((ends[:, None, :] <= places[None, :, None]).astype(jnp.int32), axis=2).astype(jnp.int32)


def routing(key):
    sub = jax.random.fold_in(key, 23)
    keys = jax.random.split(sub, 5)
    order = jax.random.permutation(keys[0], E)
    favourite = order[0]
    runner_up = order[1]
    pick = jax.random.randint(keys[1], (ROWS, ROW), 0, 16)
    others = order[2 + jax.random.randint(keys[2], (ROWS, ROW), 0, E - 2)]
    first = jnp.where(pick < 6, favourite, jnp.where(pick < 11, runner_up, others))
    coin = jax.random.randint(keys[3], (ROWS, ROW), 0, 2)
    offset = jax.random.randint(keys[4], (ROWS, ROW), 1, E)
    leaning = jnp.where(first == favourite, runner_up, favourite)
    second = jnp.where(coin == 0, leaning, (first + offset) % E)
    picked = jnp.stack([first, second], axis=-1).astype(jnp.int32)
    pairs = picked.reshape(ROWS // ROWS_DEV, ROWS_DEV * ROW * TOP)
    hits = (pairs[:, :, None] == jnp.arange(E, dtype=jnp.int32)[None, None, :]).astype(jnp.int32)
    earlier = jnp.cumsum(hits, axis=1) - hits
    ranks = jnp.sum(earlier * hits, axis=2)
    spilled = (ranks >= CAP).astype(jnp.int32).reshape(ROWS, ROW, TOP)
    return (picked, spilled)


def draw_expert_ids(key, part):
    return routing(key)[0]


def draw_overflow(key, part):
    return routing(key)[1]


def spiked(drawn, stream_key, source, target, shards_of, factor):
    owner, partner = [(jnp.arange(drawn.shape[dim]) // (drawn.shape[dim] // shards_of)).reshape([-1 if axis == dim else 1 for axis in range(drawn.ndim)]) for dim in (source, target)]
    chosen = jax.random.permutation(stream_key, shards_of)[partner]
    strong = (owner == chosen) | (owner == (partner + shards_of // 2) % shards_of)
    return jnp.where(strong, factor * drawn, drawn)


def steps_of(rng, shape, pieces, least, high):
    level, own = 1.0, jax.random.fold_in(rng, 6)
    for dim, blocks in pieces:
        heights = jnp.exp(jax.random.uniform(jax.random.fold_in(own, dim), (blocks,), jnp.float32, least / len(pieces), high / len(pieces)))
        level = level * jnp.repeat(heights, shape[dim] // blocks).reshape([-1 if axis == dim else 1 for axis in range(len(shape))])
    return level


def normal_values(rng, dims, scale, bound, cuts=(), held_as=jnp.bfloat16):
    entries = jax.random.normal(rng, dims, jnp.float32) * scale
    if len(cuts) > 0:
        entries = steps_of(rng, dims, cuts, -0.22, 0.18) * entries
    return jnp.clip(entries, min=-bound, max=bound).astype(held_as)


def bell_draw_with(own_key, dims, width, limit, shards, heavy, held_as=jnp.bfloat16):
    entries = width * jax.random.normal(own_key, dims, jnp.float32)
    if shards:
        entries = entries * steps_of(own_key, dims, shards, -0.22, 0.18)
    return jnp.clip(spiked(entries, jax.random.fold_in(own_key, 3), *heavy), -limit, limit).astype(held_as)


def setup_inputs(seed: int = 0) -> dict:
    key_list = jax.random.split(jax.random.key(seed), 15)
    inputs = normal_values(key_list[0], (ROWS, ROW, D), 1.0, 6.0, ((0, 32),), jnp.float32)
    cotangent = bell_draw_with(key_list[1], (ROWS, ROW, D), 1.0, 6.0, ((0, 32),), (0, 2, 32, 2.75), jnp.float32)
    segment_ids = draw_segment_ids(jax.random.fold_in(key_list[14], 71), 0)
    expert_ids = draw_expert_ids(jax.random.fold_in(key_list[14], 71), 0)
    overflow = draw_overflow(jax.random.fold_in(key_list[14], 71), 0)
    norm1_gain = jnp.clip(1.0 + 0.1 * jax.random.normal(key_list[5], (D,), jnp.float32), 0.5, 1.5)
    router_weight = normal_values(key_list[6], (D, E), (2 * D) ** -0.5, 0.1875, ((0, 32),), jnp.float32)
    query_weight = normal_values(key_list[7], (D, E * DH), (D // 2) ** -0.5, 0.375, ((0, 32),), jnp.float32)
    key_value_weight = normal_values(key_list[8], (D, 2 * DH), D ** -0.5, 0.25, ((0, 32),), jnp.float32)
    output_weight = normal_values(key_list[9], (E * DH, D), 2.5, 15.0, ((0, 32),), jnp.float32)
    norm2_gain = jnp.clip(1.0 + 0.1 * jax.random.normal(key_list[10], (D,), jnp.float32), 0.5, 1.5)
    up_weight = normal_values(key_list[11], (D, FF), D ** -0.5, 0.25, ((0, 32),), jnp.float32)
    up_bias = normal_values(key_list[12], (FF,), 0.5, 3.0, ((0, 32),), jnp.float32)
    down_weight = normal_values(key_list[13], (FF, D), (FF // 2) ** -0.5, 0.1875, ((0, 32),), jnp.float32)
    return dict(inputs=inputs, cotangent=cotangent, segment_ids=segment_ids, expert_ids=expert_ids, overflow=overflow, norm1_gain=norm1_gain, router_weight=router_weight, query_weight=query_weight, key_value_weight=key_value_weight, output_weight=output_weight, norm2_gain=norm2_gain, up_weight=up_weight, up_bias=up_bias, down_weight=down_weight)


EPS = 1e-05
HIGH = lax.Precision.HIGHEST
BIG = -1e+30
GELU_C = 0.7978845608028654
GELU_K = 0.044715

@jax.custom_vjp
def low(v):
    return lax.optimization_barrier(v.astype(jnp.bfloat16)).astype(jnp.float32)

@jax.custom_vjp
def low_back(v):
    return v

def low_keep(v):
    return (low(v), None)

def low_pass(kept, grad):
    return (grad,)

def back_keep(v):
    return (v, None)

def back_low(kept, grad):
    return (low(grad),)
low.defvjp(low_keep, low_pass)
low_back.defvjp(back_keep, back_low)

def matmul(left, right):
    return jnp.dot(left, right, precision=HIGH, preferred_element_type=jnp.float32)

def gelu_tanh(values):
    return 0.5 * values * (1.0 + jnp.tanh(GELU_C * (values + GELU_K * values * values * values)))

def layer_norm(rows, norm_scale):
    row_average = lax.optimization_barrier(jnp.mean(rows, axis=-1, keepdims=True))
    centred = rows - row_average
    return centred * lax.rsqrt(lax.optimization_barrier(jnp.mean(centred * centred, axis=-1, keepdims=True)) + EPS) * norm_scale

def attend_row(block):
    query, key, value, segs = block
    heads = query.reshape(ROW, E, DH)
    scores = jnp.einsum('qed,kd->eqk', heads, key, precision=HIGH) * DH ** (-0.5)
    scores = low_back(scores)
    same = (segs[:, None] == segs[None, :])[None]
    scores = jnp.where(same, scores, BIG)
    probs = low(jax.nn.softmax(scores, axis=-1))
    out = jnp.einsum('eqk,kd->qed', probs, value, precision=HIGH)
    return out.reshape(ROW, E * DH)

def layer(token_rows, segs, route, norm1_gain, router_weight, query_weight, key_value_weight, output_weight, norm2_gain, up_weight, up_bias, down_weight):
    rows = segs.shape[0]
    flat = token_rows.reshape(-1, D)
    normalized_input = low(layer_norm(flat, low(norm1_gain)))
    router_prob = jax.nn.softmax(matmul(normalized_input, low(router_weight)), axis=-1)
    query = low(low_back(matmul(normalized_input, low(query_weight))))
    paired = low(low_back(matmul(normalized_input, low(key_value_weight))))
    heads = lax.map(jax.checkpoint(attend_row), (query.reshape(rows, ROW, E * DH), paired[:, :DH].reshape(rows, ROW, DH), paired[:, DH:].reshape(rows, ROW, DH), segs))
    heads = low_back(heads.reshape(-1, E, DH))
    mixed = low((heads * (router_prob * route)[:, :, None]).reshape(-1, E * DH))
    residual_input = flat + low_back(matmul(mixed, low(output_weight)))
    second_normalized_input = low(layer_norm(residual_input, low(norm2_gain)))
    pre = low_back(matmul(second_normalized_input, low(up_weight)) + low(up_bias))
    hidden = low(gelu_tanh(pre))
    result = residual_input + low_back(matmul(hidden, low(down_weight)))
    return result.reshape(token_rows.shape)

def reference(inputs, cotangent, segment_ids, expert_ids, overflow, norm1_gain, router_weight, query_weight, key_value_weight, output_weight, norm2_gain, up_weight, up_bias, down_weight):
    params = (norm1_gain, router_weight, query_weight, key_value_weight, output_weight, norm2_gain, up_weight, up_bias, down_weight)
    hits = (expert_ids[..., None] == jnp.arange(E, dtype=jnp.int32)) & (overflow == 0)[..., None]
    route = lax.optimization_barrier(jnp.sum(jnp.where(hits, jnp.float32(1.0), jnp.float32(0.0)), axis=-2))
    groups = ROWS // ROWS_DEV

    def split(array):
        return array.reshape((groups, ROWS_DEV) + array.shape[1:])

    def step(totals, block):
        token_rows, grad_out, segs, route_block = block

        def forward(tok, *weights):
            return layer(tok, segs, route_block.reshape(-1, E), *weights)
        result, pull = jax.vjp(forward, token_rows, *params)
        grads = pull(grad_out)
        return (tuple((t + g for t, g in zip(totals, grads[1:]))), (result, grads[0]))
    init = tuple((jnp.zeros(p.shape, jnp.float32) for p in params))
    totals, (outputs, input_grads) = lax.scan(step, init, (split(inputs), split(cotangent), split(segment_ids), split(route)))
    return (outputs.reshape(inputs.shape), input_grads.reshape(inputs.shape), totals[0], totals[1], totals[2], totals[3], totals[4], totals[5], totals[6], totals[7], totals[8])
```

```python
import functools
import jax
import jax.numpy as jnp
from jax import lax
from jax.experimental import pallas as pl
from jax.experimental.pallas import tpu as pltpu
from jax.sharding import PartitionSpec as P

EPS = 1e-05
BIG = -1e30
GELU_C = 0.7978845608028654
GELU_K = 0.044715
BF = jnp.bfloat16
F32 = jnp.float32
AXES = ("dp", "fsdp")
CQ, CKV, CR, CO, CU, CW = 0, 512, 640, 768, 1280, 3328
TILES = ((0, 128, 0), (128, 256, 256), (128, 384, 768), (256, 256, 1536))


def nn(a, b):
    return lax.dot_general(a, b, (((1,), (0,)), ((), ())), preferred_element_type=F32)


def nt(a, b):
    return lax.dot_general(a, b, (((1,), (1,)), ((), ())), preferred_element_type=F32)


def tn(a, b):
    return lax.dot_general(a, b, (((0,), (0,)), ((), ())), preferred_element_type=F32)


def split(v):
    high = v.astype(BF)
    return high, (v - high.astype(F32)).astype(BF)


def lanes(shape):
    return lax.broadcasted_iota(jnp.int32, shape, len(shape) - 1)


def rows_of(shape):
    return lax.broadcasted_iota(jnp.int32, shape, len(shape) - 2)


def one_where(mask):
    return jnp.where(mask, 1.0, 0.0).astype(BF)


def norm(v):
    centred = v - jnp.mean(v, axis=-1, keepdims=True)
    inverse = lax.rsqrt(jnp.mean(centred * centred, axis=-1, keepdims=True) + EPS)
    return centred * inverse, inverse


def norm_back(grad, xhat, inverse, gain):
    scaled = grad * gain
    inner = (
        scaled
        - jnp.mean(scaled, axis=-1, keepdims=True)
        - xhat * jnp.mean(scaled * xhat, axis=-1, keepdims=True)
    )
    return inner * inverse


def gelu_both(x):
    square = x * x
    slope = (GELU_C * GELU_K) * square + GELU_C
    half = 0.5 * jnp.tanh(x * slope) + 0.5
    value = x * half
    return value, half + (value - value * half) * (6.0 * slope - 4.0 * GELU_C)


def stack_pairs(v):
    return jnp.concatenate([v[:, 128 * p : 128 * p + 128] for p in range(4)], axis=0)


class Plan:
    pass


def keys_of(s, win):
    kv, vk = s.kv[win, :], s.vk[win, :]
    low, zero = lanes(kv.shape) < 64, jnp.zeros_like(kv)
    return jnp.concatenate([jnp.where(low, kv, zero), jnp.where(low, zero, vk)], axis=0)


def values_of(s, win, extra_e, extra_o):
    kv, vk = s.kv[win, :], s.vk[win, :]
    low, zero = lanes(kv.shape) < 64, jnp.zeros_like(kv)
    even = jnp.concatenate([jnp.where(low, vk, zero), extra_e], axis=1)
    odd = jnp.concatenate([jnp.where(low, zero, kv), extra_o], axis=1)
    return jnp.concatenate([even, odd], axis=0)


def phase_norm1(s, r):
    rows = pl.ds(r * 512, 512)
    xhat, inverse = norm(s.x[rows, :])
    s.xh1[rows, :] = xhat
    s.route[rows, :] = jnp.broadcast_to(inverse, (512, 128))


def phase_forward(s, r, hook=lambda i: None):
    rows = pl.ds(r * 512, 512)
    normed = (s.xh1[rows, :] * s.g1[...]).astype(BF)
    s.normed[rows, :] = normed
    proj = nn(normed, s.weight(CQ, CO))
    query = proj[:, :512].astype(BF)
    s.q[rows, :] = query
    pair = proj[:, CKV:CR].astype(BF).astype(F32)
    swapped = pltpu.roll(pair, 64, 1)
    low = lanes((512, 128)) < 64
    s.kv[rows, :] = jnp.where(low, pair * 0.125, pair).astype(BF)
    s.vk[rows, :] = jnp.where(low, swapped, swapped * 0.125).astype(BF)
    lane = lanes((512, 128))
    logits = jnp.where(lane < 8, proj[:, CR:CO], BIG)
    top = jnp.max(logits, axis=-1, keepdims=True)
    weights = jnp.exp(logits - top)
    prob = weights / jnp.sum(weights, axis=-1, keepdims=True)
    s.prob[rows, :] = prob
    s.small[0:2, :] = jnp.where(s.over[r] == 0, s.ids[r], -1).astype(F32)
    s.small[2:3, :] = s.segs[pl.ds(r, 1), :].astype(F32)
    columns = s.small[...].T
    lane_f = lane.astype(F32)
    route = jnp.where(lane_f == columns[:, 0:1], 1.0, 0.0) + jnp.where(
        lane_f == columns[:, 1:2], 1.0, 0.0
    )
    s.route[rows, :] = jnp.where(lane == 8, s.route[rows, :], route)
    seg_row = s.small[2:3, :]
    hook(0)
    for t, (start, width, at) in enumerate(TILES):
        q4 = stack_pairs(query[128 * t : 128 * t + 128])
        win = pl.ds(r * 512 + start, width)
        scores = nt(q4, keys_of(s, win))
        even, odd = scores[:, :width], scores[:, width:]
        if t:
            same = columns[128 * t : 128 * t + 128, 2:3] == seg_row[:, start : start + width]
            bias = jnp.where(same, 0.0, BIG)
            bias = jnp.concatenate([bias] * 4, axis=0)
            even, odd = even + bias, odd + bias
        even = jnp.exp(even - jnp.max(even, axis=-1, keepdims=True)).astype(BF)
        odd = jnp.exp(odd - jnp.max(odd, axis=-1, keepdims=True)).astype(BF)
        both = jnp.concatenate([even, odd], axis=1)
        s.pu[pl.ds(r * 512, 512), at : at + 2 * width] = both
        low_w = lanes((width, 128)) < 64
        one_e = jnp.where(low_w, 1.0, 0.0).astype(BF)
        one_o = jnp.where(low_w, 0.0, 1.0).astype(BF)
        out = nn(both, values_of(s, win, one_e, one_o))
        inverse = 1.0 / out[:, 128:]
        out = out[:, :128] * inverse
        for p in range(4):
            at_rows = pl.ds(r * 512 + 128 * t, 128)
            s.heads[at_rows, 128 * p : 128 * p + 128] = out[128 * p : 128 * p + 128]
            s.pinv[at_rows, 128 * p : 128 * p + 128] = inverse[128 * p : 128 * p + 128]
        hook(1 + t)
    mixed = (s.heads[rows, :] * expand(prob * route)).astype(BF)
    s.mixed[rows, :] = mixed
    hook(5)


def phase_resid(s, r):
    rows = pl.ds(r * 512, 512)
    resid = s.x[rows, :] + nn(s.mixed[rows, :], s.weight(CO, CU))
    s.x[rows, :] = resid
    xhat, inverse = norm(resid)
    s.xh2[rows, :] = xhat
    s.route[rows, :] = jnp.where(lanes((512, 128)) == 9, inverse, s.route[rows, :])
    s.normed2[rows, :] = (xhat * s.g2[...]).astype(BF)
    s.dffn[rows, :] = s.cot[rows, :].astype(BF)


def expand(per_expert):
    high, rest = split(per_expert)
    spread = one_where(
        jnp.bitwise_and(rows_of((256, 512)), 127) == jnp.right_shift(lanes((256, 512)), 6)
    )
    return nn(jnp.concatenate([high, rest], axis=1), spread)


def phase_ffn(s, c, r):
    rows = pl.ds(r * 512, 512)
    up = s.weight(CU + 512 * c, CU + 512 * c + 512)
    down = s.down(c)
    pre = nn(s.normed2[rows, :], up) + s.bias[:, 512 * c : 512 * c + 512]
    dhidden = nt(s.dffn[rows, :], down)
    value, slope = gelu_both(pre)
    dpre = dhidden * slope
    s.biasg[:, 512 * c : 512 * c + 512] += jnp.sum(dpre, axis=0, keepdims=True)
    hidden = value.astype(BF)
    dpre = dpre.astype(BF)
    s.hidden[rows, :] = hidden
    s.dpre[rows, :] = dpre
    s.x[rows, :] += nn(hidden, down)
    back = nt(dpre, up)
    if c == 0:
        s.dn2[rows, :] = back
    else:
        s.dn2[rows, :] += back


def phase_ffn_grads(s, c):
    s.put_down(c, tn(s.hidden[...], s.dffn[...]))
    s.put(CU + 512 * c, tn(s.normed2[...], s.dpre[...]))


def phase_back(s, r, hook=lambda i: None):
    rows = pl.ds(r * 512, 512)
    grad = s.dn2[rows, :]
    xhat = s.xh2[rows, :]
    s.gaing[1:2, :] += jnp.sum(grad * xhat, axis=0, keepdims=True)
    dresid = s.cot[rows, :] + norm_back(grad, xhat, s.route[rows, 9:10], s.g2[...])
    s.dn2[rows, :] = dresid
    dbranch = dresid.astype(BF)
    s.dbranch[rows, :] = dbranch
    dmixed = nt(dbranch, s.weight(CO, CU))
    heads = s.heads[rows, :]
    gather = one_where(
        lanes((1024, 128)) == jnp.right_shift(jnp.bitwise_and(rows_of((1024, 128)), 511), 6)
    )
    dgate = nn(jnp.concatenate(split(dmixed * heads), axis=1), gather)
    prob, route = s.prob[rows, :], s.route[rows, :]
    gated = dgate * route
    dlogits = prob * (gated - jnp.sum(prob * gated, axis=-1, keepdims=True))
    s.dkr[rows, 128:256] = dlogits.astype(BF)
    dout = (dmixed * expand(prob * route) * s.pinv[rows, :]).astype(BF)
    s.dout[...] = dout
    within = dout.astype(F32) * heads
    high, rest = split(within)
    block = one_where(
        jnp.right_shift(jnp.bitwise_and(rows_of((256, 128)), 127), 6)
        == jnp.right_shift(lanes((256, 128)), 6)
    )
    place = jnp.bitwise_and(lanes((512, 128)), 63)
    for p in range(4):
        cols = slice(128 * p, 128 * p + 128)
        total = nn(jnp.concatenate([high[:, cols], rest[:, cols]], axis=1), block)
        first, second = split(total)
        s.delta[:, cols] = jnp.where(
            place == 0, first.astype(F32), jnp.where(place == 1, second.astype(F32), 0.0)
        ).astype(BF)
    s.dkv[...] = jnp.zeros_like(s.dkv)
    hook(0)
    for t, (start, width, at) in enumerate(TILES):
        here = pl.ds(128 * t, 128)
        at_rows = pl.ds(r * 512 + 128 * t, 128)
        win = pl.ds(r * 512 + start, width)
        do4 = stack_pairs(s.dout[here, :])
        de4 = stack_pairs(s.delta[here, :])
        lane = lanes((width, 128))
        neg_e = jnp.where(lane < 2, -1.0, 0.0).astype(BF)
        neg_o = jnp.where(jnp.bitwise_and(lane, 126) == 64, -1.0, 0.0).astype(BF)
        dprob = nt(jnp.concatenate([do4, de4], axis=1), values_of(s, win, neg_e, neg_o))
        weights = s.pu[pl.ds(r * 512, 512), at : at + 2 * width]
        dscore = (weights.astype(F32) * dprob).astype(BF)
        dq4 = nn(dscore, keys_of(s, win)).astype(BF)
        q4 = stack_pairs(s.q[at_rows, :])
        dk = tn(dscore, q4)
        dv = tn(weights, do4)
        for p in range(4):
            s.q[at_rows, 128 * p : 128 * p + 128] = dq4[128 * p : 128 * p + 128]
        s.dkv[pl.ds(start, width), :] += jnp.where(
            lane < 64,
            (dk[:width] + pltpu.roll(dk[width:], 64, 1)) * 0.125,
            dv[width:] + pltpu.roll(dv[:width], 64, 1),
        )
        if t < 3:
            hook(1 + t)
    s.dkr[rows, 0:128] = s.dkv[...].astype(BF)
    hook(4)


def phase_input(s, r):
    rows = pl.ds(r * 512, 512)
    dproj = jnp.concatenate([s.q[rows, :], s.dkr[rows, :]], axis=1)
    grad = nt(dproj, s.weight(CQ, CO))
    xhat = s.xh1[rows, :]
    s.gaing[0:1, :] += jnp.sum(grad * xhat, axis=0, keepdims=True)
    s.dn2[rows, :] += norm_back(grad, xhat, s.route[rows, 8:9], s.g1[...])


def local_kernel(
    x_in, cot_in, segs, ids, over, g1, g2, bias, wa, wd,
    out_y, out_dx, out_ga, out_gd, out_small, out_bias,
    x, cot, xh1, xh2, heads, pinv, dn2, normed, q, mixed, normed2, dffn, hidden, dpre,
    kv, vk, prob, route, pu, block, small, gaing, biasg, sem,
):
    s = Plan()
    s.x, s.cot, s.xh1, s.xh2, s.heads, s.pinv, s.dn2 = x, cot, xh1, xh2, heads, pinv, dn2
    s.normed, s.q, s.mixed, s.normed2, s.dffn, s.hidden, s.dpre = normed, q, mixed, normed2, dffn, hidden, dpre
    s.kv, s.vk, s.prob, s.route, s.pu, s.dkv = kv, vk, prob, route, pu, block
    s.small, s.gaing, s.biasg, s.segs, s.ids, s.over = small, gaing, biasg, segs, ids, over
    s.g1, s.g2, s.bias = g1, g2, bias
    s.dbranch = s.dffn
    s.dkr = hidden.at[:, 0:256]
    s.dout, s.delta = dpre.at[0:512, :], dpre.at[512:1024, :]
    s.weight = lambda a, b: wa[:, a:b]
    s.down = lambda c: wd[512 * c : 512 * c + 512, :]

    def put(at, value):
        out_ga[:, at : at + value.shape[1]] = value.astype(BF)

    def put_down(c, value):
        out_gd[512 * c : 512 * c + 512, :] = value.astype(BF)

    s.put, s.put_down = put, put_down
    copies = [pltpu.make_async_copy(x_in, x, sem.at[0]), pltpu.make_async_copy(cot_in, cot, sem.at[1])]
    for copy in copies:
        copy.start()
    small[...] = jnp.zeros_like(small)
    gaing[...] = jnp.zeros_like(gaing)
    biasg[...] = jnp.zeros_like(biasg)
    for copy in copies:
        copy.wait()
    nrows = x.shape[0] // 512

    def each(phase):
        lax.fori_loop(0, nrows, lambda r, _: (phase(r), 0)[1], 0)

    each(lambda r: phase_norm1(s, r))
    each(lambda r: phase_forward(s, r))
    each(lambda r: phase_resid(s, r))
    for c in range(4):
        each(lambda r: phase_ffn(s, c, r))
        phase_ffn_grads(s, c)
    finish = pltpu.make_async_copy(x, out_y, sem.at[2])
    finish.start()
    each(lambda r: phase_back(s, r))
    put(CO, tn(mixed[...], s.dbranch[...]))
    put(CQ, tn(normed[...], q[...]))
    put(CKV, tn(normed[...], s.dkr[...]))
    each(lambda r: phase_input(s, r))
    last = pltpu.make_async_copy(dn2, out_dx, sem.at[3])
    last.start()
    out_small[...] = gaing[...]
    out_bias[...] = biasg[...]
    finish.wait()
    last.wait()


def scratch(tokens):
    f = lambda *shape: pltpu.VMEM(shape, F32)
    b = lambda *shape: pltpu.VMEM(shape, BF)
    t = tokens
    return (
        [f(t, 512)] * 7 + [b(t, 512)] * 7 + [b(t, 128)] * 2
        + [f(t, 128), f(t, 128), b(t, 2048), f(512, 128)]
        + [f(8, 512), f(8, 512), f(1, 2048)]
    )


MESH = pl.DeviceIdType.MESH


class Ring:
    def __init__(self):
        self.d = lax.axis_index("dp")
        self.f = lax.axis_index("fsdp")
        self.x, self.c = jnp.right_shift(self.d, 1), jnp.bitwise_and(self.d, 1)
        self.z, self.y = jnp.right_shift(self.f, 1), jnp.bitwise_and(self.f, 1)
        self.ox, self.oc, self.oy = 1 - self.x, 1 - self.c, 1 - self.y
        self.core_peer = (2 * self.x + self.oc, self.f)
        self.x_peer = (2 * self.ox + self.c, self.f)
        self.y_peer = (self.d, 2 * self.z + self.oy)
        self.later = [jnp.bitwise_and(self.z + k, 3) for k in (1, 2, 3)]
        self.earlier = [jnp.bitwise_and(self.z - k + 4, 3) for k in (1, 2, 3)]
        self.z_peers = [(self.d, 2 * z + self.y) for z in self.later]


def remote(src, dst, send, recv, peer):
    return pltpu.make_async_remote_copy(
        src_ref=src, dst_ref=dst, send_sem=send, recv_sem=recv, device_id=peer, device_id_type=MESH
    )


class Gather:
    def __init__(self, ring, buf, kinds, send, recv):
        self.ring, self.buf, self.kinds, self.send, self.recv = ring, buf, kinds, send, recv
        self.all = slice(kinds[0][0], kinds[-1][1])

    def copies(self, k, arriving):
        g, b = self.ring, self.buf
        if k == 0:
            at = lambda z: b.at[g.x, g.c, z, g.y, :, self.all]
            moves = [(n, at(g.earlier[n] if arriving else g.z), g.z_peers[n]) for n in range(3)]
        elif k == 3:
            moves = [(7, b.at[:, g.oc if arriving else g.c, :, :, :, self.all], g.core_peer)]
        else:
            moves = []
            x, y = (g.ox, g.oy) if arriving else (g.x, g.y)
            for kind, (lo, hi) in enumerate(self.kinds):
                cols = slice(lo, hi)
                if k == 1:
                    if kind == 0:
                        moves.append((3, b.at[x, g.c, :, g.y, :, cols], g.x_peer))
                    else:
                        moves.append((4, b.at[g.x, g.c, :, y, :, cols], g.y_peer))
                elif kind == 0:
                    moves.append((5, b.at[:, g.c, :, y, :, cols], g.y_peer))
                else:
                    moves.append((6, b.at[x, g.c, :, :, :, cols], g.x_peer))
        return [remote(ref, ref, self.send.at[n], self.recv.at[n], peer) for n, ref, peer in moves]

    def step(self, k):
        if k > 0:
            for copy in self.copies(k - 1, True):
                copy.wait_recv()
        if k < 4:
            for copy in self.copies(k, False):
                copy.start()

    def finish(self):
        for k in range(4):
            for copy in self.copies(k, False):
                copy.wait_send()


class Reduce:
    def __init__(self, ring, buf, kinds, send, recv, landing, write):
        self.ring, self.buf, self.kinds, self.send, self.recv = ring, buf, kinds, send, recv
        self.first, self.halves, self.quarters, self.last = landing
        self.all = slice(kinds[0][0], kinds[-1][1])
        self.write = write

    def copies(self, k):
        g, b = self.ring, self.buf
        if k == 0:
            moves = [(0, b.at[:, g.oc, :, :, :, self.all], self.first, g.core_peer)]
        elif k == 3:
            moves = [
                (5 + n, b.at[g.x, g.c, g.later[n], g.y, :, self.all], self.last.at[n], g.z_peers[n])
                for n in range(3)
            ]
        else:
            moves = []
            for kind, (lo, hi) in enumerate(self.kinds):
                cols = slice(lo, hi)
                if k == 1:
                    if kind == 0:
                        moves.append((1, b.at[:, g.c, :, g.oy, :, cols], self.halves[0], g.y_peer))
                    else:
                        moves.append((2, b.at[g.ox, g.c, :, :, :, cols], self.halves[1], g.x_peer))
                elif kind == 0:
                    moves.append((3, b.at[g.ox, g.c, :, g.y, :, cols], self.quarters[0], g.x_peer))
                else:
                    moves.append((4, b.at[g.x, g.c, :, g.oy, :, cols], self.quarters[1], g.y_peer))
        return [remote(src, dst, self.send.at[n], self.recv.at[n], peer) for n, src, dst, peer in moves]

    def add(self, k):
        g, b = self.ring, self.buf
        if k == 0:
            b[:, g.c, :, :, :, self.all] += self.first[...]
        elif k == 3:
            total = b[g.x, g.c, g.z, g.y, :, self.all].astype(F32)
            for n in range(3):
                total = total + self.last[n].astype(F32)
            self.write(total)
        else:
            for kind, (lo, hi) in enumerate(self.kinds):
                if k == 2:
                    b[g.x, g.c, :, g.y, :, lo:hi] += self.quarters[kind][...]
                elif kind == 0:
                    b[:, g.c, :, g.y, :, lo:hi] += self.halves[0][...]
                else:
                    b[g.x, g.c, :, :, :, lo:hi] += self.halves[1][...]

    def step(self, k):
        if k > 0:
            for copy in self.copies(k - 1):
                copy.wait_recv()
            self.add(k - 1)
        if k < 4:
            for copy in self.copies(k):
                copy.start()

    def finish(self):
        for k in range(4):
            for copy in self.copies(k):
                copy.wait_send()


def landing_shapes(rows, kinds):
    b = lambda *shape: pltpu.VMEM(shape, BF)
    n = kinds[-1][1] - kinds[0][0]
    shapes = [b(2, 4, 2, rows, n), b(3, rows, n)]
    for kind, (lo, hi) in enumerate(kinds):
        shapes.append(b(2, 4, rows, hi - lo) if kind == 0 else b(4, 2, rows, hi - lo))
        shapes.append(b(4, rows, hi - lo))
    return shapes


def halves(lo, hi, cut=None):
    cut = (lo + hi) // 2 if cut is None else cut
    return ((lo, cut), (cut, hi))


GATHERS = (
    ("P0", halves(CQ, CO)), ("P1", halves(CO, CU)), ("U0", halves(CU, CU + 1024)),
    ("D0", halves(0, 256)), ("D1", halves(256, 512)), ("U1", halves(CU + 1024, CW)),
)
REDUCES = (
    ("u0", halves(CU, CU + 512)), ("u1", halves(CU + 512, CU + 1024)),
    ("u2", halves(CU + 1024, CU + 1536)), ("u3", halves(CU + 1536, CW)),
    ("d0", halves(0, 256)), ("d1", halves(256, 512)), ("o", halves(CO, CU)),
    ("q", halves(CQ, CR, 384)), ("r", ((CR, CO),)),
)
SCHEDULE = {
    "go": (("P0", 0), ("P1", 0), ("U0", 0), ("D0", 0), ("D1", 0), ("U1", 0),),
    "P0": (("P0", 1), ("P0", 2), ("P1", 1), ("U0", 1), ("P0", 3), ("D0", 1), ("P1", 2), ("P0", 4),),
    "fwd0.0": (("U0", 2), ("D1", 1),),
    "fwd0.2": (("D0", 2),),
    "fwd0.3": (("P1", 3),),
    "fwd0.4": (("U1", 1),),
    "fwd1.1": (("P1", 4),),
    "fwd1.2": (("U0", 3),),
    "fwd1.4": (("D1", 2),),
    "fwd2.0": (("U0", 4),),
    "fwd2.3": (("D0", 3),),
    "res.0": (("U1", 2),),
    "U0": (("D0", 4), ("D1", 3), ("D1", 4),),
    "ffn0.0": (("U1", 3),),
    "ffn0.2": (("U1", 4),),
    "grads0": (("u0", 0),),
    "ffn1.1": (("u0", 1),),
    "grads1": (("u1", 0),),
    "ffn2.0": (("u0", 2),),
    "ffn2.1": (("u1", 1),),
    "ffn2.2": (("u0", 3),),
    "grads2": (("u2", 0),),
    "ffn3.0": (("u1", 2),),
    "ffn3.1": (("u2", 1), ("u0", 4),),
    "ffn3.2": (("u1", 3),),
    "grads3": (("u3", 0), ("d0", 0), ("d1", 0),),
    "back0.0": (("u2", 2),),
    "back0.1": (("u3", 1),),
    "back0.2": (("u1", 4),),
    "back0.3": (("d0", 1),),
    "back0.4": (("u2", 3), ("d1", 1),),
    "back1.0": (("u3", 2),),
    "back1.3": (("d0", 2), ("u2", 4),),
    "back2.1": (("d1", 2),),
    "back2.2": (("u3", 3),),
    "back2.3": (("d0", 3),),
    "og": (("o", 0), ("d1", 3),),
    "qg": (("q", 0), ("u3", 4),),
    "inp.0": (("o", 1),),
    "inp.2": (("q", 1),),
    "end": (("r", 0), ("d0", 4), ("r", 1), ("o", 2), ("d1", 4), ("q", 2), ("r", 2), ("o", 3), ("q", 3), ("r", 3), ("o", 4), ("q", 4), ("r", 4),),
}


def mega_kernel(
    x_in, cot_in, segs, ids, over, g1_in, g2_in, bias_in, router_in, q_in, kv_in, o_in, up_in, down_in,
    out_y, out_dx, out_g1, out_router, out_q, out_kv, out_o, out_g2, out_up, out_bias, out_down,
    x, cot, xh1, xh2, heads, pinv, dn2, normed, q, mixed, normed2, dffn, hidden, dpre,
    kv, vk, prob, route, pu, block, small, gaing, biasg,
    sem, wa, wd, ga, gd, g1, g2, bias, tiny, ag_send, ag_recv, rs_send, rs_recv, *landing,
):
    s = Plan()
    s.x, s.cot, s.xh1, s.xh2, s.heads, s.pinv, s.dn2 = x, cot, xh1, xh2, heads, pinv, dn2
    s.normed, s.q, s.mixed, s.normed2, s.dffn, s.hidden, s.dpre = normed, q, mixed, normed2, dffn, hidden, dpre
    s.kv, s.vk, s.prob, s.route, s.pu, s.dkv = kv, vk, prob, route, pu, block
    s.small, s.gaing, s.biasg, s.segs, s.ids, s.over = small, gaing, biasg, segs, ids, over
    s.g1, s.g2, s.bias = g1, g2, bias
    s.dbranch = s.dffn
    s.dkr = hidden.at[:, 0:256]
    s.dout, s.delta = dpre.at[0:512, :], dpre.at[512:1024, :]
    s.weight = lambda a, b: wa[:, :, :, :, :, a:b].reshape(512, b - a)
    s.down = lambda c: wd[c // 2, c % 2].reshape(512, 512)

    def put(at, value):
        n = value.shape[1]
        ga[:, :, :, :, :, at : at + n] = value.astype(BF).reshape(2, 2, 4, 2, 16, n)

    def put_down(c, value):
        gd[c // 2, c % 2] = value.astype(BF).reshape(4, 2, 64, 512)

    s.put, s.put_down = put, put_down
    g = Ring()
    copies = [pltpu.make_async_copy(x_in, x, sem.at[0]), pltpu.make_async_copy(cot_in, cot, sem.at[1])]
    for copy in copies:
        copy.start()
    peers = [g.core_peer, g.x_peer, g.y_peer] + g.z_peers
    barrier = pltpu.get_barrier_semaphore()
    for peer in peers:
        pl.semaphore_signal(barrier, inc=1, device_id=peer, device_id_type=MESH)

    wa[g.x, g.c, g.z, g.y, :, CQ:CKV] = q_in[...].astype(BF)
    wa[g.x, g.c, g.z, g.y, :, CKV:CR] = kv_in[...].astype(BF)
    wa[g.x, g.c, g.z, g.y, :, CO:CU] = o_in[...].astype(BF)
    wa[g.x, g.c, g.z, g.y, :, CU:CW] = up_in[...].astype(BF)
    wd[g.x, g.c, g.z, g.y] = down_in[...].astype(BF)
    tiny[...] = jnp.zeros_like(tiny)
    tiny[0:8, 0:16] = router_in[...]
    tiny[8:9, 0:16] = g1_in[...]
    tiny[9:10, 0:16] = g2_in[...]
    tiny[16:17, 0:64] = bias_in[...]
    turned = tn(
        tiny[0:16, :].astype(BF), one_where(rows_of((16, 128)) == lanes((16, 128)))
    )[0:16]
    shifted = nn(tiny[16:32, :].astype(BF), one_where(rows_of((128, 128)) + 64 == lanes((128, 128))))
    wa[g.x, g.c, g.z, g.y, :, CR:CO] = (turned + shifted).astype(BF)

    pl.semaphore_wait(barrier, len(peers))
    parts = {}
    for k, (name, kinds) in enumerate(GATHERS):
        parts[name] = Gather(g, wd if name[0] == "D" else wa, kinds, ag_send.at[k], ag_recv.at[k])

    def write_to(ref, at=0):
        def write(total):
            ref[:, at : at + total.shape[1]] = total

        return write

    def write_q(total):
        out_q[...] = total[:, :512]
        out_kv[...] = total[:, 512:]

    def write_small(total):
        turned = total.T
        out_router[...] = turned[0:8]
        out_g1[...] = turned[8:9]
        out_g2[...] = turned[9:10]
        out_bias[...] = pltpu.roll(total, 64, 1)[0:1, 0:64]

    writes = [write_to(out_up, 512 * k) for k in range(4)]
    writes += [write_to(out_down, 0), write_to(out_down, 256), write_to(out_o), write_q, write_small]
    spots = list(landing)
    for k, (name, kinds) in enumerate(REDUCES):
        first, last = spots.pop(0), spots.pop(0)
        halves_in, quarters_in = [], []
        for _ in kinds:
            halves_in.append(spots.pop(0))
            quarters_in.append(spots.pop(0))
        parts[name] = Reduce(
            g, gd if name[0] == "d" else ga, kinds, rs_send.at[k], rs_recv.at[k],
            (first, halves_in, quarters_in, last), writes[k],
        )

    def hook(name):
        for part, k in SCHEDULE.get(name, ()):
            parts[part].step(k)

    hook("go")
    small[...] = jnp.zeros_like(small)
    gaing[...] = jnp.zeros_like(gaing)
    biasg[...] = jnp.zeros_like(biasg)
    nrows = x.shape[0] // 512

    def each(phase, name):
        def body(r, _):
            phase(r)
            for k in range(nrows):
                if SCHEDULE.get(name + "." + str(k)):
                    pl.when(r == k)(lambda k=k: hook(name + "." + str(k)))
            return 0

        lax.fori_loop(0, nrows, body, 0)

    copies[0].wait()
    each(lambda r: phase_norm1(s, r), "norm")
    hook("P0")
    block[...] = s.weight(CR, CO).astype(F32)
    turned = block[...].T
    g1[...] = turned[8:9]
    g2[...] = turned[9:10]
    even = block[pl.ds(0, 16, stride=32), :]
    odd = block[pl.ds(16, 16, stride=32), :]
    both = jnp.where(lanes((16, 128)) < 64, pltpu.roll(even, 64, 1), odd)
    for k in range(16):
        bias[:, 128 * k : 128 * k + 128] = both[k : k + 1]
    copies[1].wait()
    for r in range(nrows):
        phase_forward(s, r, lambda i, r=r: hook("fwd" + str(r) + "." + str(i)))
    hook("P1")
    each(lambda r: phase_resid(s, r), "res")
    hook("U0")
    for c in range(4):
        if c == 2:
            hook("U1")
        each(lambda r, c=c: phase_ffn(s, c, r), "ffn" + str(c))
        phase_ffn_grads(s, c)
        hook("grads" + str(c))
    finish = pltpu.make_async_copy(x, out_y, sem.at[2])
    finish.start()
    for r in range(nrows):
        phase_back(s, r, lambda i, r=r: hook("back" + str(r) + "." + str(i)))
    put(CO, tn(mixed[...], s.dbranch[...]))
    hook("og")
    put(CQ, tn(normed[...], q[...]))
    kvr = tn(normed[...], s.dkr[...])
    put(CKV, kvr[:, :128])
    block[...] = kvr[:, 128:]
    hook("qg")
    each(lambda r: phase_input(s, r), "inp")
    last = pltpu.make_async_copy(dn2, out_dx, sem.at[3])
    last.start()
    turned = gaing[...].T
    lane = lanes((512, 128))
    block[...] = jnp.where(
        lane == 8, turned[:, 0:1], jnp.where(lane == 9, turned[:, 1:2], block[...])
    )
    for k in range(16):
        tiny[k : k + 1, :] = biasg[:, 128 * k : 128 * k + 128]
    pieces = tiny[0:16, :]
    low = lanes((16, 128)) < 64
    even = pl.ds(0, 16, stride=32)
    block[even, :] = jnp.where(low, block[even, :], pltpu.roll(pieces, 64, 1))
    odd = pl.ds(16, 16, stride=32)
    block[odd, :] = jnp.where(low, block[odd, :], pieces)
    put(CR, block[...])
    hook("end")
    for part in parts.values():
        part.finish()
    finish.wait()
    last.wait()


def hand_on_kernel(y_in, dx_in, *refs):
    n = (len(refs) - 4) // 2
    outs, held, sem = refs[n:-2], refs[-2], refs[-1]
    pieces = sem.shape[1] // 2
    fetch, store = [], []
    for k, (src, dst) in enumerate(((y_in, outs[0]), (dx_in, outs[1]))):
        rows = src.shape[0] // pieces
        for m in range(pieces):
            at, slot = pl.ds(m * rows, rows), k * pieces + m
            fetch.append(pltpu.make_async_copy(src.at[at], held.at[k, at], sem.at[0, slot]))
            store.append(pltpu.make_async_copy(held.at[k, at], dst.at[at], sem.at[1, slot]))
    for copy in fetch:
        copy.start()
    for src, dst in zip(refs[:n], outs[2:]):
        dst[...] = src[...]
    for one, other in zip(fetch, store):
        one.wait()
        other.start()
    for copy in store:
        copy.wait()


def shards_mega(inputs, cotangent, segment_ids, expert_ids, overflow, norm1_gain, router_weight,
                query_weight, key_value_weight, output_weight, norm2_gain, up_weight, up_bias, down_weight):
    nrows, length, width = inputs.shape
    tokens = nrows * length
    v = pl.BlockSpec(memory_space=pltpu.VMEM)
    h = pl.BlockSpec(memory_space=pl.ANY)
    sd = lambda *shape: jax.ShapeDtypeStruct(shape, F32)
    b = lambda *shape: pltpu.VMEM(shape, BF)
    f = lambda *shape: pltpu.VMEM(shape, F32)
    landing = []
    for name, kinds in REDUCES:
        landing += landing_shapes(64 if name[0] == "d" else 16, kinds)
    dma = pltpu.SemaphoreType.DMA
    out = pl.pallas_call(
        mega_kernel,
        out_shape=(
            sd(tokens, width), sd(tokens, width), sd(1, 16), sd(8, 16), sd(16, 512), sd(16, 128),
            sd(16, 512), sd(1, 16), sd(16, 2048), sd(1, 64), sd(64, 512),
        ),
        in_specs=[h, h] + [v] * 12,
        out_specs=(h, h) + (v,) * 9,
        scratch_shapes=scratch(tokens) + [
            dma((4,)), b(2, 2, 4, 2, 16, CW), b(2, 2, 4, 2, 64, 512), b(2, 2, 4, 2, 16, CW),
            b(2, 2, 4, 2, 64, 512), f(1, 512), f(1, 512), f(1, 2048), f(32, 128),
            dma((6, 8)), dma((6, 8)), dma((9, 8)), dma((9, 8)),
        ] + landing,
        compiler_params=pltpu.CompilerParams(
            collective_id=0, has_side_effects=True, vmem_limit_bytes=63 * 2**20
        ),
    )(
        inputs.reshape(tokens, width), cotangent.reshape(tokens, width), segment_ids,
        jnp.swapaxes(expert_ids, 1, 2), jnp.swapaxes(overflow, 1, 2),
        norm1_gain[None], norm2_gain[None], up_bias[None], router_weight.T, query_weight, key_value_weight,
        output_weight, up_weight, down_weight,
    )
    y, dx, g1, router, query, pair, output, g2, up, bias, down = pl.pallas_call(
        hand_on_kernel,
        out_shape=tuple(jax.ShapeDtypeStruct(o.shape, o.dtype) for o in out),
        in_specs=[h, h] + [v] * 9,
        out_specs=(h, h) + (v,) * 9,
        scratch_shapes=[f(2, tokens, width), dma((2, 12))],
    )(*out)
    return (
        y.reshape(inputs.shape), dx.reshape(inputs.shape), g1[0], router.T, query, pair, output, g2[0],
        up, bias[0], down,
    )


def shards_local(inputs, cotangent, segment_ids, expert_ids, overflow, norm1_gain, router_weight,
                 query_weight, key_value_weight, output_weight, norm2_gain, up_weight, up_bias, down_weight):
    nrows, length, width = inputs.shape
    tokens = nrows * length
    whole = lambda v: lax.all_gather(v.astype(BF), AXES, axis=0, tiled=True)
    g1, g2 = whole(norm1_gain), whole(norm2_gain)
    bias = whole(up_bias)
    router = whole(router_weight)
    parts = [whole(query_weight), whole(key_value_weight), jnp.pad(router, ((0, 0), (0, 120))),
             whole(output_weight), whole(up_weight)]
    wa = jnp.concatenate(parts, axis=1)
    wd = whole(down_weight)
    v = pl.BlockSpec(memory_space=pltpu.VMEM)
    h = pl.BlockSpec(memory_space=pl.ANY)
    sd = jax.ShapeDtypeStruct
    y, dx, ga, gd, small, biasg = pl.pallas_call(
        local_kernel,
        out_shape=(sd((tokens, width), F32), sd((tokens, width), F32), sd((512, CW), BF), sd((2048, 512), BF),
                   sd((8, 512), F32), sd((1, 2048), F32)),
        in_specs=[h, h] + [v] * 8,
        out_specs=(h, h, v, v, v, v),
        scratch_shapes=scratch(tokens) + [pltpu.SemaphoreType.DMA((4,))],
        compiler_params=pltpu.CompilerParams(vmem_limit_bytes=63 * 2**20),
    )(
        inputs.reshape(tokens, width), cotangent.reshape(tokens, width), segment_ids,
        jnp.swapaxes(expert_ids, 1, 2), jnp.swapaxes(overflow, 1, 2),
        g1.astype(F32)[None], g2.astype(F32)[None], bias.astype(F32)[None], wa, wd,
    )
    total = lambda v: lax.psum_scatter(v.astype(F32), AXES, scatter_dimension=0, tiled=True)
    return (
        y.reshape(inputs.shape), dx.reshape(inputs.shape),
        total(small[0]), total(ga[:, CR : CR + 8]), total(ga[:, CQ:CKV]), total(ga[:, CKV:CR]),
        total(ga[:, CO:CU]), total(small[1]), total(ga[:, CU:]), total(biasg[0]), total(gd),
    )


def solution(mesh):
    row3, row2, row1 = P(AXES, None, None), P(AXES, None), P(AXES)
    in_specs = (row3, row3, row2, row3, row3, row1, row2, row2, row2, row2, row1, row2, row1, row2)
    out_specs = (row3, row3, row1, row2, row2, row2, row2, row1, row2, row1, row2)
    small = mesh.shape['dp'] == 4 and mesh.shape['fsdp'] == 8
    shards = shards_mega if small else shards_local
    return jax.shard_map(shards, mesh=mesh, in_specs=in_specs, out_specs=out_specs, check_vma=False)
```

```python
import functools
import jax
import jax.numpy as jnp
from jax import lax
from jax.experimental import pallas as pl
from jax.experimental.pallas import tpu as pltpu
from jax.sharding import PartitionSpec as P

EPS = 1e-05
BIG = -1e30
GELU_C = 0.7978845608028654
GELU_K = 0.044715
BF = jnp.bfloat16
F32 = jnp.float32
AXES = ("dp", "fsdp")
VLIM = 60293120
CQ, CKV, CR, CO, CU, CW = 0, 512, 640, 768, 1280, 3328
TILES = ((0, 128, 0), (128, 256, 256), (128, 384, 768), (256, 256, 1536))


def nn(a, b):
    return lax.dot_general(a, b, (((1,), (0,)), ((), ())), preferred_element_type=F32)


def nt(a, b):
    return lax.dot_general(a, b, (((1,), (1,)), ((), ())), preferred_element_type=F32)


def tn(a, b):
    return lax.dot_general(a, b, (((0,), (0,)), ((), ())), preferred_element_type=F32)


def split(v):
    high = v.astype(BF)
    return high, (v - high.astype(F32)).astype(BF)


def lanes(shape):
    return lax.broadcasted_iota(jnp.int32, shape, len(shape) - 1)


def rows_of(shape):
    return lax.broadcasted_iota(jnp.int32, shape, len(shape) - 2)


def one_where(mask):
    return jnp.where(mask, 1.0, 0.0).astype(BF)


def norm(v):
    centred = v - jnp.mean(v, axis=-1, keepdims=True)
    inverse = lax.rsqrt(jnp.mean(centred * centred, axis=-1, keepdims=True) + EPS)
    return centred * inverse, inverse


def norm_back(grad, xhat, inverse, gain):
    scaled = grad * gain
    inner = (
        scaled
        - jnp.mean(scaled, axis=-1, keepdims=True)
        - xhat * jnp.mean(scaled * xhat, axis=-1, keepdims=True)
    )
    return inner * inverse


def gelu_both(x):
    square = x * x
    slope = (GELU_C * GELU_K) * square + GELU_C
    half = 0.5 * jnp.tanh(x * slope) + 0.5
    value = x * half
    return value, half + (value - value * half) * (6.0 * slope - 4.0 * GELU_C)


def stack_pairs(v):
    return jnp.concatenate([v[:, 128 * p : 128 * p + 128] for p in range(4)], axis=0)


class Plan:
    pass


def keys_of(s, win):
    kv, vk = s.kv[win, :], s.vk[win, :]
    low, zero = lanes(kv.shape) < 64, jnp.zeros_like(kv)
    return jnp.concatenate([jnp.where(low, kv, zero), jnp.where(low, zero, vk)], axis=0)


def values_of(s, win, extra_e, extra_o):
    kv, vk = s.kv[win, :], s.vk[win, :]
    low, zero = lanes(kv.shape) < 64, jnp.zeros_like(kv)
    even = jnp.concatenate([jnp.where(low, vk, zero), extra_e], axis=1)
    odd = jnp.concatenate([jnp.where(low, zero, kv), extra_o], axis=1)
    return jnp.concatenate([even, odd], axis=0)


def phase_norm1(s, r):
    rows = pl.ds(r * 512, 512)
    xhat, inverse = norm(s.x[rows, :])
    s.xh1[rows, :] = xhat
    s.gates[rows, :] = jnp.broadcast_to(inverse, (512, 128))


def phase_forward(s, r, hook=lambda i: None):
    rows = pl.ds(r * 512, 512)
    normed = (s.xh1[rows, :] * s.g1[...]).astype(BF)
    s.normed[rows, :] = normed
    proj = nn(normed, s.weight(CQ, CO))
    query = proj[:, :512].astype(BF)
    s.q[rows, :] = query
    pair = proj[:, CKV:CR].astype(BF).astype(F32)
    swapped = pltpu.roll(pair, 64, 1)
    low = lanes((512, 128)) < 64
    s.kv[rows, :] = jnp.where(low, pair * 0.125, pair).astype(BF)
    s.vk[rows, :] = jnp.where(low, swapped, swapped * 0.125).astype(BF)
    lane = lanes((512, 128))
    logits = jnp.where(lane < 8, proj[:, CR:CO], BIG)
    top = jnp.max(logits, axis=-1, keepdims=True)
    weights = jnp.exp(logits - top)
    prob = weights / jnp.sum(weights, axis=-1, keepdims=True)
    s.small[0:2, :] = jnp.where(s.over[r] == 0, s.ids[r], -1).astype(F32)
    s.small[2:3, :] = s.segs[pl.ds(r, 1), :].astype(F32)
    columns = s.small[...].T
    lane_f = lane.astype(F32)
    route = jnp.where(lane_f == columns[:, 0:1], 1.0, 0.0) + jnp.where(
        lane_f == columns[:, 1:2], 1.0, 0.0
    )
    mix = prob * route
    s.gates[rows, :] = jnp.where(lane == 8, s.gates[rows, :], mix + pltpu.roll(prob, 64, 1))
    seg_row = s.small[2:3, :]
    hook(0)
    for t, (start, width, at) in enumerate(TILES):
        q4 = stack_pairs(query[128 * t : 128 * t + 128])
        win = pl.ds(r * 512 + start, width)
        scores = nt(q4, keys_of(s, win))
        even, odd = scores[:, :width], scores[:, width:]
        if t:
            same = columns[128 * t : 128 * t + 128, 2:3] == seg_row[:, start : start + width]
            bias = jnp.where(same, 0.0, BIG)
            bias = jnp.concatenate([bias] * 4, axis=0)
            even, odd = even + bias, odd + bias
        even = jnp.exp(even - jnp.max(even, axis=-1, keepdims=True)).astype(BF)
        odd = jnp.exp(odd - jnp.max(odd, axis=-1, keepdims=True)).astype(BF)
        both = jnp.concatenate([even, odd], axis=1)
        s.pu[pl.ds(r * 512, 512), at : at + 2 * width] = both
        low_w = lanes((width, 128)) < 64
        one_e = jnp.where(low_w, 1.0, 0.0).astype(BF)
        one_o = jnp.where(low_w, 0.0, 1.0).astype(BF)
        out = nn(both, values_of(s, win, one_e, one_o))
        inverse = 1.0 / out[:, 128:]
        out = out[:, :128] * inverse
        for p in range(4):
            at_rows = pl.ds(r * 512 + 128 * t, 128)
            s.heads[at_rows, 128 * p : 128 * p + 128] = out[128 * p : 128 * p + 128]
            s.pinv[at_rows, 128 * p : 128 * p + 128] = inverse[128 * p : 128 * p + 128]
        hook(1 + t)
    mixed = (s.heads[rows, :] * expand(mix)).astype(BF)
    s.mixed[rows, :] = mixed
    hook(5)


def phase_resid(s, r):
    rows = pl.ds(r * 512, 512)
    resid = s.x[rows, :] + nn(s.mixed[rows, :], s.weight(CO, CU))
    s.x[rows, :] = resid
    xhat, inverse = norm(resid)
    s.xh2[rows, :] = xhat
    s.gates[rows, :] = jnp.where(lanes((512, 128)) == 9, inverse, s.gates[rows, :])
    s.normed2[rows, :] = (xhat * s.g2[...]).astype(BF)
    s.dffn[rows, :] = s.cotangent(rows).astype(BF)


def expand(per_expert):
    high, rest = split(per_expert)
    spread = one_where(
        jnp.bitwise_and(rows_of((256, 512)), 127) == jnp.right_shift(lanes((256, 512)), 6)
    )
    return nn(jnp.concatenate([high, rest], axis=1), spread)


def phase_ffn(s, c, r):
    rows = pl.ds(r * 512, 512)
    up = s.weight(CU + 512 * c, CU + 512 * c + 512)
    down = s.down(c)
    pre = nn(s.normed2[rows, :], up) + s.bias[:, 512 * c : 512 * c + 512]
    dhidden = nt(s.dffn[rows, :], down)
    value, slope = gelu_both(pre)
    dpre = dhidden * slope
    s.biasg[:, 512 * c : 512 * c + 512] += jnp.sum(dpre, axis=0, keepdims=True)
    hidden = value.astype(BF)
    dpre = dpre.astype(BF)
    s.hidden[rows, :] = hidden
    s.dpre[rows, :] = dpre
    s.x[rows, :] += nn(hidden, down)
    back = nt(dpre, up)
    if c == 0:
        s.dn2[rows, :] = back
    else:
        s.dn2[rows, :] += back


def phase_ffn_grads(s, c):
    s.put_down(c, tn(s.hidden[...], s.dffn[...]))
    s.put(CU + 512 * c, tn(s.normed2[...], s.dpre[...]))


def phase_back(s, r, hook=lambda i: None):
    rows = pl.ds(r * 512, 512)
    grad = s.dn2[rows, :]
    xhat = s.xh2[rows, :]
    s.gaing[1:2, :] += jnp.sum(grad * xhat, axis=0, keepdims=True)
    dresid = s.cotangent_row(r) + norm_back(grad, xhat, s.gates[rows, 9:10], s.g2[...])
    s.dn2[rows, :] = dresid
    dbranch = dresid.astype(BF)
    s.dbranch[rows, :] = dbranch
    dmixed = nt(dbranch, s.weight(CO, CU))
    heads = s.heads[rows, :]
    gather = one_where(
        lanes((1024, 128)) == jnp.right_shift(jnp.bitwise_and(rows_of((1024, 128)), 511), 6)
    )
    dgate = nn(jnp.concatenate(split(dmixed * heads), axis=1), gather)
    gates = s.gates[rows, :]
    first8 = lanes((512, 128)) < 8
    mix = jnp.where(first8, gates, 0.0)
    prob = jnp.where(first8, pltpu.roll(gates, 64, 1), 0.0)
    weighted = dgate * mix
    dlogits = weighted - prob * jnp.sum(weighted, axis=-1, keepdims=True)
    s.dkr[rows, 128:256] = dlogits.astype(BF)
    dout = (dmixed * expand(mix) * s.pinv[rows, :]).astype(BF)
    s.dout[...] = dout
    within = dout.astype(F32) * heads
    high, rest = split(within)
    block = one_where(
        jnp.right_shift(jnp.bitwise_and(rows_of((256, 128)), 127), 6)
        == jnp.right_shift(lanes((256, 128)), 6)
    )
    place = jnp.bitwise_and(lanes((512, 128)), 63)
    for p in range(4):
        cols = slice(128 * p, 128 * p + 128)
        total = nn(jnp.concatenate([high[:, cols], rest[:, cols]], axis=1), block)
        first, second = split(total)
        s.delta[:, cols] = jnp.where(
            place == 0, first.astype(F32), jnp.where(place == 1, second.astype(F32), 0.0)
        ).astype(BF)
    s.dkv[...] = jnp.zeros_like(s.dkv)
    hook(0)
    for t, (start, width, at) in enumerate(TILES):
        here = pl.ds(128 * t, 128)
        at_rows = pl.ds(r * 512 + 128 * t, 128)
        win = pl.ds(r * 512 + start, width)
        do4 = stack_pairs(s.dout[here, :])
        de4 = stack_pairs(s.delta[here, :])
        lane = lanes((width, 128))
        neg_e = jnp.where(lane < 2, -1.0, 0.0).astype(BF)
        neg_o = jnp.where(jnp.bitwise_and(lane, 126) == 64, -1.0, 0.0).astype(BF)
        dprob = nt(jnp.concatenate([do4, de4], axis=1), values_of(s, win, neg_e, neg_o))
        weights = s.pu[pl.ds(r * 512, 512), at : at + 2 * width]
        dscore = (weights.astype(F32) * dprob).astype(BF)
        dq4 = nn(dscore, keys_of(s, win)).astype(BF)
        q4 = stack_pairs(s.q[at_rows, :])
        dk = tn(dscore, q4)
        dv = tn(weights, do4)
        for p in range(4):
            s.q[at_rows, 128 * p : 128 * p + 128] = dq4[128 * p : 128 * p + 128]
        s.dkv[pl.ds(start, width), :] += jnp.where(
            lane < 64,
            (dk[:width] + pltpu.roll(dk[width:], 64, 1)) * 0.125,
            dv[width:] + pltpu.roll(dv[:width], 64, 1),
        )
        if t < 3:
            hook(1 + t)
    s.dkr[rows, 0:128] = s.dkv[...].astype(BF)
    hook(4)


def phase_input(s, r):
    rows = pl.ds(r * 512, 512)
    dproj = jnp.concatenate([s.q[rows, :], s.dkr[rows, :]], axis=1)
    grad = nt(dproj, s.weight(CQ, CO))
    xhat = s.xh1[rows, :]
    s.gaing[0:1, :] += jnp.sum(grad * xhat, axis=0, keepdims=True)
    s.dn2[rows, :] += norm_back(grad, xhat, s.gates[rows, 8:9], s.g1[...])


def local_kernel(
    x_in, cot_in, segs, ids, over, g1, g2, bias, wa, wd,
    out_y, out_dx, out_ga, out_gd, out_small, out_bias,
    x, cot, xh1, xh2, heads, pinv, dn2, normed, q, mixed, normed2, dffn, hidden, dpre,
    kv, vk, gates, pu, block, small, gaing, biasg, sem,
):
    s = Plan()
    s.x, s.xh1, s.xh2, s.heads, s.pinv, s.dn2 = x, xh1, xh2, heads, pinv, dn2
    s.cotangent = lambda rows: cot[rows, :]
    s.cotangent_row = lambda r: cot[pl.ds(r * 512, 512), :]
    s.normed, s.q, s.mixed, s.normed2, s.dffn, s.hidden, s.dpre = normed, q, mixed, normed2, dffn, hidden, dpre
    s.kv, s.vk, s.gates, s.pu, s.dkv = kv, vk, gates, pu, block
    s.small, s.gaing, s.biasg, s.segs, s.ids, s.over = small, gaing, biasg, segs, ids, over
    s.g1, s.g2, s.bias = g1, g2, bias
    s.dbranch = s.dffn
    s.dkr = hidden.at[:, 0:256]
    s.dout, s.delta = dpre.at[0:512, :], dpre.at[512:1024, :]
    s.weight = lambda a, b: wa[:, a:b]
    s.down = lambda c: wd[512 * c : 512 * c + 512, :]

    def put(at, value):
        out_ga[:, at : at + value.shape[1]] = value.astype(BF)

    def put_down(c, value):
        out_gd[512 * c : 512 * c + 512, :] = value.astype(BF)

    s.put, s.put_down = put, put_down
    copies = [pltpu.make_async_copy(x_in, x, sem.at[0]), pltpu.make_async_copy(cot_in, cot, sem.at[1])]
    for copy in copies:
        copy.start()
    small[...] = jnp.zeros_like(small)
    gaing[...] = jnp.zeros_like(gaing)
    biasg[...] = jnp.zeros_like(biasg)
    for copy in copies:
        copy.wait()
    nrows = x.shape[0] // 512

    def each(phase):
        lax.fori_loop(0, nrows, lambda r, _: (phase(r), 0)[1], 0)

    each(lambda r: phase_norm1(s, r))
    each(lambda r: phase_forward(s, r))
    each(lambda r: phase_resid(s, r))
    for c in range(4):
        each(lambda r: phase_ffn(s, c, r))
        phase_ffn_grads(s, c)
    finish = pltpu.make_async_copy(x, out_y, sem.at[2])
    finish.start()
    each(lambda r: phase_back(s, r))
    put(CO, tn(mixed[...], s.dbranch[...]))
    put(CQ, tn(normed[...], q[...]))
    put(CKV, tn(normed[...], s.dkr[...]))
    each(lambda r: phase_input(s, r))
    last = pltpu.make_async_copy(dn2, out_dx, sem.at[3])
    last.start()
    out_small[...] = gaing[...]
    out_bias[...] = biasg[...]
    finish.wait()
    last.wait()


def scratch(tokens):
    f = lambda *shape: pltpu.VMEM(shape, F32)
    b = lambda *shape: pltpu.VMEM(shape, BF)
    t = tokens
    return (
        [f(t, 512)] * 7 + [b(t, 512)] * 7 + [b(t, 128)] * 2
        + [f(t, 128), b(t, 2048), f(512, 128)]
        + [f(8, 512), f(8, 512), f(1, 2048)]
    )


MESH = pl.DeviceIdType.MESH


class Ring:
    def __init__(self):
        self.d = lax.axis_index("dp")
        self.f = lax.axis_index("fsdp")
        self.x, self.c = jnp.right_shift(self.d, 1), jnp.bitwise_and(self.d, 1)
        self.z, self.y = jnp.right_shift(self.f, 1), jnp.bitwise_and(self.f, 1)
        self.ox, self.oc, self.oy = 1 - self.x, 1 - self.c, 1 - self.y
        self.core_peer = (2 * self.x + self.oc, self.f)
        self.x_peer = (2 * self.ox + self.c, self.f)
        self.y_peer = (self.d, 2 * self.z + self.oy)
        self.later = [jnp.bitwise_and(self.z + k, 3) for k in (1, 2, 3)]
        self.earlier = [jnp.bitwise_and(self.z - k + 4, 3) for k in (1, 2, 3)]
        self.z_peers = [(self.d, 2 * z + self.y) for z in self.later]


def remote(src, dst, send, recv, peer):
    return pltpu.make_async_remote_copy(
        src_ref=src, dst_ref=dst, send_sem=send, recv_sem=recv, device_id=peer, device_id_type=MESH
    )


class Gather:
    def __init__(self, ring, buf, kinds, send, recv):
        self.ring, self.buf, self.kinds, self.send, self.recv = ring, buf, kinds, send, recv
        self.all = slice(kinds[0][0], kinds[-1][1])

    def copies(self, k, arriving):
        g, b = self.ring, self.buf
        if k == 0:
            at = lambda z: b.at[g.x, g.c, z, g.y, :, self.all]
            moves = [(n, at(g.earlier[n] if arriving else g.z), g.z_peers[n]) for n in range(3)]
        elif k == 3:
            moves = [(7, b.at[:, g.oc if arriving else g.c, :, :, :, self.all], g.core_peer)]
        else:
            moves = []
            x, y = (g.ox, g.oy) if arriving else (g.x, g.y)
            for kind, (lo, hi) in enumerate(self.kinds):
                cols = slice(lo, hi)
                if k == 1:
                    if kind == 0:
                        moves.append((3, b.at[x, g.c, :, g.y, :, cols], g.x_peer))
                    else:
                        moves.append((4, b.at[g.x, g.c, :, y, :, cols], g.y_peer))
                elif kind == 0:
                    moves.append((5, b.at[:, g.c, :, y, :, cols], g.y_peer))
                else:
                    moves.append((6, b.at[x, g.c, :, :, :, cols], g.x_peer))
        return [remote(ref, ref, self.send.at[n], self.recv.at[n], peer) for n, ref, peer in moves]

    def step(self, k):
        if k > 0:
            for copy in self.copies(k - 1, True):
                copy.wait_recv()
        if k < 4:
            for copy in self.copies(k, False):
                copy.start()

    def finish(self):
        for k in range(4):
            for copy in self.copies(k, False):
                copy.wait_send()


class Reduce:
    def __init__(self, ring, buf, kinds, send, recv, landing, write):
        self.ring, self.buf, self.kinds, self.send, self.recv = ring, buf, kinds, send, recv
        self.first, self.halves, self.quarters, self.last = landing
        self.all = slice(kinds[0][0], kinds[-1][1])
        self.write = write

    def copies(self, k):
        g, b = self.ring, self.buf
        if k == 0:
            moves = [(0, b.at[:, g.oc, :, :, :, self.all], self.first, g.core_peer)]
        elif k == 3:
            moves = [
                (5 + n, b.at[g.x, g.c, g.later[n], g.y, :, self.all], self.last.at[n], g.z_peers[n])
                for n in range(3)
            ]
        else:
            moves = []
            for kind, (lo, hi) in enumerate(self.kinds):
                cols = slice(lo, hi)
                if k == 1:
                    if kind == 0:
                        moves.append((1, b.at[:, g.c, :, g.oy, :, cols], self.halves[0], g.y_peer))
                    else:
                        moves.append((2, b.at[g.ox, g.c, :, :, :, cols], self.halves[1], g.x_peer))
                elif kind == 0:
                    moves.append((3, b.at[g.ox, g.c, :, g.y, :, cols], self.quarters[0], g.x_peer))
                else:
                    moves.append((4, b.at[g.x, g.c, :, g.oy, :, cols], self.quarters[1], g.y_peer))
        return [remote(src, dst, self.send.at[n], self.recv.at[n], peer) for n, src, dst, peer in moves]

    def add(self, k):
        g, b = self.ring, self.buf
        if k == 0:
            b[:, g.c, :, :, :, self.all] += self.first[...]
        elif k == 3:
            total = b[g.x, g.c, g.z, g.y, :, self.all].astype(F32)
            for n in range(3):
                total = total + self.last[n].astype(F32)
            self.write(total)
        else:
            for kind, (lo, hi) in enumerate(self.kinds):
                if k == 2:
                    b[g.x, g.c, :, g.y, :, lo:hi] += self.quarters[kind][...]
                elif kind == 0:
                    b[:, g.c, :, g.y, :, lo:hi] += self.halves[0][...]
                else:
                    b[g.x, g.c, :, :, :, lo:hi] += self.halves[1][...]

    def step(self, k):
        if k > 0:
            for copy in self.copies(k - 1):
                copy.wait_recv()
            self.add(k - 1)
        if k < 4:
            for copy in self.copies(k):
                copy.start()

    def finish(self):
        for k in range(4):
            for copy in self.copies(k):
                copy.wait_send()


class GatherOne:
    def __init__(self, ring, buf, z, send, recv):
        self.ring, self.buf, self.z, self.send, self.recv = ring, buf, z, send, recv

    def spread(self):
        g, b = self.ring, self.buf.at[self.ring.x, self.ring.c, self.z, self.ring.y]
        return [remote(b, b, self.send.at[n], self.recv.at[0], g.z_peers[n]) for n in range(3)]

    def copies(self, k, arriving):
        g, b, z = self.ring, self.buf, self.z
        x, y, c = (g.ox, g.oy, g.oc) if arriving else (g.x, g.y, g.c)
        low, high = slice(0, 256), slice(256, 512)
        if k == 1:
            moves = [
                (3, b.at[x, g.c, z, g.y, :, low], g.x_peer), (4, b.at[g.x, g.c, z, y, :, high], g.y_peer),
            ]
        elif k == 2:
            moves = [
                (5, b.at[:, g.c, z, y, :, low], g.y_peer), (6, b.at[x, g.c, z, :, :, high], g.x_peer),
            ]
        else:
            moves = [(7, b.at[:, c, z], g.core_peer)]
        return [remote(ref, ref, self.send.at[n], self.recv.at[n], peer) for n, ref, peer in moves]

    def step(self, k):
        if k == 0:
            @pl.when(self.ring.z == self.z)
            def _():
                for copy in self.spread():
                    copy.start()
        if k == 1:
            @pl.when(self.ring.z != self.z)
            def _():
                self.spread()[0].wait_recv()
        if k > 1:
            for copy in self.copies(k - 1, True):
                copy.wait_recv()
        if 0 < k < 4:
            for copy in self.copies(k, False):
                copy.start()

    def finish(self):
        @pl.when(self.ring.z == self.z)
        def _():
            for copy in self.spread():
                copy.wait_send()

        for k in (1, 2, 3):
            for copy in self.copies(k, False):
                copy.wait_send()


class ReduceOne:
    def __init__(self, ring, buf, z, send, recv, landing, write):
        self.ring, self.buf, self.z, self.send, self.recv = ring, buf, z, send, recv
        self.first, self.halves, self.quarters, self.last = landing
        self.write = write

    def copies(self, k):
        g, b, z = self.ring, self.buf, self.z
        low, high = slice(0, 256), slice(256, 512)
        if k == 0:
            moves = [(0, b.at[:, g.oc, z], self.first, g.core_peer)]
        elif k == 1:
            moves = [
                (1, b.at[:, g.c, z, g.oy, :, low], self.halves[0], g.y_peer),
                (2, b.at[g.ox, g.c, z, :, :, high], self.halves[1], g.x_peer),
            ]
        else:
            moves = [
                (3, b.at[g.ox, g.c, z, g.y, :, low], self.quarters[0], g.x_peer),
                (4, b.at[g.x, g.c, z, g.oy, :, high], self.quarters[1], g.y_peer),
            ]
        return [remote(src, dst, self.send.at[n], self.recv.at[n], peer) for n, src, dst, peer in moves]

    def collect(self, sender):
        g = self.ring
        slot = jnp.bitwise_and(sender - self.z + 3, 3)
        return remote(
            self.buf.at[g.x, g.c, self.z, g.y], self.last.at[slot], self.send.at[5], self.recv.at[5 + slot],
            (g.d, 2 * self.z + g.y),
        )

    def step(self, k):
        g, b, z = self.ring, self.buf, self.z
        low, high = slice(0, 256), slice(256, 512)
        if 0 < k < 4:
            for copy in self.copies(k - 1):
                copy.wait_recv()
        if k == 1:
            b[:, g.c, z] += self.first[...]
        if k == 2:
            b[:, g.c, z, g.y, :, low] += self.halves[0][...]
            b[g.x, g.c, z, :, :, high] += self.halves[1][...]
        if k == 3:
            b[g.x, g.c, z, g.y, :, low] += self.quarters[0][...]
            b[g.x, g.c, z, g.y, :, high] += self.quarters[1][...]

            @pl.when(g.z != z)
            def _():
                self.collect(g.z).start()
        if k < 3:
            for copy in self.copies(k):
                copy.start()
        if k == 4:
            @pl.when(g.z == z)
            def _():
                total = b[g.x, g.c, z, g.y].astype(F32)
                for n in range(3):
                    self.collect((z + 1 + n) % 4).wait_recv()
                    total = total + self.last[n].astype(F32)
                self.write(total)

    def finish(self):
        for k in range(3):
            for copy in self.copies(k):
                copy.wait_send()

        @pl.when(self.ring.z != self.z)
        def _():
            self.collect(self.ring.z).wait_send()


def landing_shapes(rows, kinds):
    b = lambda *shape: pltpu.VMEM(shape, BF)
    if isinstance(kinds, int):
        return [
            b(2, 2, rows, 512), b(3, rows, 512), b(2, rows, 256), b(rows, 256), b(2, rows, 256), b(rows, 256),
        ]
    n = kinds[-1][1] - kinds[0][0]
    shapes = [b(2, 4, 2, rows, n), b(3, rows, n)]
    for kind, (lo, hi) in enumerate(kinds):
        shapes.append(b(2, 4, rows, hi - lo) if kind == 0 else b(4, 2, rows, hi - lo))
        shapes.append(b(4, rows, hi - lo))
    return shapes


def halves(lo, hi, cut=None):
    cut = (lo + hi) // 2 if cut is None else cut
    return ((lo, cut), (cut, hi))


GATHERS = (
    ("P0", halves(CQ, CO)), ("P1", halves(CO, CU)), ("U0", halves(CU, CU + 512)), ("D0", 0),
    ("U1", halves(CU + 512, CU + 1024)), ("D1", 1), ("U2", halves(CU + 1024, CW)), ("D2", 2), ("D3", 3),
)
REDUCES = (
    ("u0", halves(CU, CU + 512)), ("u1", halves(CU + 512, CU + 1024)),
    ("u2", halves(CU + 1024, CU + 1536)), ("u3", halves(CU + 1536, CW)),
    ("d0", 0), ("d1", 1), ("d2", 2), ("d3", 3), ("o", halves(CO, CU)),
    ("q", halves(CQ, CR, 384)), ("r", ((CR, CO),)),
)
SHARED = {"d2": "d0", "d3": "d1"}
SCHEDULE = {
    "go": (("P0", 0), ("P1", 0), ("U0", 0), ("D0", 0), ("U1", 0), ("D1", 0), ("U2", 0), ("D2", 0), ("D3", 0),),
    "P0": (("P0", 1), ("P0", 2), ("P1", 1), ("U0", 1), ("P0", 3), ("D0", 1), ("P1", 2), ("U0", 2), ("U1", 1), ("P0", 4),),
    "fwd0.0": (("D0", 2),),
    "fwd0.3": (("P1", 3), ("D1", 1),),
    "fwd1.0": (("U0", 3),),
    "fwd1.1": (("U1", 2),),
    "fwd1.2": (("P1", 4),),
    "fwd1.3": (("U2", 1), ("D0", 3),),
    "fwd1.4": (("U0", 4), ("D1", 2),),
    "fwd2.2": (("D0", 4), ("D2", 1), ("U1", 3),),
    "fwd2.4": (("U2", 2),),
    "res.0": (("U1", 4),),
    "res.1": (("D1", 3),),
    "res.2": (("D2", 2),),
    "ffn0.0": (("D3", 1), ("D1", 4),),
    "ffn0.2": (("U2", 3), ("D2", 3),),
    "grads0": (("d0", 0), ("u0", 0), ("D3", 2),),
    "ffn1.0": (("U2", 4),),
    "ffn1.1": (("D2", 4), ("d0", 1), ("u0", 1),),
    "ffn1.2": (("D3", 3),),
    "grads1": (("d1", 0), ("u1", 0),),
    "ffn2.0": (("D3", 4), ("d0", 2),),
    "ffn2.1": (("u0", 2), ("d1", 1), ("u1", 1),),
    "ffn2.2": (("d0", 3),),
    "grads2": (("d2", 0), ("u2", 0), ("u0", 3),),
    "ffn3.0": (("d1", 2),),
    "ffn3.1": (("d2", 1), ("u1", 2), ("u2", 1),),
    "ffn3.2": (("d1", 3),),
    "grads3": (("d3", 0), ("u3", 0), ("d0", 4), ("u0", 4), ("d2", 2),),
    "back0.0": (("u1", 3),),
    "back0.1": (("d3", 1), ("u2", 2),),
    "back0.2": (("u3", 1),),
    "back0.3": (("d2", 3), ("d1", 4),),
    "back1.0": (("u1", 4), ("d3", 2),),
    "back1.1": (("u2", 3),),
    "back1.3": (("u3", 2),),
    "back2.0": (("d3", 3), ("d2", 4),),
    "back2.2": (("u2", 4), ("u3", 3),),
    "og": (("o", 0),),
    "qg": (("q", 0),),
    "inp.0": (("o", 1),),
    "inp.1": (("d3", 4),),
    "inp.2": (("q", 1),),
    "end": (("r", 0), ("u3", 4), ("o", 2), ("r", 1), ("q", 2), ("o", 3), ("r", 2), ("q", 3), ("r", 3), ("o", 4), ("q", 4), ("r", 4),),
}


def mega_kernel(
    x_in, cot_in, segs_in, ids_in, over_in, g1_in, g2_in, bias_in, router_in, q_in, kv_in, o_in, up_in, down_in,
    x, dn2, out_g1, out_router, out_q, out_kv, out_o, out_g2, out_up, out_bias, out_down,
    xh1, xh2, heads, pinv, normed, q, mixed, normed2, dffn, hidden, dpre,
    kv, vk, gates, pu, block, small, gaing, biasg,
    sem, cot_row, segs, ids, over, small_in, router_at, bias_at, wa, wd, ga, gd, g1, g2, bias, tiny, ag_send, ag_recv, rs_send, rs_recv, *landing,
):
    s = Plan()
    s.x, s.xh1, s.xh2, s.heads, s.pinv, s.dn2 = x, xh1, xh2, heads, pinv, dn2
    s.cotangent = lambda rows: dn2[rows, :]

    def fetch_row(r):
        return pltpu.make_async_copy(cot_in.at[512 * r : 512 * r + 512], cot_row, sem.at[17 + r])

    def cotangent_row(r):
        fetch_row(r).wait()
        return cot_row[...]

    s.cotangent_row = cotangent_row
    s.normed, s.q, s.mixed, s.normed2, s.dffn, s.hidden, s.dpre = normed, q, mixed, normed2, dffn, hidden, dpre
    s.kv, s.vk, s.gates, s.pu, s.dkv = kv, vk, gates, pu, block
    s.small, s.gaing, s.biasg, s.segs, s.ids, s.over = small, gaing, biasg, segs, ids, over
    s.g1, s.g2, s.bias = g1, g2, bias
    s.dbranch = s.dffn
    s.dkr = hidden.at[:, 0:256]
    s.dout, s.delta = dpre.at[0:512, :], dpre.at[512:1024, :]
    s.weight = lambda a, b: wa[:, :, :, :, :, a:b].reshape(512, b - a)
    s.down = lambda c: wd[:, :, c].reshape(512, 512)

    def put(at, value):
        n = value.shape[1]
        ga[:, :, :, :, :, at : at + n] = value.astype(BF).reshape(2, 2, 4, 2, 16, n)

    def put_down(c, value):
        gd[:, :, c] = value.astype(BF).reshape(2, 2, 2, 64, 512)

    s.put, s.put_down = put, put_down
    g = Ring()
    peers = [g.core_peer, g.x_peer, g.y_peer] + g.z_peers
    barrier = pltpu.get_barrier_semaphore()
    for peer in peers:
        pl.semaphore_signal(barrier, inc=1, device_id=peer, device_id_type=MESH)
    moves = [
        (q_in, dn2.at[0:16]), (o_in, dn2.at[16:32]), (kv_in, dn2.at[32:48, 0:128]), (down_in, dn2.at[128:192]),
        (router_in, router_at), (g1_in, small_in.at[0:1]), (g2_in, small_in.at[8:9]), (bias_in, bias_at),
    ]
    moves += [
        (up_in.at[:, 512 * k : 512 * k + 512], dn2.at[48 + 16 * k : 64 + 16 * k]) for k in range(4)
    ]
    moves += [(x_in, x), (segs_in, segs), (ids_in, ids), (over_in, over), (cot_in, dn2)]
    copies = [pltpu.make_async_copy(src, dst, sem.at[n]) for n, (src, dst) in enumerate(moves)]
    for copy in copies[:16]:
        copy.start()
    for copy in copies[:12]:
        copy.wait()

    wa[g.x, g.c, g.z, g.y, :, CQ:CKV] = dn2[0:16, :].astype(BF)
    wa[g.x, g.c, g.z, g.y, :, CKV:CR] = dn2[32:48, 0:128].astype(BF)
    wa[g.x, g.c, g.z, g.y, :, CO:CU] = dn2[16:32, :].astype(BF)
    for k in range(16):
        at = CU + 512 * (k % 4) + 128 * (k // 4)
        wa[g.x, g.c, g.z, g.y, :, at : at + 128] = dn2[
            48 + 16 * (k // 4) : 64 + 16 * (k // 4), 128 * (k % 4) : 128 * (k % 4) + 128
        ].astype(BF)
    wd[g.x, g.c, g.z, g.y] = dn2[128:192, :].astype(BF)
    tiny[...] = jnp.zeros_like(tiny)
    tiny[0:8, 0:16] = router_at[...]
    tiny[8:9, 0:16] = small_in[0:1]
    tiny[9:10, 0:16] = small_in[8:9]
    tiny[16:17, 0:64] = bias_at[...]
    turned = tn(
        tiny[0:16, :].astype(BF), one_where(rows_of((16, 128)) == lanes((16, 128)))
    )[0:16]
    shifted = nn(tiny[16:32, :].astype(BF), one_where(rows_of((128, 128)) + 64 == lanes((128, 128))))
    wa[g.x, g.c, g.z, g.y, :, CR:CO] = (turned + shifted).astype(BF)

    copies[16].start()
    pl.semaphore_wait(barrier, len(peers))
    parts = {}
    for k, (name, kinds) in enumerate(GATHERS):
        make, buf = (GatherOne, wd) if name[0] == "D" else (Gather, wa)
        parts[name] = make(g, buf, kinds, ag_send.at[k], ag_recv.at[k])

    def write_to(ref, at=0):
        def write(total):
            ref[:, at : at + total.shape[1]] = total

        return write

    def write_q(total):
        out_q[...] = total[:, :512]
        out_kv[...] = total[:, 512:]

    def write_small(total):
        turned = total.T
        out_router[...] = turned[0:8]
        out_g1[...] = turned[8:9]
        out_g2[...] = turned[9:10]
        out_bias[...] = pltpu.roll(total, 64, 1)[0:1, 0:64]

    def write_up(c):
        def write(total):
            for k in range(4):
                at = 512 * k + 128 * c
                out_up[:, at : at + 128] = total[:, 128 * k : 128 * k + 128]

        return write

    writes = [write_up(c) for c in range(4)] + [write_to(out_down)] * 4 + [write_to(out_o), write_q, write_small]
    spots = list(landing)
    for k, (name, kinds) in enumerate(REDUCES):
        first = parts[SHARED[name]].first if name in SHARED else spots.pop(0)
        last = spots.pop(0)
        halves_in, quarters_in = [], []
        for _ in range(2 if isinstance(kinds, int) else len(kinds)):
            halves_in.append(spots.pop(0))
            quarters_in.append(spots.pop(0))
        make, buf = (ReduceOne, gd) if name[0] == "d" else (Reduce, ga)
        parts[name] = make(
            g, buf, kinds, rs_send.at[k], rs_recv.at[k],
            (first, halves_in, quarters_in, last), writes[k],
        )

    def hook(name):
        for part, k in SCHEDULE.get(name, ()):
            parts[part].step(k)

    hook("go")
    small[...] = jnp.zeros_like(small)
    gaing[...] = jnp.zeros_like(gaing)
    biasg[...] = jnp.zeros_like(biasg)
    nrows = x.shape[0] // 512

    def each(phase, name):
        def body(r, _):
            phase(r)
            for k in range(nrows):
                if SCHEDULE.get(name + "." + str(k)):
                    pl.when(r == k)(lambda k=k: hook(name + "." + str(k)))
            return 0

        lax.fori_loop(0, nrows, body, 0)

    copies[12].wait()
    each(lambda r: phase_norm1(s, r), "norm")
    hook("P0")
    block[...] = s.weight(CR, CO).astype(F32)
    turned = block[...].T
    g1[...] = turned[8:9]
    g2[...] = turned[9:10]
    even = block[pl.ds(0, 16, stride=32), :]
    odd = block[pl.ds(16, 16, stride=32), :]
    both = jnp.where(lanes((16, 128)) < 64, pltpu.roll(even, 64, 1), odd)
    for k in range(16):
        at = 512 * (k % 4) + 128 * (k // 4)
        bias[:, at : at + 128] = both[k : k + 1]
    for copy in copies[13:]:
        copy.wait()
    for r in range(nrows):
        phase_forward(s, r, lambda i, r=r: hook("fwd" + str(r) + "." + str(i)))
    hook("P1")
    each(lambda r: phase_resid(s, r), "res")
    fetch_row(0).start()
    for c in range(4):
        hook("ffn" + str(c))
        each(lambda r, c=c: phase_ffn(s, c, r), "ffn" + str(c))
        phase_ffn_grads(s, c)
        hook("grads" + str(c))
    def back_hook(r, i):
        if i == 0 and r + 1 < nrows:
            fetch_row(r + 1).start()
        hook("back" + str(r) + "." + str(i))

    for r in range(nrows):
        phase_back(s, r, functools.partial(back_hook, r))
    put(CO, tn(mixed[...], s.dbranch[...]))
    hook("og")
    put(CQ, tn(normed[...], q[...]))
    kvr = tn(normed[...], s.dkr[...])
    put(CKV, kvr[:, :128])
    block[...] = kvr[:, 128:]
    hook("qg")
    each(lambda r: phase_input(s, r), "inp")
    turned = gaing[...].T
    lane = lanes((512, 128))
    block[...] = jnp.where(
        lane == 8, turned[:, 0:1], jnp.where(lane == 9, turned[:, 1:2], block[...])
    )
    for k in range(16):
        at = 512 * (k % 4) + 128 * (k // 4)
        tiny[k : k + 1, :] = biasg[:, at : at + 128]
    pieces = tiny[0:16, :]
    low = lanes((16, 128)) < 64
    even = pl.ds(0, 16, stride=32)
    block[even, :] = jnp.where(low, block[even, :], pltpu.roll(pieces, 64, 1))
    odd = pl.ds(16, 16, stride=32)
    block[odd, :] = jnp.where(low, block[odd, :], pieces)
    put(CR, block[...])
    hook("end")
    for part in parts.values():
        part.finish()


def hand_on_kernel(*refs):
    n = len(refs) // 2
    copies = [pltpu.make_async_copy(refs[k], refs[n + k], refs[-1].at[k]) for k in range(n)]
    for copy in copies:
        copy.start()
    for copy in copies:
        copy.wait()


def shards_mega(inputs, cotangent, segment_ids, expert_ids, overflow, norm1_gain, router_weight,
                query_weight, key_value_weight, output_weight, norm2_gain, up_weight, up_bias, down_weight):
    nrows, length, width = inputs.shape
    tokens = nrows * length
    v = pl.BlockSpec(memory_space=pltpu.VMEM)
    h = pl.BlockSpec(memory_space=pl.ANY)
    sd = lambda *shape: jax.ShapeDtypeStruct(shape, F32)
    b = lambda *shape: pltpu.VMEM(shape, BF)
    f = lambda *shape: pltpu.VMEM(shape, F32)
    n = lambda *shape: pltpu.VMEM(shape, jnp.int32)
    landing = []
    for name, kinds in REDUCES:
        landing += landing_shapes(64 if name[0] == "d" else 16, kinds)[name in SHARED :]
    dma = pltpu.SemaphoreType.DMA
    out = pl.pallas_call(
        mega_kernel,
        out_shape=(
            f(tokens, width), f(tokens, width), f(1, 16), f(8, 16), f(16, 512), f(16, 128),
            f(16, 512), f(1, 16), f(16, 2048), f(1, 64), f(64, 512),
        ),
        in_specs=[h] * 14,
        out_specs=(v,) * 11,
        scratch_shapes=scratch(tokens)[2:6] + scratch(tokens)[7:] + [
            dma((20,)), f(512, 512), n(3, 512), n(3, 2, 512), n(3, 2, 512), f(16, 16), f(8, 16), f(1, 64), b(2, 2, 4, 2, 16, CW), b(2, 2, 4, 2, 64, 512), b(2, 2, 4, 2, 16, CW),
            b(2, 2, 4, 2, 64, 512), f(1, 512), f(1, 512), f(1, 2048), f(32, 128),
            dma((9, 8)), dma((9, 8)), dma((11, 8)), dma((11, 8)),
        ] + landing,
        compiler_params=pltpu.CompilerParams(
            collective_id=0, has_side_effects=True, vmem_limit_bytes=VLIM
        ),
    )(
        inputs.reshape(tokens, width), cotangent.reshape(tokens, width), segment_ids,
        jnp.swapaxes(expert_ids, 1, 2), jnp.swapaxes(overflow, 1, 2),
        norm1_gain[None], norm2_gain[None], up_bias[None], router_weight.T, query_weight, key_value_weight,
        output_weight, up_weight, down_weight,
    )
    y, dx, g1, router, query, pair, output, g2, up, bias, down = pl.pallas_call(
        hand_on_kernel,
        out_shape=tuple(sd(*o.shape) for o in out),
        in_specs=[h] * 11,
        out_specs=(h,) * 11,
        scratch_shapes=[dma((11,))],
        compiler_params=pltpu.CompilerParams(vmem_limit_bytes=32 * 1024),
    )(*out)
    return (
        y.reshape(inputs.shape), dx.reshape(inputs.shape), g1[0], router.T, query, pair, output, g2[0],
        up, bias[0], down,
    )


def shards_local(inputs, cotangent, segment_ids, expert_ids, overflow, norm1_gain, router_weight,
                 query_weight, key_value_weight, output_weight, norm2_gain, up_weight, up_bias, down_weight):
    nrows, length, width = inputs.shape
    tokens = nrows * length
    whole = lambda v: lax.all_gather(v.astype(BF), AXES, axis=0, tiled=True)
    g1, g2 = whole(norm1_gain), whole(norm2_gain)
    bias = whole(up_bias)
    router = whole(router_weight)
    parts = [whole(query_weight), whole(key_value_weight), jnp.pad(router, ((0, 0), (0, 120))),
             whole(output_weight), whole(up_weight)]
    wa = jnp.concatenate(parts, axis=1)
    wd = whole(down_weight)
    v = pl.BlockSpec(memory_space=pltpu.VMEM)
    h = pl.BlockSpec(memory_space=pl.ANY)
    sd = jax.ShapeDtypeStruct
    y, dx, ga, gd, small, biasg = pl.pallas_call(
        local_kernel,
        out_shape=(sd((tokens, width), F32), sd((tokens, width), F32), sd((512, CW), BF), sd((2048, 512), BF),
                   sd((8, 512), F32), sd((1, 2048), F32)),
        in_specs=[h, h] + [v] * 8,
        out_specs=(h, h, v, v, v, v),
        scratch_shapes=scratch(tokens) + [pltpu.SemaphoreType.DMA((4,))],
        compiler_params=pltpu.CompilerParams(vmem_limit_bytes=63 * 2**20),
    )(
        inputs.reshape(tokens, width), cotangent.reshape(tokens, width), segment_ids,
        jnp.swapaxes(expert_ids, 1, 2), jnp.swapaxes(overflow, 1, 2),
        g1.astype(F32)[None], g2.astype(F32)[None], bias.astype(F32)[None], wa, wd,
    )
    total = lambda v: lax.psum_scatter(v.astype(F32), AXES, scatter_dimension=0, tiled=True)
    return (
        y.reshape(inputs.shape), dx.reshape(inputs.shape),
        total(small[0]), total(ga[:, CR : CR + 8]), total(ga[:, CQ:CKV]), total(ga[:, CKV:CR]),
        total(ga[:, CO:CU]), total(small[1]), total(ga[:, CU:]), total(biasg[0]), total(gd),
    )


def solution(mesh):
    row3, row2, row1 = P(AXES, None, None), P(AXES, None), P(AXES)
    in_specs = (row3, row3, row2, row3, row3, row1, row2, row2, row2, row2, row1, row2, row1, row2)
    out_specs = (row3, row3, row1, row2, row2, row2, row2, row1, row2, row1, row2)
    small = mesh.shape['dp'] == 4 and mesh.shape['fsdp'] == 8
    shards = shards_mega if small else shards_local
    return jax.shard_map(shards, mesh=mesh, in_specs=in_specs, out_specs=out_specs, check_vma=False)
```

```python
import functools
import jax
import jax.numpy as jnp
from jax import lax
from jax.experimental import pallas as pl
from jax.experimental.pallas import tpu as pltpu
from jax.sharding import PartitionSpec as P

EPS = 1e-05
BIG = -1e30
GELU_C = 0.7978845608028654
GELU_K = 0.044715
BF = jnp.bfloat16
F32 = jnp.float32
AXES = ("dp", "fsdp")
VLIM = 60293120
CQ, CKV, CR, CO, CU, CW = 0, 512, 640, 768, 1280, 3328
TILES = ((0, 128, 0), (128, 256, 256), (128, 384, 768), (256, 256, 1536))


def nn(a, b):
    return lax.dot_general(a, b, (((1,), (0,)), ((), ())), preferred_element_type=F32)


def nt(a, b):
    return lax.dot_general(a, b, (((1,), (1,)), ((), ())), preferred_element_type=F32)


def tn(a, b):
    return lax.dot_general(a, b, (((0,), (0,)), ((), ())), preferred_element_type=F32)


def split(v):
    high = v.astype(BF)
    return high, (v - high.astype(F32)).astype(BF)


def lanes(shape):
    return lax.broadcasted_iota(jnp.int32, shape, len(shape) - 1)


def rows_of(shape):
    return lax.broadcasted_iota(jnp.int32, shape, len(shape) - 2)


def one_where(mask):
    return jnp.where(mask, 1.0, 0.0).astype(BF)


def norm(v):
    centred = v - jnp.mean(v, axis=-1, keepdims=True)
    inverse = lax.rsqrt(jnp.mean(centred * centred, axis=-1, keepdims=True) + EPS)
    return centred * inverse, inverse


def norm_back(grad, xhat, inverse, gain):
    scaled = grad * gain
    inner = (
        scaled
        - jnp.mean(scaled, axis=-1, keepdims=True)
        - xhat * jnp.mean(scaled * xhat, axis=-1, keepdims=True)
    )
    return inner * inverse


def gelu_both(x):
    square = x * x
    slope = (GELU_C * GELU_K) * square + GELU_C
    half = 0.5 * jnp.tanh(x * slope) + 0.5
    value = x * half
    return value, half + (value - value * half) * (6.0 * slope - 4.0 * GELU_C)


def stack_pairs(v):
    return jnp.concatenate([v[:, 128 * p : 128 * p + 128] for p in range(4)], axis=0)


class Plan:
    pass


def keys_of(s, win):
    kv, vk = s.kv[win, :], s.vk[win, :]
    low, zero = lanes(kv.shape) < 64, jnp.zeros_like(kv)
    return jnp.concatenate([jnp.where(low, kv, zero), jnp.where(low, zero, vk)], axis=0)


def values_of(s, win, extra_e, extra_o):
    kv, vk = s.kv[win, :], s.vk[win, :]
    low, zero = lanes(kv.shape) < 64, jnp.zeros_like(kv)
    even = jnp.concatenate([jnp.where(low, vk, zero), extra_e], axis=1)
    odd = jnp.concatenate([jnp.where(low, zero, kv), extra_o], axis=1)
    return jnp.concatenate([even, odd], axis=0)


def phase_norm1(s, r):
    rows = pl.ds(r * 512, 512)
    xhat, inverse = norm(s.x[rows, :])
    s.xh1[rows, :] = xhat
    s.gates[rows, :] = jnp.broadcast_to(inverse, (512, 128))


def phase_forward(s, r, hook=lambda i: None):
    rows = pl.ds(r * 512, 512)
    normed = (s.xh1[rows, :] * s.g1[...]).astype(BF)
    s.normed[rows, :] = normed
    proj = nn(normed, s.weight(CQ, CO))
    query = proj[:, :512].astype(BF)
    s.q[rows, :] = query
    pair = proj[:, CKV:CR].astype(BF).astype(F32)
    swapped = pltpu.roll(pair, 64, 1)
    low = lanes((512, 128)) < 64
    s.kv[rows, :] = jnp.where(low, pair * 0.125, pair).astype(BF)
    s.vk[rows, :] = jnp.where(low, swapped, swapped * 0.125).astype(BF)
    lane = lanes((512, 128))
    logits = jnp.where(lane < 8, proj[:, CR:CO], BIG)
    top = jnp.max(logits, axis=-1, keepdims=True)
    weights = jnp.exp(logits - top)
    prob = weights / jnp.sum(weights, axis=-1, keepdims=True)
    s.small[0:2, :] = jnp.where(s.over[r] == 0, s.ids[r], -1).astype(F32)
    s.small[2:3, :] = s.segs[pl.ds(r, 1), :].astype(F32)
    columns = s.small[...].T
    lane_f = lane.astype(F32)
    route = jnp.where(lane_f == columns[:, 0:1], 1.0, 0.0) + jnp.where(
        lane_f == columns[:, 1:2], 1.0, 0.0
    )
    mix = prob * route
    s.gates[rows, :] = jnp.where(lane == 8, s.gates[rows, :], mix + pltpu.roll(prob, 64, 1))
    seg_row = s.small[2:3, :]
    hook(0)
    for t, (start, width, at) in enumerate(TILES):
        q4 = stack_pairs(query[128 * t : 128 * t + 128])
        win = pl.ds(r * 512 + start, width)
        scores = nt(q4, keys_of(s, win))
        even, odd = scores[:, :width], scores[:, width:]
        if t:
            same = columns[128 * t : 128 * t + 128, 2:3] == seg_row[:, start : start + width]
            bias = jnp.where(same, 0.0, BIG)
            bias = jnp.concatenate([bias] * 4, axis=0)
            even, odd = even + bias, odd + bias
        even = jnp.exp(even - jnp.max(even, axis=-1, keepdims=True)).astype(BF)
        odd = jnp.exp(odd - jnp.max(odd, axis=-1, keepdims=True)).astype(BF)
        both = jnp.concatenate([even, odd], axis=1)
        s.pu[pl.ds(r * 512, 512), at : at + 2 * width] = both
        low_w = lanes((width, 128)) < 64
        one_e = jnp.where(low_w, 1.0, 0.0).astype(BF)
        one_o = jnp.where(low_w, 0.0, 1.0).astype(BF)
        out = nn(both, values_of(s, win, one_e, one_o))
        inverse = 1.0 / out[:, 128:]
        out = out[:, :128] * inverse
        for p in range(4):
            at_rows = pl.ds(r * 512 + 128 * t, 128)
            s.heads[at_rows, 128 * p : 128 * p + 128] = out[128 * p : 128 * p + 128]
            s.pinv[at_rows, 128 * p : 128 * p + 128] = inverse[128 * p : 128 * p + 128]
        hook(1 + t)
    mixed = (s.heads[rows, :] * expand(mix)).astype(BF)
    s.mixed[rows, :] = mixed
    hook(5)


def phase_resid(s, r):
    rows = pl.ds(r * 512, 512)
    resid = s.x[rows, :] + nn(s.mixed[rows, :], s.weight(CO, CU))
    s.x[rows, :] = resid
    xhat, inverse = norm(resid)
    s.xh2[rows, :] = xhat
    s.gates[rows, :] = jnp.where(lanes((512, 128)) == 9, inverse, s.gates[rows, :])
    s.normed2[rows, :] = (xhat * s.g2[...]).astype(BF)
    s.dffn[rows, :] = s.cotangent(rows).astype(BF)


def expand(per_expert):
    high, rest = split(per_expert)
    spread = one_where(
        jnp.bitwise_and(rows_of((256, 512)), 127) == jnp.right_shift(lanes((256, 512)), 6)
    )
    return nn(jnp.concatenate([high, rest], axis=1), spread)


def phase_ffn(s, c, r):
    rows = pl.ds(r * 512, 512)
    up = s.weight(CU + 512 * c, CU + 512 * c + 512)
    down = s.down(c)
    pre = nn(s.normed2[rows, :], up) + s.bias[:, 512 * c : 512 * c + 512]
    dhidden = nt(s.dffn[rows, :], down)
    value, slope = gelu_both(pre)
    dpre = dhidden * slope
    s.biasg[:, 512 * c : 512 * c + 512] += jnp.sum(dpre, axis=0, keepdims=True)
    hidden = value.astype(BF)
    dpre = dpre.astype(BF)
    s.hidden[rows, :] = hidden
    s.dpre[rows, :] = dpre
    s.x[rows, :] += nn(hidden, down)
    back = nt(dpre, up)
    if c == 0:
        s.dn2[rows, :] = back
    else:
        s.dn2[rows, :] += back


def phase_ffn_grads(s, c):
    s.put_down(c, tn(s.hidden[...], s.dffn[...]))
    s.put(CU + 512 * c, tn(s.normed2[...], s.dpre[...]))


def phase_norm2_back(s, r):
    rows = pl.ds(r * 512, 512)
    grad = s.dn2[rows, :]
    xhat = s.xh2[rows, :]
    s.gaing[1:2, :] += jnp.sum(grad * xhat, axis=0, keepdims=True)
    dresid = s.cotangent_row(r) + norm_back(grad, xhat, s.gates[rows, 9:10], s.g2[...])
    s.dn2[rows, :] = dresid
    dbranch = dresid.astype(BF)
    s.dbranch[rows, :] = dbranch


def phase_back(s, r, hook=lambda i: None):
    rows = pl.ds(r * 512, 512)
    dmixed = nt(s.dbranch[rows, :], s.weight(CO, CU))
    heads = s.heads[rows, :]
    gather = one_where(
        lanes((1024, 128)) == jnp.right_shift(jnp.bitwise_and(rows_of((1024, 128)), 511), 6)
    )
    dgate = nn(jnp.concatenate(split(dmixed * heads), axis=1), gather)
    gates = s.gates[rows, :]
    first8 = lanes((512, 128)) < 8
    mix = jnp.where(first8, gates, 0.0)
    prob = jnp.where(first8, pltpu.roll(gates, 64, 1), 0.0)
    weighted = dgate * mix
    dlogits = weighted - prob * jnp.sum(weighted, axis=-1, keepdims=True)
    s.dkr[rows, 128:256] = dlogits.astype(BF)
    dout = (dmixed * expand(mix) * s.pinv[rows, :]).astype(BF)
    s.dout[...] = dout
    within = dout.astype(F32) * heads
    high, rest = split(within)
    block = one_where(
        jnp.right_shift(jnp.bitwise_and(rows_of((256, 128)), 127), 6)
        == jnp.right_shift(lanes((256, 128)), 6)
    )
    place = jnp.bitwise_and(lanes((512, 128)), 63)
    for p in range(4):
        cols = slice(128 * p, 128 * p + 128)
        total = nn(jnp.concatenate([high[:, cols], rest[:, cols]], axis=1), block)
        first, second = split(total)
        s.delta[:, cols] = jnp.where(
            place == 0, first.astype(F32), jnp.where(place == 1, second.astype(F32), 0.0)
        ).astype(BF)
    s.dkv[...] = jnp.zeros_like(s.dkv)
    hook(0)
    for t, (start, width, at) in enumerate(TILES):
        here = pl.ds(128 * t, 128)
        at_rows = pl.ds(r * 512 + 128 * t, 128)
        win = pl.ds(r * 512 + start, width)
        do4 = stack_pairs(s.dout[here, :])
        de4 = stack_pairs(s.delta[here, :])
        lane = lanes((width, 128))
        neg_e = jnp.where(lane < 2, -1.0, 0.0).astype(BF)
        neg_o = jnp.where(jnp.bitwise_and(lane, 126) == 64, -1.0, 0.0).astype(BF)
        dprob = nt(jnp.concatenate([do4, de4], axis=1), values_of(s, win, neg_e, neg_o))
        weights = s.pu[pl.ds(r * 512, 512), at : at + 2 * width]
        dscore = (weights.astype(F32) * dprob).astype(BF)
        dq4 = nn(dscore, keys_of(s, win)).astype(BF)
        q4 = stack_pairs(s.q[at_rows, :])
        dk = tn(dscore, q4)
        dv = tn(weights, do4)
        for p in range(4):
            s.q[at_rows, 128 * p : 128 * p + 128] = dq4[128 * p : 128 * p + 128]
        s.dkv[pl.ds(start, width), :] += jnp.where(
            lane < 64,
            (dk[:width] + pltpu.roll(dk[width:], 64, 1)) * 0.125,
            dv[width:] + pltpu.roll(dv[:width], 64, 1),
        )
        if t < 3:
            hook(1 + t)
    s.dkr[rows, 0:128] = s.dkv[...].astype(BF)
    hook(4)


def phase_input(s, r):
    rows = pl.ds(r * 512, 512)
    dproj = jnp.concatenate([s.q[rows, :], s.dkr[rows, :]], axis=1)
    grad = nt(dproj, s.weight(CQ, CO))
    xhat = s.xh1[rows, :]
    s.gaing[0:1, :] += jnp.sum(grad * xhat, axis=0, keepdims=True)
    s.dn2[rows, :] += norm_back(grad, xhat, s.gates[rows, 8:9], s.g1[...])


def local_kernel(
    x_in, cot_in, segs, ids, over, g1, g2, bias, wa, wd,
    out_y, out_dx, out_ga, out_gd, out_small, out_bias,
    x, cot, xh1, xh2, heads, pinv, dn2, normed, q, mixed, normed2, dffn, hidden, dpre,
    kv, vk, gates, pu, block, small, gaing, biasg, sem,
):
    s = Plan()
    s.x, s.xh1, s.xh2, s.heads, s.pinv, s.dn2 = x, xh1, xh2, heads, pinv, dn2
    s.cotangent = lambda rows: cot[rows, :]
    s.cotangent_row = lambda r: cot[pl.ds(r * 512, 512), :]
    s.normed, s.q, s.mixed, s.normed2, s.dffn, s.hidden, s.dpre = normed, q, mixed, normed2, dffn, hidden, dpre
    s.kv, s.vk, s.gates, s.pu, s.dkv = kv, vk, gates, pu, block
    s.small, s.gaing, s.biasg, s.segs, s.ids, s.over = small, gaing, biasg, segs, ids, over
    s.g1, s.g2, s.bias = g1, g2, bias
    s.dbranch = s.dffn
    s.dkr = hidden.at[:, 0:256]
    s.dout, s.delta = dpre.at[0:512, :], dpre.at[512:1024, :]
    s.weight = lambda a, b: wa[:, a:b]
    s.down = lambda c: wd[512 * c : 512 * c + 512, :]

    def put(at, value):
        out_ga[:, at : at + value.shape[1]] = value.astype(BF)

    def put_down(c, value):
        out_gd[512 * c : 512 * c + 512, :] = value.astype(BF)

    s.put, s.put_down = put, put_down
    copies = [pltpu.make_async_copy(x_in, x, sem.at[0]), pltpu.make_async_copy(cot_in, cot, sem.at[1])]
    for copy in copies:
        copy.start()
    small[...] = jnp.zeros_like(small)
    gaing[...] = jnp.zeros_like(gaing)
    biasg[...] = jnp.zeros_like(biasg)
    for copy in copies:
        copy.wait()
    nrows = x.shape[0] // 512

    def each(phase):
        lax.fori_loop(0, nrows, lambda r, _: (phase(r), 0)[1], 0)

    each(lambda r: phase_norm1(s, r))
    each(lambda r: phase_forward(s, r))
    each(lambda r: phase_resid(s, r))
    for c in range(4):
        each(lambda r: phase_ffn(s, c, r))
        phase_ffn_grads(s, c)
    finish = pltpu.make_async_copy(x, out_y, sem.at[2])
    finish.start()
    each(lambda r: phase_norm2_back(s, r))
    each(lambda r: phase_back(s, r))
    put(CO, tn(mixed[...], s.dbranch[...]))
    put(CQ, tn(normed[...], q[...]))
    put(CKV, tn(normed[...], s.dkr[...]))
    each(lambda r: phase_input(s, r))
    last = pltpu.make_async_copy(dn2, out_dx, sem.at[3])
    last.start()
    out_small[...] = gaing[...]
    out_bias[...] = biasg[...]
    finish.wait()
    last.wait()


def scratch(tokens):
    f = lambda *shape: pltpu.VMEM(shape, F32)
    b = lambda *shape: pltpu.VMEM(shape, BF)
    t = tokens
    return (
        [f(t, 512)] * 7 + [b(t, 512)] * 7 + [b(t, 128)] * 2
        + [f(t, 128), b(t, 2048), f(512, 128)]
        + [f(8, 512), f(8, 512), f(1, 2048)]
    )


MESH = pl.DeviceIdType.MESH


class Ring:
    def __init__(self):
        self.d = lax.axis_index("dp")
        self.f = lax.axis_index("fsdp")
        self.x, self.c = jnp.right_shift(self.d, 1), jnp.bitwise_and(self.d, 1)
        self.z, self.y = jnp.right_shift(self.f, 1), jnp.bitwise_and(self.f, 1)
        self.ox, self.oc, self.oy = 1 - self.x, 1 - self.c, 1 - self.y
        self.core_peer = (2 * self.x + self.oc, self.f)
        self.x_peer = (2 * self.ox + self.c, self.f)
        self.y_peer = (self.d, 2 * self.z + self.oy)
        self.far_peer = (2 * self.ox + self.c, 2 * self.z + self.oy)
        self.later = [jnp.bitwise_and(self.z + k, 3) for k in (1, 2, 3)]
        self.earlier = [jnp.bitwise_and(self.z - k + 4, 3) for k in (1, 2, 3)]
        self.z_peers = [(self.d, 2 * z + self.y) for z in self.later]


def remote(src, dst, send, recv, peer):
    return pltpu.make_async_remote_copy(
        src_ref=src, dst_ref=dst, send_sem=send, recv_sem=recv, device_id=peer, device_id_type=MESH
    )


class Gather:
    def __init__(self, ring, buf, kinds, send, recv):
        self.ring, self.buf, self.kinds, self.send, self.recv = ring, buf, kinds, send, recv
        self.all = slice(kinds[0][0], kinds[-1][1])

    def copies(self, k, arriving):
        g, b = self.ring, self.buf
        if k == 0:
            at = lambda z: b.at[g.x, g.c, z, g.y, :, self.all]
            moves = [(n, at(g.earlier[n] if arriving else g.z), g.z_peers[n]) for n in range(3)]
        elif k == 3:
            moves = [(7, b.at[:, g.oc if arriving else g.c, :, :, :, self.all], g.core_peer)]
        else:
            moves = []
            x, y = (g.ox, g.oy) if arriving else (g.x, g.y)
            for kind, (lo, hi) in enumerate(self.kinds):
                cols = slice(lo, hi)
                if k == 1:
                    if kind == 0:
                        moves.append((3, b.at[x, g.c, :, g.y, :, cols], g.x_peer))
                    else:
                        moves.append((4, b.at[g.x, g.c, :, y, :, cols], g.y_peer))
                elif kind == 0:
                    moves.append((5, b.at[:, g.c, :, y, :, cols], g.y_peer))
                else:
                    moves.append((6, b.at[x, g.c, :, :, :, cols], g.x_peer))
        return [remote(ref, ref, self.send.at[n], self.recv.at[n], peer) for n, ref, peer in moves]

    def step(self, k):
        if k > 0:
            for copy in self.copies(k - 1, True):
                copy.wait_recv()
        if k < 4:
            for copy in self.copies(k, False):
                copy.start()

    def finish(self):
        for k in range(4):
            for copy in self.copies(k, False):
                copy.wait_send()


class Reduce:
    def __init__(self, ring, buf, kinds, send, recv, landing, write):
        self.ring, self.buf, self.kinds, self.send, self.recv = ring, buf, kinds, send, recv
        self.first, self.halves, self.quarters, self.last = landing
        self.all = slice(kinds[0][0], kinds[-1][1])
        self.write = write

    def copies(self, k):
        g, b = self.ring, self.buf
        if k == 0:
            moves = [(0, b.at[:, g.oc, :, :, :, self.all], self.first, g.core_peer)]
        elif k == 3:
            moves = [
                (5 + n, b.at[g.x, g.c, g.later[n], g.y, :, self.all], self.last.at[n], g.z_peers[n])
                for n in range(3)
            ]
        else:
            moves = []
            for kind, (lo, hi) in enumerate(self.kinds):
                cols = slice(lo, hi)
                if k == 1:
                    if kind == 0:
                        moves.append((1, b.at[:, g.c, :, g.oy, :, cols], self.halves[0], g.y_peer))
                    else:
                        moves.append((2, b.at[g.ox, g.c, :, :, :, cols], self.halves[1], g.x_peer))
                elif kind == 0:
                    moves.append((3, b.at[g.ox, g.c, :, g.y, :, cols], self.quarters[0], g.x_peer))
                else:
                    moves.append((4, b.at[g.x, g.c, :, g.oy, :, cols], self.quarters[1], g.y_peer))
        return [remote(src, dst, self.send.at[n], self.recv.at[n], peer) for n, src, dst, peer in moves]

    def add(self, k):
        g, b = self.ring, self.buf
        if k == 0:
            b[:, g.c, :, :, :, self.all] += self.first[...]
        elif k == 3:
            total = b[g.x, g.c, g.z, g.y, :, self.all].astype(F32)
            for n in range(3):
                total = total + self.last[n].astype(F32)
            self.write(total)
        else:
            for kind, (lo, hi) in enumerate(self.kinds):
                if k == 2:
                    b[g.x, g.c, :, g.y, :, lo:hi] += self.quarters[kind][...]
                elif kind == 0:
                    b[:, g.c, :, g.y, :, lo:hi] += self.halves[0][...]
                else:
                    b[g.x, g.c, :, :, :, lo:hi] += self.halves[1][...]

    def step(self, k):
        if k > 0:
            for copy in self.copies(k - 1):
                copy.wait_recv()
            self.add(k - 1)
        if k < 4:
            for copy in self.copies(k):
                copy.start()

    def finish(self):
        for k in range(4):
            for copy in self.copies(k):
                copy.wait_send()


class GatherOne:
    def __init__(self, ring, buf, z, send, recv):
        self.ring, self.buf, self.z, self.send, self.recv = ring, buf, z, send, recv

    def spread(self):
        g, b = self.ring, self.buf.at[self.ring.x, self.ring.c, self.z, self.ring.y]
        return [remote(b, b, self.send.at[n], self.recv.at[0], g.z_peers[n]) for n in range(3)]

    def copies(self, k, arriving):
        g, b, z = self.ring, self.buf, self.z
        x, y, c = (g.ox, g.oy, g.oc) if arriving else (g.x, g.y, g.c)
        low, high = slice(0, 256), slice(256, 512)
        if k == 1:
            moves = [
                (3, b.at[x, g.c, z, g.y, :, low], g.x_peer), (4, b.at[g.x, g.c, z, y, :, high], g.y_peer),
            ]
        elif k == 2:
            moves = [
                (5, b.at[:, g.c, z, y, :, low], g.y_peer), (6, b.at[x, g.c, z, :, :, high], g.x_peer),
            ]
        else:
            moves = [(7, b.at[:, c, z], g.core_peer)]
        return [remote(ref, ref, self.send.at[n], self.recv.at[n], peer) for n, ref, peer in moves]

    def step(self, k):
        if k == 0:
            @pl.when(self.ring.z == self.z)
            def _():
                for copy in self.spread():
                    copy.start()
        if k == 1:
            @pl.when(self.ring.z != self.z)
            def _():
                self.spread()[0].wait_recv()
        if k > 1:
            for copy in self.copies(k - 1, True):
                copy.wait_recv()
        if 0 < k < 4:
            for copy in self.copies(k, False):
                copy.start()

    def finish(self):
        @pl.when(self.ring.z == self.z)
        def _():
            for copy in self.spread():
                copy.wait_send()

        for k in (1, 2, 3):
            for copy in self.copies(k, False):
                copy.wait_send()


class ReduceOne:
    def __init__(self, ring, buf, z, send, recv, landing, write):
        self.ring, self.buf, self.z, self.send, self.recv = ring, buf, z, send, recv
        self.first, self.halves, self.quarters, self.last = landing
        self.write = write

    def copies(self, k):
        g, b, z = self.ring, self.buf, self.z
        low, high = slice(0, 256), slice(256, 512)
        if k == 0:
            moves = [(0, b.at[:, g.oc, z], self.first, g.core_peer)]
        elif k == 1:
            moves = [
                (1, b.at[:, g.c, z, g.oy, :, low], self.halves[0], g.y_peer),
                (2, b.at[g.ox, g.c, z, :, :, high], self.halves[1], g.x_peer),
            ]
        else:
            moves = [
                (3, b.at[g.ox, g.c, z, g.y, :, low], self.quarters[0], g.x_peer),
                (4, b.at[g.x, g.c, z, g.oy, :, high], self.quarters[1], g.y_peer),
            ]
        return [remote(src, dst, self.send.at[n], self.recv.at[n], peer) for n, src, dst, peer in moves]

    def collect(self, sender):
        g = self.ring
        slot = jnp.bitwise_and(sender - self.z + 3, 3)
        return remote(
            self.buf.at[g.x, g.c, self.z, g.y], self.last.at[slot], self.send.at[5], self.recv.at[5 + slot],
            (g.d, 2 * self.z + g.y),
        )

    def step(self, k):
        g, b, z = self.ring, self.buf, self.z
        low, high = slice(0, 256), slice(256, 512)
        if 0 < k < 4:
            for copy in self.copies(k - 1):
                copy.wait_recv()
        if k == 1:
            b[:, g.c, z] += self.first[...]
        if k == 2:
            b[:, g.c, z, g.y, :, low] += self.halves[0][...]
            b[g.x, g.c, z, :, :, high] += self.halves[1][...]
        if k == 3:
            b[g.x, g.c, z, g.y, :, low] += self.quarters[0][...]
            b[g.x, g.c, z, g.y, :, high] += self.quarters[1][...]

            @pl.when(g.z != z)
            def _():
                self.collect(g.z).start()
        if k < 3:
            for copy in self.copies(k):
                copy.start()
        if k == 4:
            @pl.when(g.z == z)
            def _():
                total = b[g.x, g.c, z, g.y].astype(F32)
                for n in range(3):
                    self.collect((z + 1 + n) % 4).wait_recv()
                    total = total + self.last[n].astype(F32)
                self.write(total)

    def finish(self):
        for k in range(3):
            for copy in self.copies(k):
                copy.wait_send()

        @pl.when(self.ring.z != self.z)
        def _():
            self.collect(self.ring.z).wait_send()


class ReduceShort:
    def __init__(self, ring, buf, cols, send, recv, landing, write):
        self.ring, self.buf, self.all, self.send, self.recv = ring, buf, slice(*cols), send, recv
        self.first, self.last, self.plane = landing
        self.write = write

    def copies(self, k):
        g, b = self.ring, self.buf
        if k == 0:
            moves = [(0, b.at[:, g.oc, :, :, :, self.all], self.first, g.core_peer)]
        elif k == 1:
            moves = [
                (1, b.at[g.ox, g.c, :, g.y, :, self.all], self.plane.at[0], g.x_peer),
                (2, b.at[g.x, g.c, :, g.oy, :, self.all], self.plane.at[1], g.y_peer),
                (3, b.at[g.ox, g.c, :, g.oy, :, self.all], self.plane.at[2], g.far_peer),
            ]
        else:
            moves = [
                (5 + n, b.at[g.x, g.c, g.later[n], g.y, :, self.all], self.last.at[n], g.z_peers[n])
                for n in range(3)
            ]
        return [remote(src, dst, self.send.at[n], self.recv.at[n], peer) for n, src, dst, peer in moves]

    def step(self, k):
        g, b = self.ring, self.buf
        if k > 0:
            for copy in self.copies(k - 1):
                copy.wait_recv()
        if k == 1:
            b[:, g.c, :, :, :, self.all] += self.first[...]
        if k > 1:
            mine = (g.x, g.c, slice(None), g.y) if k == 2 else (g.x, g.c, g.z, g.y)
            total = b[(*mine, slice(None), self.all)].astype(F32)
            for n in range(3):
                total = total + (self.plane if k == 2 else self.last)[n].astype(F32)
            if k == 2:
                b[(*mine, slice(None), self.all)] = total.astype(BF)
            else:
                self.write(total)
        if k < 3:
            for copy in self.copies(k):
                copy.start()

    def finish(self):
        for k in range(3):
            for copy in self.copies(k):
                copy.wait_send()


def landing_shapes(rows, kinds):
    b = lambda *shape: pltpu.VMEM(shape, BF)
    if isinstance(kinds, int):
        return [
            b(2, 2, rows, 512), b(3, rows, 512), b(2, rows, 256), b(rows, 256), b(2, rows, 256), b(rows, 256),
        ]
    if isinstance(kinds[0], int):
        n = kinds[1] - kinds[0]
        return [b(2, 4, 2, rows, n), b(3, rows, n), b(3, 4, rows, n)]
    n = kinds[-1][1] - kinds[0][0]
    shapes = [b(2, 4, 2, rows, n), b(3, rows, n)]
    for kind, (lo, hi) in enumerate(kinds):
        shapes.append(b(2, 4, rows, hi - lo) if kind == 0 else b(4, 2, rows, hi - lo))
        shapes.append(b(4, rows, hi - lo))
    return shapes


def halves(lo, hi, cut=None):
    cut = (lo + hi) // 2 if cut is None else cut
    return ((lo, cut), (cut, hi))


GATHERS = (
    ("P0", halves(CQ, CO)), ("P1", halves(CO, CU)), ("U0", halves(CU, CU + 512)), ("D0", 0),
    ("U1", halves(CU + 512, CU + 1024)), ("D1", 1), ("U2", halves(CU + 1024, CW)), ("D2", 2), ("D3", 3),
)
REDUCES = (
    ("u0", halves(CU, CU + 512)), ("u1", halves(CU + 512, CU + 1024)),
    ("u2", halves(CU + 1024, CU + 1536)), ("u3", halves(CU + 1536, CW)),
    ("d0", 0), ("d1", 1), ("d2", 2), ("d3", 3), ("o", halves(CO, CU)),
    ("q", (CQ, CR)), ("r", (CR, CO)),
)
SHARED = {"d2": "d0", "d3": "d1"}
SCHEDULE = {
    "go": (("P0", 0),),
    "P0": (("P0", 1), ("P1", 0), ("U0", 0), ("D0", 0), ("P0", 2), ("U1", 0), ("D1", 0), ("P1", 1), ("U0", 1), ("P0", 3), ("U2", 0), ("D2", 0), ("D3", 0), ("P1", 2), ("D0", 1), ("U0", 2), ("P0", 4),),
    "fwd0.3": (("U1", 1),),
    "fwd1.1": (("D1", 1), ("P1", 3),),
    "fwd1.2": (("D0", 2),),
    "fwd1.4": (("U0", 3),),
    "fwd2.0": (("U2", 1),),
    "fwd2.2": (("U1", 2), ("P1", 4),),
    "fwd2.4": (("D2", 1),),
    "fwd2.5": (("D1", 2), ("U0", 4),),
    "res.1": (("D0", 3),),
    "ffn0": (("D3", 1), ("U2", 2), ("U1", 3), ("D0", 4),),
    "ffn0.1": (("D2", 2),),
    "ffn0.2": (("U1", 4), ("D1", 3), ("D3", 2),),
    "grads0": (("d0", 0), ("u0", 0),),
    "ffn1": (("U2", 3), ("D1", 4),),
    "ffn1.1": (("D2", 3), ("d0", 1),),
    "ffn1.2": (("D3", 3), ("u0", 1),),
    "grads1": (("d1", 0), ("u1", 0), ("U2", 4), ("D2", 4),),
    "ffn2.0": (("D3", 4), ("d0", 2), ("d1", 1),),
    "ffn2.1": (("u0", 2), ("u1", 1),),
    "grads2": (("d2", 0), ("u2", 0), ("d0", 3), ("d1", 2), ("u0", 3),),
    "ffn3.0": (("u1", 2), ("d2", 1),),
    "ffn3.1": (("u2", 1),),
    "ffn3.2": (("d1", 3),),
    "grads3": (("d3", 0), ("u3", 0), ("u1", 3), ("d2", 2), ("d0", 4),),
    "back0.0": (("u2", 2), ("u0", 4), ("d3", 1),),
    "back0.1": (("u3", 1),),
    "back0.3": (("d2", 3), ("d1", 4),),
    "back0.4": (("u1", 4), ("u2", 3),),
    "og": (("o", 0), ("d3", 2), ("u3", 2),),
    "back1.3": (("o", 1), ("d2", 4),),
    "back1.4": (("u2", 4),),
    "back2.0": (("d3", 3),),
    "back2.1": (("u3", 3),),
    "back2.4": (("o", 2),),
    "qg": (("q", 0),),
    "inp.2": (("q", 1), ("o", 3), ("d3", 4),),
    "end": (("r", 0), ("u3", 4), ("r", 1), ("o", 4), ("q", 2), ("r", 2), ("q", 3), ("r", 3),),
}


def mega_kernel(
    x_in, cot_in, segs_in, ids_in, over_in, g1_in, g2_in, bias_in, router_in, q_in, kv_in, o_in, up_in, down_in,
    x, dn2, out_g1, out_router, out_q, out_kv, out_o, out_g2, out_up, out_bias, out_down,
    xh1, xh2, heads, pinv, normed, q, mixed, normed2, dffn, hidden, dpre,
    kv, vk, gates, pu, block, small, gaing, biasg,
    sem, cot_row, segs, ids, over, small_in, router_at, bias_at, wa, wd, ga, gd, g1, g2, bias, tiny, ag_send, ag_recv, rs_send, rs_recv, *landing,
):
    s = Plan()
    s.x, s.xh1, s.xh2, s.heads, s.pinv, s.dn2 = x, xh1, xh2, heads, pinv, dn2
    s.cotangent = lambda rows: dn2[rows, :]

    def fetch_row(r):
        return pltpu.make_async_copy(cot_in.at[512 * r : 512 * r + 512], cot_row, sem.at[17 + r])

    def cotangent_row(r):
        fetch_row(r).wait()
        return cot_row[...]

    s.cotangent_row = cotangent_row
    s.normed, s.q, s.mixed, s.normed2, s.dffn, s.hidden, s.dpre = normed, q, mixed, normed2, dffn, hidden, dpre
    s.kv, s.vk, s.gates, s.pu, s.dkv = kv, vk, gates, pu, block
    s.small, s.gaing, s.biasg, s.segs, s.ids, s.over = small, gaing, biasg, segs, ids, over
    s.g1, s.g2, s.bias = g1, g2, bias
    s.dbranch = s.dffn
    s.dkr = hidden.at[:, 0:256]
    s.dout, s.delta = dpre.at[0:512, :], dpre.at[512:1024, :]
    s.weight = lambda a, b: wa[:, :, :, :, :, a:b].reshape(512, b - a)
    s.down = lambda c: wd[:, :, c].reshape(512, 512)

    def put(at, value):
        n = value.shape[1]
        ga[:, :, :, :, :, at : at + n] = value.astype(BF).reshape(2, 2, 4, 2, 16, n)

    def put_down(c, value):
        gd[:, :, c] = value.astype(BF).reshape(2, 2, 2, 64, 512)

    s.put, s.put_down = put, put_down
    g = Ring()
    peers = [g.core_peer, g.x_peer, g.y_peer, g.far_peer] + g.z_peers
    barrier = pltpu.get_barrier_semaphore()
    for peer in peers:
        pl.semaphore_signal(barrier, inc=1, device_id=peer, device_id_type=MESH)
    moves = [
        (q_in, dn2.at[0:16]), (o_in, dn2.at[16:32]), (kv_in, dn2.at[32:48, 0:128]), (down_in, dn2.at[128:192]),
        (router_in, router_at), (g1_in, small_in.at[0:1]), (g2_in, small_in.at[8:9]), (bias_in, bias_at),
    ]
    moves += [
        (up_in.at[:, 512 * k : 512 * k + 512], dn2.at[48 + 16 * k : 64 + 16 * k]) for k in range(4)
    ]
    moves += [(x_in, x), (segs_in, segs), (ids_in, ids), (over_in, over), (cot_in, dn2)]
    copies = [pltpu.make_async_copy(src, dst, sem.at[n]) for n, (src, dst) in enumerate(moves)]
    for copy in copies[:16]:
        copy.start()
    for copy in copies[:12]:
        copy.wait()

    wa[g.x, g.c, g.z, g.y, :, CQ:CKV] = dn2[0:16, :].astype(BF)
    wa[g.x, g.c, g.z, g.y, :, CKV:CR] = dn2[32:48, 0:128].astype(BF)
    wa[g.x, g.c, g.z, g.y, :, CO:CU] = dn2[16:32, :].astype(BF)
    for k in range(16):
        at = CU + 512 * (k % 4) + 128 * (k // 4)
        wa[g.x, g.c, g.z, g.y, :, at : at + 128] = dn2[
            48 + 16 * (k // 4) : 64 + 16 * (k // 4), 128 * (k % 4) : 128 * (k % 4) + 128
        ].astype(BF)
    wd[g.x, g.c, g.z, g.y] = dn2[128:192, :].astype(BF)
    tiny[...] = jnp.zeros_like(tiny)
    tiny[0:8, 0:16] = router_at[...]
    tiny[8:9, 0:16] = small_in[0:1]
    tiny[9:10, 0:16] = small_in[8:9]
    tiny[16:17, 0:64] = bias_at[...]
    turned = tn(
        tiny[0:16, :].astype(BF), one_where(rows_of((16, 128)) == lanes((16, 128)))
    )[0:16]
    shifted = nn(tiny[16:32, :].astype(BF), one_where(rows_of((128, 128)) + 64 == lanes((128, 128))))
    wa[g.x, g.c, g.z, g.y, :, CR:CO] = (turned + shifted).astype(BF)

    copies[16].start()
    pl.semaphore_wait(barrier, len(peers))
    parts = {}
    for k, (name, kinds) in enumerate(GATHERS):
        make, buf = (GatherOne, wd) if name[0] == "D" else (Gather, wa)
        parts[name] = make(g, buf, kinds, ag_send.at[k], ag_recv.at[k])

    def write_to(ref, at=0):
        def write(total):
            ref[:, at : at + total.shape[1]] = total

        return write

    def write_q(total):
        out_q[...] = total[:, :512]
        out_kv[...] = total[:, 512:]

    def write_small(total):
        turned = total.T
        out_router[...] = turned[0:8]
        out_g1[...] = turned[8:9]
        out_g2[...] = turned[9:10]
        out_bias[...] = pltpu.roll(total, 64, 1)[0:1, 0:64]

    def write_up(c):
        def write(total):
            for k in range(4):
                at = 512 * k + 128 * c
                out_up[:, at : at + 128] = total[:, 128 * k : 128 * k + 128]

        return write

    writes = [write_up(c) for c in range(4)] + [write_to(out_down)] * 4 + [write_to(out_o), write_q, write_small]
    spots = list(landing)
    for k, (name, kinds) in enumerate(REDUCES):
        first = parts[SHARED[name]].first if name in SHARED else spots.pop(0)
        last = spots.pop(0)
        if name in ("q", "r"):
            parts[name] = ReduceShort(
                g, ga, kinds, rs_send.at[k], rs_recv.at[k], (first, last, spots.pop(0)), writes[k]
            )
            continue
        halves_in, quarters_in = [], []
        for _ in range(2 if isinstance(kinds, int) else len(kinds)):
            halves_in.append(spots.pop(0))
            quarters_in.append(spots.pop(0))
        make, buf = (ReduceOne, gd) if name[0] == "d" else (Reduce, ga)
        parts[name] = make(
            g, buf, kinds, rs_send.at[k], rs_recv.at[k],
            (first, halves_in, quarters_in, last), writes[k],
        )

    def hook(name):
        for part, k in SCHEDULE.get(name, ()):
            parts[part].step(k)

    hook("go")
    small[...] = jnp.zeros_like(small)
    gaing[...] = jnp.zeros_like(gaing)
    biasg[...] = jnp.zeros_like(biasg)
    nrows = x.shape[0] // 512

    def each(phase, name):
        def body(r, _):
            phase(r)
            for k in range(nrows):
                if SCHEDULE.get(name + "." + str(k)):
                    pl.when(r == k)(lambda k=k: hook(name + "." + str(k)))
            return 0

        lax.fori_loop(0, nrows, body, 0)

    copies[12].wait()
    each(lambda r: phase_norm1(s, r), "norm")
    hook("P0")
    block[...] = s.weight(CR, CO).astype(F32)
    turned = block[...].T
    g1[...] = turned[8:9]
    g2[...] = turned[9:10]
    even = block[pl.ds(0, 16, stride=32), :]
    odd = block[pl.ds(16, 16, stride=32), :]
    both = jnp.where(lanes((16, 128)) < 64, pltpu.roll(even, 64, 1), odd)
    for k in range(16):
        at = 512 * (k % 4) + 128 * (k // 4)
        bias[:, at : at + 128] = both[k : k + 1]
    for copy in copies[13:]:
        copy.wait()
    for r in range(nrows):
        phase_forward(s, r, lambda i, r=r: hook("fwd" + str(r) + "." + str(i)))
    hook("P1")
    each(lambda r: phase_resid(s, r), "res")
    fetch_row(0).start()
    for c in range(4):
        hook("ffn" + str(c))
        each(lambda r, c=c: phase_ffn(s, c, r), "ffn" + str(c))
        phase_ffn_grads(s, c)
        hook("grads" + str(c))
    def norm2_back(r):
        phase_norm2_back(s, r)
        if r + 1 < nrows:
            fetch_row(r + 1).start()
        else:
            put(CO, tn(mixed[...], s.dbranch[...]))
            hook("og")

    def back_hook(r, i):
        if i == 0 and r > 0:
            for later in range(r + 1, nrows):
                if later > done[-1]:
                    done.append(later)
                    norm2_back(later)
        hook("back" + str(r) + "." + str(i))

    done = [0]
    norm2_back(0)
    for r in range(nrows):
        if r > done[-1]:
            done.append(r)
            norm2_back(r)
        phase_back(s, r, functools.partial(back_hook, r))
    put(CQ, tn(normed[...], q[...]))
    kvr = tn(normed[...], s.dkr[...])
    put(CKV, kvr[:, :128])
    block[...] = kvr[:, 128:]
    hook("qg")
    each(lambda r: phase_input(s, r), "inp")
    turned = gaing[...].T
    lane = lanes((512, 128))
    block[...] = jnp.where(
        lane == 8, turned[:, 0:1], jnp.where(lane == 9, turned[:, 1:2], block[...])
    )
    for k in range(16):
        at = 512 * (k % 4) + 128 * (k // 4)
        tiny[k : k + 1, :] = biasg[:, at : at + 128]
    pieces = tiny[0:16, :]
    low = lanes((16, 128)) < 64
    even = pl.ds(0, 16, stride=32)
    block[even, :] = jnp.where(low, block[even, :], pltpu.roll(pieces, 64, 1))
    odd = pl.ds(16, 16, stride=32)
    block[odd, :] = jnp.where(low, block[odd, :], pieces)
    put(CR, block[...])
    hook("end")
    for part in parts.values():
        part.finish()


def hand_on_kernel(*refs):
    n = len(refs) // 2
    copies = [pltpu.make_async_copy(refs[k], refs[n + k], refs[-1].at[k]) for k in range(n)]
    for copy in copies:
        copy.start()
    for copy in copies:
        copy.wait()


def shards_mega(inputs, cotangent, segment_ids, expert_ids, overflow, norm1_gain, router_weight,
                query_weight, key_value_weight, output_weight, norm2_gain, up_weight, up_bias, down_weight):
    nrows, length, width = inputs.shape
    tokens = nrows * length
    v = pl.BlockSpec(memory_space=pltpu.VMEM)
    h = pl.BlockSpec(memory_space=pl.ANY)
    sd = lambda *shape: jax.ShapeDtypeStruct(shape, F32)
    b = lambda *shape: pltpu.VMEM(shape, BF)
    f = lambda *shape: pltpu.VMEM(shape, F32)
    n = lambda *shape: pltpu.VMEM(shape, jnp.int32)
    landing = []
    for name, kinds in REDUCES:
        landing += landing_shapes(64 if name[0] == "d" else 16, kinds)[name in SHARED :]
    dma = pltpu.SemaphoreType.DMA
    out = pl.pallas_call(
        mega_kernel,
        out_shape=(
            f(tokens, width), f(tokens, width), f(1, 16), f(8, 16), f(16, 512), f(16, 128),
            f(16, 512), f(1, 16), f(16, 2048), f(1, 64), f(64, 512),
        ),
        in_specs=[h] * 14,
        out_specs=(v,) * 11,
        scratch_shapes=scratch(tokens)[2:6] + scratch(tokens)[7:] + [
            dma((20,)), f(512, 512), n(3, 512), n(3, 2, 512), n(3, 2, 512), f(16, 16), f(8, 16), f(1, 64), b(2, 2, 4, 2, 16, CW), b(2, 2, 4, 2, 64, 512), b(2, 2, 4, 2, 16, CW),
            b(2, 2, 4, 2, 64, 512), f(1, 512), f(1, 512), f(1, 2048), f(32, 128),
            dma((9, 8)), dma((9, 8)), dma((11, 8)), dma((11, 8)),
        ] + landing,
        compiler_params=pltpu.CompilerParams(
            collective_id=0, has_side_effects=True, vmem_limit_bytes=VLIM
        ),
    )(
        inputs.reshape(tokens, width), cotangent.reshape(tokens, width), segment_ids,
        jnp.swapaxes(expert_ids, 1, 2), jnp.swapaxes(overflow, 1, 2),
        norm1_gain[None], norm2_gain[None], up_bias[None], router_weight.T, query_weight, key_value_weight,
        output_weight, up_weight, down_weight,
    )
    y, dx, g1, router, query, pair, output, g2, up, bias, down = pl.pallas_call(
        hand_on_kernel,
        out_shape=tuple(sd(*o.shape) for o in out),
        in_specs=[h] * 11,
        out_specs=(h,) * 11,
        scratch_shapes=[dma((11,))],
        compiler_params=pltpu.CompilerParams(vmem_limit_bytes=32 * 1024),
    )(*out)
    return (
        y.reshape(inputs.shape), dx.reshape(inputs.shape), g1[0], router.T, query, pair, output, g2[0],
        up, bias[0], down,
    )


def shards_local(inputs, cotangent, segment_ids, expert_ids, overflow, norm1_gain, router_weight,
                 query_weight, key_value_weight, output_weight, norm2_gain, up_weight, up_bias, down_weight):
    nrows, length, width = inputs.shape
    tokens = nrows * length
    whole = lambda v: lax.all_gather(v.astype(BF), AXES, axis=0, tiled=True)
    g1, g2 = whole(norm1_gain), whole(norm2_gain)
    bias = whole(up_bias)
    router = whole(router_weight)
    parts = [whole(query_weight), whole(key_value_weight), jnp.pad(router, ((0, 0), (0, 120))),
             whole(output_weight), whole(up_weight)]
    wa = jnp.concatenate(parts, axis=1)
    wd = whole(down_weight)
    v = pl.BlockSpec(memory_space=pltpu.VMEM)
    h = pl.BlockSpec(memory_space=pl.ANY)
    sd = jax.ShapeDtypeStruct
    y, dx, ga, gd, small, biasg = pl.pallas_call(
        local_kernel,
        out_shape=(sd((tokens, width), F32), sd((tokens, width), F32), sd((512, CW), BF), sd((2048, 512), BF),
                   sd((8, 512), F32), sd((1, 2048), F32)),
        in_specs=[h, h] + [v] * 8,
        out_specs=(h, h, v, v, v, v),
        scratch_shapes=scratch(tokens) + [pltpu.SemaphoreType.DMA((4,))],
        compiler_params=pltpu.CompilerParams(vmem_limit_bytes=63 * 2**20),
    )(
        inputs.reshape(tokens, width), cotangent.reshape(tokens, width), segment_ids,
        jnp.swapaxes(expert_ids, 1, 2), jnp.swapaxes(overflow, 1, 2),
        g1.astype(F32)[None], g2.astype(F32)[None], bias.astype(F32)[None], wa, wd,
    )
    total = lambda v: lax.psum_scatter(v.astype(F32), AXES, scatter_dimension=0, tiled=True)
    return (
        y.reshape(inputs.shape), dx.reshape(inputs.shape),
        total(small[0]), total(ga[:, CR : CR + 8]), total(ga[:, CQ:CKV]), total(ga[:, CKV:CR]),
        total(ga[:, CO:CU]), total(small[1]), total(ga[:, CU:]), total(biasg[0]), total(gd),
    )


def solution(mesh):
    row3, row2, row1 = P(AXES, None, None), P(AXES, None), P(AXES)
    in_specs = (row3, row3, row2, row3, row3, row1, row2, row2, row2, row2, row1, row2, row1, row2)
    out_specs = (row3, row3, row1, row2, row2, row2, row2, row1, row2, row1, row2)
    small = mesh.shape['dp'] == 4 and mesh.shape['fsdp'] == 8
    shards = shards_mega if small else shards_local
    return jax.shard_map(shards, mesh=mesh, in_specs=in_specs, out_specs=out_specs, check_vma=False)
```

```python
import functools
import jax
import jax.numpy as jnp
from jax import lax
from jax.experimental import pallas as pl
from jax.experimental.pallas import tpu as pltpu
from jax.sharding import PartitionSpec as P

EPS = 1e-05
BIG = -1e30
GELU_C = 0.7978845608028654
GELU_K = 0.044715
BF = jnp.bfloat16
F32 = jnp.float32
AXES = ("dp", "fsdp")
VLIM = 60293120
CQ, CKV, CR, CO, CU, CW = 0, 512, 640, 768, 1280, 3328
TILES = ((0, 128, 0), (128, 256, 256), (128, 384, 768), (256, 256, 1536))


def nn(a, b):
    return lax.dot_general(a, b, (((1,), (0,)), ((), ())), preferred_element_type=F32)


def nt(a, b):
    return lax.dot_general(a, b, (((1,), (1,)), ((), ())), preferred_element_type=F32)


def tn(a, b):
    return lax.dot_general(a, b, (((0,), (0,)), ((), ())), preferred_element_type=F32)


def split(v):
    high = v.astype(BF)
    return high, (v - high.astype(F32)).astype(BF)


def lanes(shape):
    return lax.broadcasted_iota(jnp.int32, shape, len(shape) - 1)


def rows_of(shape):
    return lax.broadcasted_iota(jnp.int32, shape, len(shape) - 2)


def one_where(mask):
    return jnp.where(mask, 1.0, 0.0).astype(BF)


def norm(v):
    centred = v - jnp.mean(v, axis=-1, keepdims=True)
    inverse = lax.rsqrt(jnp.mean(centred * centred, axis=-1, keepdims=True) + EPS)
    return centred * inverse, inverse


def norm_back(grad, xhat, inverse, gain):
    scaled = grad * gain
    inner = (
        scaled
        - jnp.mean(scaled, axis=-1, keepdims=True)
        - xhat * jnp.mean(scaled * xhat, axis=-1, keepdims=True)
    )
    return inner * inverse


def gelu_both(x):
    square = x * x
    slope = (GELU_C * GELU_K) * square + GELU_C
    half = 0.5 * jnp.tanh(x * slope) + 0.5
    value = x * half
    return value, half + (value - value * half) * (6.0 * slope - 4.0 * GELU_C)


def stack_pairs(v):
    return jnp.concatenate([v[:, 128 * p : 128 * p + 128] for p in range(4)], axis=0)


class Plan:
    pass


def keys_of(s, win):
    kv, vk = s.kv[win, :], s.vk[win, :]
    low, zero = lanes(kv.shape) < 64, jnp.zeros_like(kv)
    return jnp.concatenate([jnp.where(low, kv, zero), jnp.where(low, zero, vk)], axis=0)


def values_of(s, win, extra_e, extra_o):
    kv, vk = s.kv[win, :], s.vk[win, :]
    low, zero = lanes(kv.shape) < 64, jnp.zeros_like(kv)
    even = jnp.concatenate([jnp.where(low, vk, zero), extra_e], axis=1)
    odd = jnp.concatenate([jnp.where(low, zero, kv), extra_o], axis=1)
    return jnp.concatenate([even, odd], axis=0)


def phase_norm1(s, r):
    rows = pl.ds(r * 512, 512)
    xhat, inverse = norm(s.x[rows, :])
    s.xh1[rows, :] = xhat
    s.gates[rows, :] = jnp.broadcast_to(inverse, (512, 128))


def phase_forward(s, r, hook=lambda i: None):
    rows = pl.ds(r * 512, 512)
    normed = (s.xh1[rows, :] * s.g1[...]).astype(BF)
    s.normed[rows, :] = normed
    proj = nn(normed, s.weight(CQ, CO))
    query = proj[:, :512].astype(BF)
    s.q[rows, :] = query
    pair = proj[:, CKV:CR].astype(BF).astype(F32)
    swapped = pltpu.roll(pair, 64, 1)
    low = lanes((512, 128)) < 64
    s.kv[rows, :] = jnp.where(low, pair * 0.125, pair).astype(BF)
    s.vk[rows, :] = jnp.where(low, swapped, swapped * 0.125).astype(BF)
    lane = lanes((512, 128))
    logits = jnp.where(lane < 8, proj[:, CR:CO], BIG)
    top = jnp.max(logits, axis=-1, keepdims=True)
    weights = jnp.exp(logits - top)
    prob = weights / jnp.sum(weights, axis=-1, keepdims=True)
    s.small[0:2, :] = jnp.where(s.over[r] == 0, s.ids[r], -1).astype(F32)
    s.small[2:3, :] = s.segs[pl.ds(r, 1), :].astype(F32)
    columns = s.small[...].T
    lane_f = lane.astype(F32)
    route = jnp.where(lane_f == columns[:, 0:1], 1.0, 0.0) + jnp.where(
        lane_f == columns[:, 1:2], 1.0, 0.0
    )
    mix = prob * route
    s.gates[rows, :] = jnp.where(lane == 8, s.gates[rows, :], mix + pltpu.roll(prob, 64, 1))
    seg_row = s.small[2:3, :]
    hook(0)
    for t, (start, width, at) in enumerate(TILES):
        q4 = stack_pairs(query[128 * t : 128 * t + 128])
        win = pl.ds(r * 512 + start, width)
        scores = nt(q4, keys_of(s, win))
        even, odd = scores[:, :width], scores[:, width:]
        if t:
            same = columns[128 * t : 128 * t + 128, 2:3] == seg_row[:, start : start + width]
            bias = jnp.where(same, 0.0, BIG)
            bias = jnp.concatenate([bias] * 4, axis=0)
            even, odd = even + bias, odd + bias
        even = jnp.exp(even - jnp.max(even, axis=-1, keepdims=True)).astype(BF)
        odd = jnp.exp(odd - jnp.max(odd, axis=-1, keepdims=True)).astype(BF)
        both = jnp.concatenate([even, odd], axis=1)
        s.pu[pl.ds(r * 512, 512), at : at + 2 * width] = both
        low_w = lanes((width, 128)) < 64
        one_e = jnp.where(low_w, 1.0, 0.0).astype(BF)
        one_o = jnp.where(low_w, 0.0, 1.0).astype(BF)
        out = nn(both, values_of(s, win, one_e, one_o))
        inverse = 1.0 / out[:, 128:]
        out = out[:, :128] * inverse
        for p in range(4):
            at_rows = pl.ds(r * 512 + 128 * t, 128)
            s.heads[at_rows, 128 * p : 128 * p + 128] = out[128 * p : 128 * p + 128]
            s.pinv[at_rows, 128 * p : 128 * p + 128] = inverse[128 * p : 128 * p + 128]
        hook(1 + t)
    mixed = (s.heads[rows, :] * expand(mix)).astype(BF)
    s.mixed[rows, :] = mixed
    hook(5)


def phase_resid(s, r):
    rows = pl.ds(r * 512, 512)
    resid = s.x[rows, :] + nn(s.mixed[rows, :], s.weight(CO, CU))
    s.x[rows, :] = resid
    xhat, inverse = norm(resid)
    s.xh2[rows, :] = xhat
    s.gates[rows, :] = jnp.where(lanes((512, 128)) == 9, inverse, s.gates[rows, :])
    s.normed2[rows, :] = (xhat * s.g2[...]).astype(BF)
    s.dffn[rows, :] = s.cotangent(rows).astype(BF)


def expand(per_expert):
    high, rest = split(per_expert)
    spread = one_where(
        jnp.bitwise_and(rows_of((256, 512)), 127) == jnp.right_shift(lanes((256, 512)), 6)
    )
    return nn(jnp.concatenate([high, rest], axis=1), spread)


def phase_ffn(s, c, r):
    rows = pl.ds(r * 512, 512)
    up = s.weight(CU + 512 * c, CU + 512 * c + 512)
    down = s.down(c)
    pre = nn(s.normed2[rows, :], up) + s.bias[:, 512 * c : 512 * c + 512]
    dhidden = nt(s.dffn[rows, :], down)
    value, slope = gelu_both(pre)
    dpre = dhidden * slope
    s.biasg[:, 512 * c : 512 * c + 512] += jnp.sum(dpre, axis=0, keepdims=True)
    hidden = value.astype(BF)
    dpre = dpre.astype(BF)
    s.hidden[rows, :] = hidden
    s.dpre[rows, :] = dpre
    s.x[rows, :] += nn(hidden, down)
    back = nt(dpre, up)
    if c == 0:
        s.dn2[rows, :] = back
    else:
        s.dn2[rows, :] += back


def phase_ffn_grads(s, c):
    s.put_down(c, tn(s.hidden[...], s.dffn[...]))
    s.put(CU + 512 * c, tn(s.normed2[...], s.dpre[...]))


def phase_norm2_back(s, r):
    rows = pl.ds(r * 512, 512)
    grad = s.dn2[rows, :]
    xhat = s.xh2[rows, :]
    s.gaing[1:2, :] += jnp.sum(grad * xhat, axis=0, keepdims=True)
    dresid = s.cotangent_row(r) + norm_back(grad, xhat, s.gates[rows, 9:10], s.g2[...])
    s.dn2[rows, :] = dresid
    dbranch = dresid.astype(BF)
    s.dbranch[rows, :] = dbranch


def phase_back(s, r, hook=lambda i: None):
    rows = pl.ds(r * 512, 512)
    dmixed = nt(s.dbranch[rows, :], s.weight(CO, CU))
    heads = s.heads[rows, :]
    gather = one_where(
        lanes((1024, 128)) == jnp.right_shift(jnp.bitwise_and(rows_of((1024, 128)), 511), 6)
    )
    dgate = nn(jnp.concatenate(split(dmixed * heads), axis=1), gather)
    gates = s.gates[rows, :]
    first8 = lanes((512, 128)) < 8
    mix = jnp.where(first8, gates, 0.0)
    prob = jnp.where(first8, pltpu.roll(gates, 64, 1), 0.0)
    weighted = dgate * mix
    dlogits = weighted - prob * jnp.sum(weighted, axis=-1, keepdims=True)
    s.dkr[rows, 128:256] = dlogits.astype(BF)
    dout = (dmixed * expand(mix) * s.pinv[rows, :]).astype(BF)
    s.dout[...] = dout
    within = dout.astype(F32) * heads
    high, rest = split(within)
    block = one_where(
        jnp.right_shift(jnp.bitwise_and(rows_of((256, 128)), 127), 6)
        == jnp.right_shift(lanes((256, 128)), 6)
    )
    place = jnp.bitwise_and(lanes((512, 128)), 63)
    for p in range(4):
        cols = slice(128 * p, 128 * p + 128)
        total = nn(jnp.concatenate([high[:, cols], rest[:, cols]], axis=1), block)
        first, second = split(total)
        s.delta[:, cols] = jnp.where(
            place == 0, first.astype(F32), jnp.where(place == 1, second.astype(F32), 0.0)
        ).astype(BF)
    s.dkv[...] = jnp.zeros_like(s.dkv)
    hook(0)
    for t, (start, width, at) in enumerate(TILES):
        here = pl.ds(128 * t, 128)
        at_rows = pl.ds(r * 512 + 128 * t, 128)
        win = pl.ds(r * 512 + start, width)
        do4 = stack_pairs(s.dout[here, :])
        de4 = stack_pairs(s.delta[here, :])
        lane = lanes((width, 128))
        neg_e = jnp.where(lane < 2, -1.0, 0.0).astype(BF)
        neg_o = jnp.where(jnp.bitwise_and(lane, 126) == 64, -1.0, 0.0).astype(BF)
        dprob = nt(jnp.concatenate([do4, de4], axis=1), values_of(s, win, neg_e, neg_o))
        weights = s.pu[pl.ds(r * 512, 512), at : at + 2 * width]
        dscore = (weights.astype(F32) * dprob).astype(BF)
        dq4 = nn(dscore, keys_of(s, win)).astype(BF)
        q4 = stack_pairs(s.q[at_rows, :])
        dk = tn(dscore, q4)
        dv = tn(weights, do4)
        for p in range(4):
            s.q[at_rows, 128 * p : 128 * p + 128] = dq4[128 * p : 128 * p + 128]
        s.dkv[pl.ds(start, width), :] += jnp.where(
            lane < 64,
            (dk[:width] + pltpu.roll(dk[width:], 64, 1)) * 0.125,
            dv[width:] + pltpu.roll(dv[:width], 64, 1),
        )
        if t < 3:
            hook(1 + t)
    s.dkr[rows, 0:128] = s.dkv[...].astype(BF)
    hook(4)


def phase_input(s, r):
    rows = pl.ds(r * 512, 512)
    dproj = jnp.concatenate([s.q[rows, :], s.dkr[rows, :]], axis=1)
    grad = nt(dproj, s.weight(CQ, CO))
    xhat = s.xh1[rows, :]
    s.gaing[0:1, :] += jnp.sum(grad * xhat, axis=0, keepdims=True)
    s.dn2[rows, :] += norm_back(grad, xhat, s.gates[rows, 8:9], s.g1[...])


def local_kernel(
    x_in, cot_in, segs, ids, over, g1, g2, bias, wa, wd,
    out_y, out_dx, out_ga, out_gd, out_small, out_bias,
    x, cot, xh1, xh2, heads, pinv, dn2, normed, q, mixed, normed2, dffn, hidden, dpre,
    kv, vk, gates, pu, block, small, gaing, biasg, sem,
):
    s = Plan()
    s.x, s.xh1, s.xh2, s.heads, s.pinv, s.dn2 = x, xh1, xh2, heads, pinv, dn2
    s.cotangent = lambda rows: cot[rows, :]
    s.cotangent_row = lambda r: cot[pl.ds(r * 512, 512), :]
    s.normed, s.q, s.mixed, s.normed2, s.dffn, s.hidden, s.dpre = normed, q, mixed, normed2, dffn, hidden, dpre
    s.kv, s.vk, s.gates, s.pu, s.dkv = kv, vk, gates, pu, block
    s.small, s.gaing, s.biasg, s.segs, s.ids, s.over = small, gaing, biasg, segs, ids, over
    s.g1, s.g2, s.bias = g1, g2, bias
    s.dbranch = s.dffn
    s.dkr = hidden.at[:, 0:256]
    s.dout, s.delta = dpre.at[0:512, :], dpre.at[512:1024, :]
    s.weight = lambda a, b: wa[:, a:b]
    s.down = lambda c: wd[512 * c : 512 * c + 512, :]

    def put(at, value):
        out_ga[:, at : at + value.shape[1]] = value.astype(BF)

    def put_down(c, value):
        out_gd[512 * c : 512 * c + 512, :] = value.astype(BF)

    s.put, s.put_down = put, put_down
    copies = [pltpu.make_async_copy(x_in, x, sem.at[0]), pltpu.make_async_copy(cot_in, cot, sem.at[1])]
    for copy in copies:
        copy.start()
    small[...] = jnp.zeros_like(small)
    gaing[...] = jnp.zeros_like(gaing)
    biasg[...] = jnp.zeros_like(biasg)
    for copy in copies:
        copy.wait()
    nrows = x.shape[0] // 512

    def each(phase):
        lax.fori_loop(0, nrows, lambda r, _: (phase(r), 0)[1], 0)

    each(lambda r: phase_norm1(s, r))
    each(lambda r: phase_forward(s, r))
    each(lambda r: phase_resid(s, r))
    for c in range(4):
        each(lambda r: phase_ffn(s, c, r))
        phase_ffn_grads(s, c)
    finish = pltpu.make_async_copy(x, out_y, sem.at[2])
    finish.start()
    each(lambda r: phase_norm2_back(s, r))
    each(lambda r: phase_back(s, r))
    put(CO, tn(mixed[...], s.dbranch[...]))
    put(CQ, tn(normed[...], q[...]))
    put(CKV, tn(normed[...], s.dkr[...]))
    each(lambda r: phase_input(s, r))
    last = pltpu.make_async_copy(dn2, out_dx, sem.at[3])
    last.start()
    out_small[...] = gaing[...]
    out_bias[...] = biasg[...]
    finish.wait()
    last.wait()


def scratch(tokens):
    f = lambda *shape: pltpu.VMEM(shape, F32)
    b = lambda *shape: pltpu.VMEM(shape, BF)
    t = tokens
    return (
        [f(t, 512)] * 7 + [b(t, 512)] * 7 + [b(t, 128)] * 2
        + [f(t, 128), b(t, 2048), f(512, 128)]
        + [f(8, 512), f(8, 512), f(1, 2048)]
    )


MESH = pl.DeviceIdType.MESH


class Ring:
    def __init__(self):
        self.d = lax.axis_index("dp")
        self.f = lax.axis_index("fsdp")
        self.x, self.c = jnp.right_shift(self.d, 1), jnp.bitwise_and(self.d, 1)
        self.z, self.y = jnp.right_shift(self.f, 1), jnp.bitwise_and(self.f, 1)
        self.ox, self.oc, self.oy = 1 - self.x, 1 - self.c, 1 - self.y
        self.core_peer = (2 * self.x + self.oc, self.f)
        self.x_peer = (2 * self.ox + self.c, self.f)
        self.y_peer = (self.d, 2 * self.z + self.oy)
        self.far_peer = (2 * self.ox + self.c, 2 * self.z + self.oy)
        self.later = [jnp.bitwise_and(self.z + k, 3) for k in (1, 2, 3)]
        self.earlier = [jnp.bitwise_and(self.z - k + 4, 3) for k in (1, 2, 3)]
        self.z_peers = [(self.d, 2 * z + self.y) for z in self.later]


def remote(src, dst, send, recv, peer):
    return pltpu.make_async_remote_copy(
        src_ref=src, dst_ref=dst, send_sem=send, recv_sem=recv, device_id=peer, device_id_type=MESH
    )


class Gather:
    def __init__(self, ring, buf, kinds, send, recv):
        self.ring, self.buf, self.kinds, self.send, self.recv = ring, buf, kinds, send, recv
        self.all = slice(kinds[0][0], kinds[-1][1])

    def copies(self, k, arriving):
        g, b = self.ring, self.buf
        if k == 0:
            at = lambda z: b.at[g.x, g.c, z, g.y, :, self.all]
            moves = [(n, at(g.earlier[n] if arriving else g.z), g.z_peers[n]) for n in range(3)]
        elif k == 3:
            moves = [(7, b.at[:, g.oc if arriving else g.c, :, :, :, self.all], g.core_peer)]
        else:
            moves = []
            x, y = (g.ox, g.oy) if arriving else (g.x, g.y)
            for kind, (lo, hi) in enumerate(self.kinds):
                cols = slice(lo, hi)
                if k == 1:
                    if kind == 0:
                        moves.append((3, b.at[x, g.c, :, g.y, :, cols], g.x_peer))
                    else:
                        moves.append((4, b.at[g.x, g.c, :, y, :, cols], g.y_peer))
                elif kind == 0:
                    moves.append((5, b.at[:, g.c, :, y, :, cols], g.y_peer))
                else:
                    moves.append((6, b.at[x, g.c, :, :, :, cols], g.x_peer))
        return [remote(ref, ref, self.send.at[n], self.recv.at[n], peer) for n, ref, peer in moves]

    def step(self, k):
        if k > 0:
            for copy in self.copies(k - 1, True):
                copy.wait_recv()
        if k < 4:
            for copy in self.copies(k, False):
                copy.start()

    def finish(self):
        for k in range(4):
            for copy in self.copies(k, False):
                copy.wait_send()


class Reduce:
    def __init__(self, ring, buf, kinds, send, recv, landing, write):
        self.ring, self.buf, self.kinds, self.send, self.recv = ring, buf, kinds, send, recv
        self.first, self.halves, self.quarters, self.last = landing
        self.all = slice(kinds[0][0], kinds[-1][1])
        self.write = write

    def copies(self, k):
        g, b = self.ring, self.buf
        if k == 0:
            moves = [(0, b.at[:, g.oc, :, :, :, self.all], self.first, g.core_peer)]
        elif k == 3:
            moves = [
                (5 + n, b.at[g.x, g.c, g.later[n], g.y, :, self.all], self.last.at[n], g.z_peers[n])
                for n in range(3)
            ]
        else:
            moves = []
            for kind, (lo, hi) in enumerate(self.kinds):
                cols = slice(lo, hi)
                if k == 1:
                    if kind == 0:
                        moves.append((1, b.at[:, g.c, :, g.oy, :, cols], self.halves[0], g.y_peer))
                    else:
                        moves.append((2, b.at[g.ox, g.c, :, :, :, cols], self.halves[1], g.x_peer))
                elif kind == 0:
                    moves.append((3, b.at[g.ox, g.c, :, g.y, :, cols], self.quarters[0], g.x_peer))
                else:
                    moves.append((4, b.at[g.x, g.c, :, g.oy, :, cols], self.quarters[1], g.y_peer))
        return [remote(src, dst, self.send.at[n], self.recv.at[n], peer) for n, src, dst, peer in moves]

    def add(self, k):
        g, b = self.ring, self.buf
        if k == 0:
            b[:, g.c, :, :, :, self.all] += self.first[...]
        elif k == 3:
            total = b[g.x, g.c, g.z, g.y, :, self.all].astype(F32)
            for n in range(3):
                total = total + self.last[n].astype(F32)
            self.write(total)
        else:
            for kind, (lo, hi) in enumerate(self.kinds):
                if k == 2:
                    b[g.x, g.c, :, g.y, :, lo:hi] += self.quarters[kind][...]
                elif kind == 0:
                    b[:, g.c, :, g.y, :, lo:hi] += self.halves[0][...]
                else:
                    b[g.x, g.c, :, :, :, lo:hi] += self.halves[1][...]

    def step(self, k):
        if k > 0:
            for copy in self.copies(k - 1):
                copy.wait_recv()
            self.add(k - 1)
        if k < 4:
            for copy in self.copies(k):
                copy.start()

    def finish(self):
        for k in range(4):
            for copy in self.copies(k):
                copy.wait_send()


class GatherOne:
    def __init__(self, ring, buf, z, send, recv):
        self.ring, self.buf, self.z, self.send, self.recv = ring, buf, z, send, recv

    def spread(self):
        g, b = self.ring, self.buf.at[self.ring.x, self.ring.c, self.z, self.ring.y]
        return [remote(b, b, self.send.at[n], self.recv.at[0], g.z_peers[n]) for n in range(3)]

    def copies(self, k, arriving):
        g, b, z = self.ring, self.buf, self.z
        x, y, c = (g.ox, g.oy, g.oc) if arriving else (g.x, g.y, g.c)
        low, high = slice(0, 256), slice(256, 512)
        if k == 1:
            moves = [
                (3, b.at[x, g.c, z, g.y, :, low], g.x_peer), (4, b.at[g.x, g.c, z, y, :, high], g.y_peer),
            ]
        elif k == 2:
            moves = [
                (5, b.at[:, g.c, z, y, :, low], g.y_peer), (6, b.at[x, g.c, z, :, :, high], g.x_peer),
            ]
        else:
            moves = [(7, b.at[:, c, z], g.core_peer)]
        return [remote(ref, ref, self.send.at[n], self.recv.at[n], peer) for n, ref, peer in moves]

    def step(self, k):
        if k == 0:
            @pl.when(self.ring.z == self.z)
            def _():
                for copy in self.spread():
                    copy.start()
        if k == 1:
            @pl.when(self.ring.z != self.z)
            def _():
                self.spread()[0].wait_recv()
        if k > 1:
            for copy in self.copies(k - 1, True):
                copy.wait_recv()
        if 0 < k < 4:
            for copy in self.copies(k, False):
                copy.start()

    def finish(self):
        @pl.when(self.ring.z == self.z)
        def _():
            for copy in self.spread():
                copy.wait_send()

        for k in (1, 2, 3):
            for copy in self.copies(k, False):
                copy.wait_send()


class ReduceOne:
    def __init__(self, ring, buf, z, send, recv, landing, write):
        self.ring, self.buf, self.z, self.send, self.recv = ring, buf, z, send, recv
        self.first, self.halves, self.quarters, self.last = landing
        self.write = write

    def copies(self, k):
        g, b, z = self.ring, self.buf, self.z
        low, high = slice(0, 256), slice(256, 512)
        if k == 0:
            moves = [(0, b.at[:, g.oc, z], self.first, g.core_peer)]
        elif k == 1:
            moves = [
                (1, b.at[:, g.c, z, g.oy, :, low], self.halves[0], g.y_peer),
                (2, b.at[g.ox, g.c, z, :, :, high], self.halves[1], g.x_peer),
            ]
        else:
            moves = [
                (3, b.at[g.ox, g.c, z, g.y, :, low], self.quarters[0], g.x_peer),
                (4, b.at[g.x, g.c, z, g.oy, :, high], self.quarters[1], g.y_peer),
            ]
        return [remote(src, dst, self.send.at[n], self.recv.at[n], peer) for n, src, dst, peer in moves]

    def collect(self, sender):
        g = self.ring
        slot = jnp.bitwise_and(sender - self.z + 3, 3)
        return remote(
            self.buf.at[g.x, g.c, self.z, g.y], self.last.at[slot], self.send.at[5], self.recv.at[5 + slot],
            (g.d, 2 * self.z + g.y),
        )

    def step(self, k):
        g, b, z = self.ring, self.buf, self.z
        low, high = slice(0, 256), slice(256, 512)
        if 0 < k < 4:
            for copy in self.copies(k - 1):
                copy.wait_recv()
        if k == 1:
            b[:, g.c, z] += self.first[...]
        if k == 2:
            b[:, g.c, z, g.y, :, low] += self.halves[0][...]
            b[g.x, g.c, z, :, :, high] += self.halves[1][...]
        if k == 3:
            b[g.x, g.c, z, g.y, :, low] += self.quarters[0][...]
            b[g.x, g.c, z, g.y, :, high] += self.quarters[1][...]

            @pl.when(g.z != z)
            def _():
                self.collect(g.z).start()
        if k < 3:
            for copy in self.copies(k):
                copy.start()
        if k == 4:
            @pl.when(g.z == z)
            def _():
                total = b[g.x, g.c, z, g.y].astype(F32)
                for n in range(3):
                    self.collect((z + 1 + n) % 4).wait_recv()
                    total = total + self.last[n].astype(F32)
                self.write(total)

    def finish(self):
        for k in range(3):
            for copy in self.copies(k):
                copy.wait_send()

        @pl.when(self.ring.z != self.z)
        def _():
            self.collect(self.ring.z).wait_send()


class ReduceShort:
    def __init__(self, ring, buf, cols, send, recv, landing, write):
        self.ring, self.buf, self.all, self.send, self.recv = ring, buf, slice(*cols), send, recv
        self.first, self.last, self.plane = landing
        self.write = write

    def copies(self, k):
        g, b = self.ring, self.buf
        if k == 0:
            moves = [(0, b.at[:, g.oc, :, :, :, self.all], self.first, g.core_peer)]
        elif k == 1:
            moves = [
                (1, b.at[g.ox, g.c, :, g.y, :, self.all], self.plane.at[0], g.x_peer),
                (2, b.at[g.x, g.c, :, g.oy, :, self.all], self.plane.at[1], g.y_peer),
                (3, b.at[g.ox, g.c, :, g.oy, :, self.all], self.plane.at[2], g.far_peer),
            ]
        else:
            moves = [
                (5 + n, b.at[g.x, g.c, g.later[n], g.y, :, self.all], self.last.at[n], g.z_peers[n])
                for n in range(3)
            ]
        return [remote(src, dst, self.send.at[n], self.recv.at[n], peer) for n, src, dst, peer in moves]

    def step(self, k):
        g, b = self.ring, self.buf
        if k > 0:
            for copy in self.copies(k - 1):
                copy.wait_recv()
        if k == 1:
            b[:, g.c, :, :, :, self.all] += self.first[...]
        if k > 1:
            mine = (g.x, g.c, slice(None), g.y) if k == 2 else (g.x, g.c, g.z, g.y)
            total = b[(*mine, slice(None), self.all)].astype(F32)
            for n in range(3):
                total = total + (self.plane if k == 2 else self.last)[n].astype(F32)
            if k == 2:
                b[(*mine, slice(None), self.all)] = total.astype(BF)
            else:
                self.write(total)
        if k < 3:
            for copy in self.copies(k):
                copy.start()

    def finish(self):
        for k in range(3):
            for copy in self.copies(k):
                copy.wait_send()


def landing_shapes(rows, kinds):
    b = lambda *shape: pltpu.VMEM(shape, BF)
    if isinstance(kinds, int):
        return [
            b(2, 2, rows, 512), b(3, rows, 512), b(2, rows, 256), b(rows, 256), b(2, rows, 256), b(rows, 256),
        ]
    if isinstance(kinds[0], int):
        n = kinds[1] - kinds[0]
        return [b(2, 4, 2, rows, n), b(3, rows, n), b(3, 4, rows, n)]
    n = kinds[-1][1] - kinds[0][0]
    shapes = [b(2, 4, 2, rows, n), b(3, rows, n)]
    for kind, (lo, hi) in enumerate(kinds):
        shapes.append(b(2, 4, rows, hi - lo) if kind == 0 else b(4, 2, rows, hi - lo))
        shapes.append(b(4, rows, hi - lo))
    return shapes


def halves(lo, hi, cut=None):
    cut = (lo + hi) // 2 if cut is None else cut
    return ((lo, cut), (cut, hi))


GATHERS = (
    ("P0", halves(CQ, CO)), ("P1", halves(CO, CU)), ("U0", halves(CU, CU + 512)), ("D0", 0),
    ("U1", halves(CU + 512, CU + 1024)), ("D1", 1), ("U2", halves(CU + 1024, CW)), ("D2", 2), ("D3", 3),
)
REDUCES = (
    ("u0", halves(CU, CU + 512)), ("u1", halves(CU + 512, CU + 1024)),
    ("u2", halves(CU + 1024, CU + 1536)), ("u3", halves(CU + 1536, CW)),
    ("d0", 0), ("d1", 1), ("d2", 2), ("d3", 3), ("o", halves(CO, CU)),
    ("q", (CQ, CR)), ("r", (CR, CO)),
)
SHARED = {"d2": "d0", "d3": "d1"}
SCHEDULE = {
    "go": (("P0", 0),),
    "P0": (("P0", 1), ("P1", 0), ("U0", 0), ("D0", 0), ("P0", 2), ("U1", 0), ("D1", 0), ("P1", 1), ("U0", 1), ("P0", 3), ("U2", 0), ("D2", 0), ("D3", 0), ("P1", 2), ("D0", 1), ("U0", 2), ("P0", 4),),
    "fwd0.3": (("U1", 1),),
    "fwd1.1": (("D1", 1), ("P1", 3),),
    "fwd1.2": (("D0", 2),),
    "fwd1.4": (("U0", 3),),
    "fwd2.0": (("U2", 1),),
    "fwd2.2": (("U1", 2), ("P1", 4),),
    "fwd2.4": (("D2", 1),),
    "fwd2.5": (("D1", 2), ("U0", 4),),
    "res.1": (("D0", 3),),
    "ffn0": (("D3", 1), ("U2", 2), ("U1", 3), ("D0", 4),),
    "ffn0.1": (("D2", 2),),
    "ffn0.2": (("U1", 4), ("D1", 3), ("D3", 2),),
    "grads0": (("d0", 0), ("u0", 0),),
    "ffn1": (("U2", 3), ("D1", 4),),
    "ffn1.1": (("D2", 3), ("d0", 1),),
    "ffn1.2": (("D3", 3),),
    "grads1": (("d1", 0), ("u1", 0), ("u0", 1), ("U2", 4), ("D2", 4),),
    "ffn2.0": (("D3", 4),),
    "ffn2.1": (("d0", 2), ("d1", 1), ("u1", 1),),
    "grads2": (("d2", 0), ("u2", 0), ("u0", 2), ("d0", 3),),
    "ffn3.1": (("d1", 2), ("d2", 1), ("u1", 2), ("u2", 1), ("u0", 3),),
    "grads3": (("d3", 0), ("u3", 0), ("d1", 3), ("d0", 4),),
    "back0.0": (("d2", 2), ("u0", 4), ("u1", 3), ("d3", 1),),
    "back0.4": (("u3", 1), ("u2", 2),),
    "og": (("o", 0), ("d2", 3), ("d1", 4), ("d3", 2), ("u1", 4),),
    "back1.4": (("u3", 2), ("u2", 3), ("o", 1),),
    "back2.0": (("d3", 3),),
    "back2.4": (("d2", 4), ("u3", 3),),
    "qg": (("q", 0), ("u2", 4), ("o", 2),),
    "inp.1": (("q", 1),),
    "end": (("r", 0), ("d3", 4), ("o", 3), ("u3", 4), ("r", 1), ("q", 2), ("o", 4), ("r", 2), ("q", 3), ("r", 3),),
}


def mega_kernel(
    x_in, cot_in, segs_in, ids_in, over_in, g1_in, g2_in, bias_in, router_in, q_in, kv_in, o_in, up_in, down_in,
    x, dn2, out_g1, out_router, out_q, out_kv, out_o, out_g2, out_up, out_bias, out_down,
    xh1, xh2, heads, pinv, normed, q, mixed, normed2, dffn, hidden, dpre,
    kv, vk, gates, pu, block, small, gaing, biasg,
    sem, cot_row, segs, ids, over, small_in, router_at, bias_at, wa, wd, ga, gd, g1, g2, bias, tiny, ag_send, ag_recv, rs_send, rs_recv, *landing,
):
    s = Plan()
    s.x, s.xh1, s.xh2, s.heads, s.pinv, s.dn2 = x, xh1, xh2, heads, pinv, dn2
    s.cotangent = lambda rows: dn2[rows, :]

    def fetch_row(r):
        return pltpu.make_async_copy(cot_in.at[512 * r : 512 * r + 512], cot_row, sem.at[17 + r])

    def cotangent_row(r):
        fetch_row(r).wait()
        return cot_row[...]

    s.cotangent_row = cotangent_row
    s.normed, s.q, s.mixed, s.normed2, s.dffn, s.hidden, s.dpre = normed, q, mixed, normed2, dffn, hidden, dpre
    s.kv, s.vk, s.gates, s.pu, s.dkv = kv, vk, gates, pu, block
    s.small, s.gaing, s.biasg, s.segs, s.ids, s.over = small, gaing, biasg, segs, ids, over
    s.g1, s.g2, s.bias = g1, g2, bias
    s.dbranch = s.dffn
    s.dkr = hidden.at[:, 0:256]
    s.dout, s.delta = dpre.at[0:512, :], dpre.at[512:1024, :]
    s.weight = lambda a, b: wa[:, :, :, :, :, a:b].reshape(512, b - a)
    s.down = lambda c: wd[:, :, c].reshape(512, 512)

    def put(at, value):
        n = value.shape[1]
        ga[:, :, :, :, :, at : at + n] = value.astype(BF).reshape(2, 2, 4, 2, 16, n)

    def put_down(c, value):
        gd[:, :, c] = value.astype(BF).reshape(2, 2, 2, 64, 512)

    s.put, s.put_down = put, put_down
    g = Ring()
    peers = [g.core_peer, g.x_peer, g.y_peer, g.far_peer] + g.z_peers
    barrier = pltpu.get_barrier_semaphore()
    for peer in peers:
        pl.semaphore_signal(barrier, inc=1, device_id=peer, device_id_type=MESH)
    moves = [
        (q_in, dn2.at[0:16]), (o_in, dn2.at[16:32]), (kv_in, dn2.at[32:48, 0:128]), (down_in, dn2.at[128:192]),
        (router_in, router_at), (g1_in, small_in.at[0:1]), (g2_in, small_in.at[8:9]), (bias_in, bias_at),
    ]
    moves += [
        (up_in.at[:, 512 * k : 512 * k + 512], dn2.at[48 + 16 * k : 64 + 16 * k]) for k in range(4)
    ]
    moves += [(x_in, x), (segs_in, segs), (ids_in, ids), (over_in, over), (cot_in, dn2)]
    copies = [pltpu.make_async_copy(src, dst, sem.at[n]) for n, (src, dst) in enumerate(moves)]
    for copy in copies[:16]:
        copy.start()
    for copy in copies[:12]:
        copy.wait()

    wa[g.x, g.c, g.z, g.y, :, CQ:CKV] = dn2[0:16, :].astype(BF)
    wa[g.x, g.c, g.z, g.y, :, CKV:CR] = dn2[32:48, 0:128].astype(BF)
    wa[g.x, g.c, g.z, g.y, :, CO:CU] = dn2[16:32, :].astype(BF)
    for k in range(16):
        at = CU + 512 * (k % 4) + 128 * (k // 4)
        wa[g.x, g.c, g.z, g.y, :, at : at + 128] = dn2[
            48 + 16 * (k // 4) : 64 + 16 * (k // 4), 128 * (k % 4) : 128 * (k % 4) + 128
        ].astype(BF)
    wd[g.x, g.c, g.z, g.y] = dn2[128:192, :].astype(BF)
    tiny[...] = jnp.zeros_like(tiny)
    tiny[0:8, 0:16] = router_at[...]
    tiny[8:9, 0:16] = small_in[0:1]
    tiny[9:10, 0:16] = small_in[8:9]
    tiny[16:17, 0:64] = bias_at[...]
    turned = tn(
        tiny[0:16, :].astype(BF), one_where(rows_of((16, 128)) == lanes((16, 128)))
    )[0:16]
    shifted = nn(tiny[16:32, :].astype(BF), one_where(rows_of((128, 128)) + 64 == lanes((128, 128))))
    wa[g.x, g.c, g.z, g.y, :, CR:CO] = (turned + shifted).astype(BF)

    copies[16].start()
    pl.semaphore_wait(barrier, len(peers))
    parts = {}
    for k, (name, kinds) in enumerate(GATHERS):
        make, buf = (GatherOne, wd) if name[0] == "D" else (Gather, wa)
        parts[name] = make(g, buf, kinds, ag_send.at[k], ag_recv.at[k])

    def write_to(ref, at=0):
        def write(total):
            ref[:, at : at + total.shape[1]] = total

        return write

    def write_q(total):
        out_q[...] = total[:, :512]
        out_kv[...] = total[:, 512:]

    def write_small(total):
        turned = total.T
        out_router[...] = turned[0:8]
        out_g1[...] = turned[8:9]
        out_g2[...] = turned[9:10]
        out_bias[...] = pltpu.roll(total, 64, 1)[0:1, 0:64]

    def write_up(c):
        def write(total):
            for k in range(4):
                at = 512 * k + 128 * c
                out_up[:, at : at + 128] = total[:, 128 * k : 128 * k + 128]

        return write

    writes = [write_up(c) for c in range(4)] + [write_to(out_down)] * 4 + [write_to(out_o), write_q, write_small]
    spots = list(landing)
    for k, (name, kinds) in enumerate(REDUCES):
        first = parts[SHARED[name]].first if name in SHARED else spots.pop(0)
        last = spots.pop(0)
        if name in ("q", "r"):
            parts[name] = ReduceShort(
                g, ga, kinds, rs_send.at[k], rs_recv.at[k], (first, last, spots.pop(0)), writes[k]
            )
            continue
        halves_in, quarters_in = [], []
        for _ in range(2 if isinstance(kinds, int) else len(kinds)):
            halves_in.append(spots.pop(0))
            quarters_in.append(spots.pop(0))
        make, buf = (ReduceOne, gd) if name[0] == "d" else (Reduce, ga)
        parts[name] = make(
            g, buf, kinds, rs_send.at[k], rs_recv.at[k],
            (first, halves_in, quarters_in, last), writes[k],
        )

    def hook(name):
        for part, k in SCHEDULE.get(name, ()):
            parts[part].step(k)

    hook("go")
    small[...] = jnp.zeros_like(small)
    gaing[...] = jnp.zeros_like(gaing)
    biasg[...] = jnp.zeros_like(biasg)
    nrows = x.shape[0] // 512

    def each(phase, name):
        def body(r, _):
            phase(r)
            for k in range(nrows):
                if SCHEDULE.get(name + "." + str(k)):
                    pl.when(r == k)(lambda k=k: hook(name + "." + str(k)))
            return 0

        lax.fori_loop(0, nrows, body, 0)

    copies[12].wait()
    each(lambda r: phase_norm1(s, r), "norm")
    hook("P0")
    block[...] = s.weight(CR, CO).astype(F32)
    turned = block[...].T
    g1[...] = turned[8:9]
    g2[...] = turned[9:10]
    even = block[pl.ds(0, 16, stride=32), :]
    odd = block[pl.ds(16, 16, stride=32), :]
    both = jnp.where(lanes((16, 128)) < 64, pltpu.roll(even, 64, 1), odd)
    for k in range(16):
        at = 512 * (k % 4) + 128 * (k // 4)
        bias[:, at : at + 128] = both[k : k + 1]
    for copy in copies[13:]:
        copy.wait()
    for r in range(nrows):
        phase_forward(s, r, lambda i, r=r: hook("fwd" + str(r) + "." + str(i)))
    hook("P1")
    each(lambda r: phase_resid(s, r), "res")
    fetch_row(0).start()
    for c in range(4):
        hook("ffn" + str(c))
        each(lambda r, c=c: phase_ffn(s, c, r), "ffn" + str(c))
        phase_ffn_grads(s, c)
        hook("grads" + str(c))
    def norm2_back(r):
        phase_norm2_back(s, r)
        if r + 1 < nrows:
            fetch_row(r + 1).start()
        else:
            put(CO, tn(mixed[...], s.dbranch[...]))
            hook("og")

    def back_hook(r, i):
        if i == 0 and r > 0:
            for later in range(r + 1, nrows):
                if later > done[-1]:
                    done.append(later)
                    norm2_back(later)
        hook("back" + str(r) + "." + str(i))

    done = [0]
    norm2_back(0)
    for r in range(nrows):
        if r > done[-1]:
            done.append(r)
            norm2_back(r)
        phase_back(s, r, functools.partial(back_hook, r))
    put(CQ, tn(normed[...], q[...]))
    kvr = tn(normed[...], s.dkr[...])
    put(CKV, kvr[:, :128])
    block[...] = kvr[:, 128:]
    hook("qg")
    each(lambda r: phase_input(s, r), "inp")
    turned = gaing[...].T
    lane = lanes((512, 128))
    block[...] = jnp.where(
        lane == 8, turned[:, 0:1], jnp.where(lane == 9, turned[:, 1:2], block[...])
    )
    for k in range(16):
        at = 512 * (k % 4) + 128 * (k // 4)
        tiny[k : k + 1, :] = biasg[:, at : at + 128]
    pieces = tiny[0:16, :]
    low = lanes((16, 128)) < 64
    even = pl.ds(0, 16, stride=32)
    block[even, :] = jnp.where(low, block[even, :], pltpu.roll(pieces, 64, 1))
    odd = pl.ds(16, 16, stride=32)
    block[odd, :] = jnp.where(low, block[odd, :], pieces)
    put(CR, block[...])
    hook("end")
    for part in parts.values():
        part.finish()


def hand_on_kernel(*refs):
    n = len(refs) // 2
    copies = [pltpu.make_async_copy(refs[k], refs[n + k], refs[-1].at[k]) for k in range(n)]
    for copy in copies:
        copy.start()
    for copy in copies:
        copy.wait()


def shards_mega(inputs, cotangent, segment_ids, expert_ids, overflow, norm1_gain, router_weight,
                query_weight, key_value_weight, output_weight, norm2_gain, up_weight, up_bias, down_weight):
    nrows, length, width = inputs.shape
    tokens = nrows * length
    v = pl.BlockSpec(memory_space=pltpu.VMEM)
    h = pl.BlockSpec(memory_space=pl.ANY)
    sd = lambda *shape: jax.ShapeDtypeStruct(shape, F32)
    b = lambda *shape: pltpu.VMEM(shape, BF)
    f = lambda *shape: pltpu.VMEM(shape, F32)
    n = lambda *shape: pltpu.VMEM(shape, jnp.int32)
    landing = []
    for name, kinds in REDUCES:
        landing += landing_shapes(64 if name[0] == "d" else 16, kinds)[name in SHARED :]
    dma = pltpu.SemaphoreType.DMA
    out = pl.pallas_call(
        mega_kernel,
        out_shape=(
            f(tokens, width), f(tokens, width), f(1, 16), f(8, 16), f(16, 512), f(16, 128),
            f(16, 512), f(1, 16), f(16, 2048), f(1, 64), f(64, 512),
        ),
        in_specs=[h] * 14,
        out_specs=(v,) * 11,
        scratch_shapes=scratch(tokens)[2:6] + scratch(tokens)[7:] + [
            dma((20,)), f(512, 512), n(3, 512), n(3, 2, 512), n(3, 2, 512), f(16, 16), f(8, 16), f(1, 64), b(2, 2, 4, 2, 16, CW), b(2, 2, 4, 2, 64, 512), b(2, 2, 4, 2, 16, CW),
            b(2, 2, 4, 2, 64, 512), f(1, 512), f(1, 512), f(1, 2048), f(32, 128),
            dma((9, 8)), dma((9, 8)), dma((11, 8)), dma((11, 8)),
        ] + landing,
        compiler_params=pltpu.CompilerParams(
            collective_id=0, has_side_effects=True, vmem_limit_bytes=VLIM
        ),
    )(
        inputs.reshape(tokens, width), cotangent.reshape(tokens, width), segment_ids,
        jnp.swapaxes(expert_ids, 1, 2), jnp.swapaxes(overflow, 1, 2),
        norm1_gain[None], norm2_gain[None], up_bias[None], router_weight.T, query_weight, key_value_weight,
        output_weight, up_weight, down_weight,
    )
    y, dx, g1, router, query, pair, output, g2, up, bias, down = pl.pallas_call(
        hand_on_kernel,
        out_shape=tuple(sd(*o.shape) for o in out),
        in_specs=[h] * 11,
        out_specs=(h,) * 11,
        scratch_shapes=[dma((11,))],
        compiler_params=pltpu.CompilerParams(vmem_limit_bytes=32 * 1024),
    )(*out)
    return (
        y.reshape(inputs.shape), dx.reshape(inputs.shape), g1[0], router.T, query, pair, output, g2[0],
        up, bias[0], down,
    )


def shards_local(inputs, cotangent, segment_ids, expert_ids, overflow, norm1_gain, router_weight,
                 query_weight, key_value_weight, output_weight, norm2_gain, up_weight, up_bias, down_weight):
    nrows, length, width = inputs.shape
    tokens = nrows * length
    whole = lambda v: lax.all_gather(v.astype(BF), AXES, axis=0, tiled=True)
    g1, g2 = whole(norm1_gain), whole(norm2_gain)
    bias = whole(up_bias)
    router = whole(router_weight)
    parts = [whole(query_weight), whole(key_value_weight), jnp.pad(router, ((0, 0), (0, 120))),
             whole(output_weight), whole(up_weight)]
    wa = jnp.concatenate(parts, axis=1)
    wd = whole(down_weight)
    v = pl.BlockSpec(memory_space=pltpu.VMEM)
    h = pl.BlockSpec(memory_space=pl.ANY)
    sd = jax.ShapeDtypeStruct
    y, dx, ga, gd, small, biasg = pl.pallas_call(
        local_kernel,
        out_shape=(sd((tokens, width), F32), sd((tokens, width), F32), sd((512, CW), BF), sd((2048, 512), BF),
                   sd((8, 512), F32), sd((1, 2048), F32)),
        in_specs=[h, h] + [v] * 8,
        out_specs=(h, h, v, v, v, v),
        scratch_shapes=scratch(tokens) + [pltpu.SemaphoreType.DMA((4,))],
        compiler_params=pltpu.CompilerParams(vmem_limit_bytes=63 * 2**20),
    )(
        inputs.reshape(tokens, width), cotangent.reshape(tokens, width), segment_ids,
        jnp.swapaxes(expert_ids, 1, 2), jnp.swapaxes(overflow, 1, 2),
        g1.astype(F32)[None], g2.astype(F32)[None], bias.astype(F32)[None], wa, wd,
    )
    total = lambda v: lax.psum_scatter(v.astype(F32), AXES, scatter_dimension=0, tiled=True)
    return (
        y.reshape(inputs.shape), dx.reshape(inputs.shape),
        total(small[0]), total(ga[:, CR : CR + 8]), total(ga[:, CQ:CKV]), total(ga[:, CKV:CR]),
        total(ga[:, CO:CU]), total(small[1]), total(ga[:, CU:]), total(biasg[0]), total(gd),
    )


def solution(mesh):
    row3, row2, row1 = P(AXES, None, None), P(AXES, None), P(AXES)
    in_specs = (row3, row3, row2, row3, row3, row1, row2, row2, row2, row2, row1, row2, row1, row2)
    out_specs = (row3, row3, row1, row2, row2, row2, row2, row1, row2, row1, row2)
    small = mesh.shape['dp'] == 4 and mesh.shape['fsdp'] == 8
    shards = shards_mega if small else shards_local
    return jax.shard_map(shards, mesh=mesh, in_specs=in_specs, out_specs=out_specs, check_vma=False)
```

```python
import functools
import jax
import jax.numpy as jnp
from jax import lax
from jax.experimental import pallas as pl
from jax.experimental.pallas import tpu as pltpu
from jax.sharding import PartitionSpec as P

EPS = 1e-05
BIG = -1e30
GELU_C = 0.7978845608028654
GELU_K = 0.044715
BF = jnp.bfloat16
F32 = jnp.float32
AXES = ("dp", "fsdp")
VLIM = 60293120
CQ, CKV, CR, CO, CU, CW = 0, 512, 640, 768, 1280, 3328
TILES = ((0, 128, 0), (128, 256, 256), (128, 384, 768), (256, 256, 1536))


def nn(a, b):
    return lax.dot_general(a, b, (((1,), (0,)), ((), ())), preferred_element_type=F32)


def nt(a, b):
    return lax.dot_general(a, b, (((1,), (1,)), ((), ())), preferred_element_type=F32)


def tn(a, b):
    return lax.dot_general(a, b, (((0,), (0,)), ((), ())), preferred_element_type=F32)


def split(v):
    high = v.astype(BF)
    return high, (v - high.astype(F32)).astype(BF)


def lanes(shape):
    return lax.broadcasted_iota(jnp.int32, shape, len(shape) - 1)


def rows_of(shape):
    return lax.broadcasted_iota(jnp.int32, shape, len(shape) - 2)


def one_where(mask):
    return jnp.where(mask, 1.0, 0.0).astype(BF)


def norm(v):
    centred = v - jnp.mean(v, axis=-1, keepdims=True)
    inverse = lax.rsqrt(jnp.mean(centred * centred, axis=-1, keepdims=True) + EPS)
    return centred * inverse, inverse


def norm_back(grad, xhat, inverse, gain):
    scaled = grad * gain
    inner = (
        scaled
        - jnp.mean(scaled, axis=-1, keepdims=True)
        - xhat * jnp.mean(scaled * xhat, axis=-1, keepdims=True)
    )
    return inner * inverse


def gelu_both(x):
    square = x * x
    slope = (GELU_C * GELU_K) * square + GELU_C
    half = 0.5 * jnp.tanh(x * slope) + 0.5
    value = x * half
    return value, half + (value - value * half) * (6.0 * slope - 4.0 * GELU_C)


def stack_pairs(v):
    return jnp.concatenate([v[:, 128 * p : 128 * p + 128] for p in range(4)], axis=0)


class Plan:
    pass


def keys_of(s, win):
    kv, vk = s.kv[win, :], s.vk[win, :]
    low, zero = lanes(kv.shape) < 64, jnp.zeros_like(kv)
    return jnp.concatenate([jnp.where(low, kv, zero), jnp.where(low, zero, vk)], axis=0)


def values_of(s, win, extra_e, extra_o):
    kv, vk = s.kv[win, :], s.vk[win, :]
    low, zero = lanes(kv.shape) < 64, jnp.zeros_like(kv)
    even = jnp.concatenate([jnp.where(low, vk, zero), extra_e], axis=1)
    odd = jnp.concatenate([jnp.where(low, zero, kv), extra_o], axis=1)
    return jnp.concatenate([even, odd], axis=0)


def phase_norm1(s, r):
    rows = pl.ds(r * 512, 512)
    xhat, inverse = norm(s.x[rows, :])
    s.xh1[rows, :] = xhat
    s.gates[rows, :] = jnp.broadcast_to(inverse, (512, 128))


def phase_forward(s, r, hook=lambda i: None):
    rows = pl.ds(r * 512, 512)
    normed = (s.xh1[rows, :] * s.g1[...]).astype(BF)
    s.normed[rows, :] = normed
    proj = nn(normed, s.weight(CQ, CO))
    query = proj[:, :512].astype(BF)
    s.q[rows, :] = query
    pair = proj[:, CKV:CR].astype(BF).astype(F32)
    swapped = pltpu.roll(pair, 64, 1)
    low = lanes((512, 128)) < 64
    s.kv[rows, :] = jnp.where(low, pair * 0.125, pair).astype(BF)
    s.vk[rows, :] = jnp.where(low, swapped, swapped * 0.125).astype(BF)
    lane = lanes((512, 128))
    logits = jnp.where(lane < 8, proj[:, CR:CO], BIG)
    top = jnp.max(logits, axis=-1, keepdims=True)
    weights = jnp.exp(logits - top)
    prob = weights / jnp.sum(weights, axis=-1, keepdims=True)
    s.small[0:2, :] = jnp.where(s.over[r] == 0, s.ids[r], -1).astype(F32)
    s.small[2:3, :] = s.segs[pl.ds(r, 1), :].astype(F32)
    columns = s.small[...].T
    lane_f = lane.astype(F32)
    route = jnp.where(lane_f == columns[:, 0:1], 1.0, 0.0) + jnp.where(
        lane_f == columns[:, 1:2], 1.0, 0.0
    )
    mix = prob * route
    s.gates[rows, :] = jnp.where(lane == 8, s.gates[rows, :], mix + pltpu.roll(prob, 64, 1))
    seg_row = s.small[2:3, :]
    hook(0)
    for t, (start, width, at) in enumerate(TILES):
        q4 = stack_pairs(query[128 * t : 128 * t + 128])
        win = pl.ds(r * 512 + start, width)
        scores = nt(q4, keys_of(s, win))
        even, odd = scores[:, :width], scores[:, width:]
        if t:
            same = columns[128 * t : 128 * t + 128, 2:3] == seg_row[:, start : start + width]
            bias = jnp.where(same, 0.0, BIG)
            bias = jnp.concatenate([bias] * 4, axis=0)
            even, odd = even + bias, odd + bias
        even = jnp.exp(even - jnp.max(even, axis=-1, keepdims=True)).astype(BF)
        odd = jnp.exp(odd - jnp.max(odd, axis=-1, keepdims=True)).astype(BF)
        both = jnp.concatenate([even, odd], axis=1)
        s.pu[pl.ds(r * 512, 512), at : at + 2 * width] = both
        low_w = lanes((width, 128)) < 64
        one_e = jnp.where(low_w, 1.0, 0.0).astype(BF)
        one_o = jnp.where(low_w, 0.0, 1.0).astype(BF)
        out = nn(both, values_of(s, win, one_e, one_o))
        inverse = 1.0 / out[:, 128:]
        out = out[:, :128] * inverse
        for p in range(4):
            at_rows = pl.ds(r * 512 + 128 * t, 128)
            s.heads[at_rows, 128 * p : 128 * p + 128] = out[128 * p : 128 * p + 128]
            s.pinv[at_rows, 128 * p : 128 * p + 128] = inverse[128 * p : 128 * p + 128]
        hook(1 + t)
    mixed = (s.heads[rows, :] * expand(mix)).astype(BF)
    s.mixed[rows, :] = mixed
    hook(5)


def phase_resid(s, r):
    rows = pl.ds(r * 512, 512)
    resid = s.x[rows, :] + nn(s.mixed[rows, :], s.weight(CO, CU))
    s.x[rows, :] = resid
    xhat, inverse = norm(resid)
    s.xh2[rows, :] = xhat
    s.gates[rows, :] = jnp.where(lanes((512, 128)) == 9, inverse, s.gates[rows, :])
    s.normed2[rows, :] = (xhat * s.g2[...]).astype(BF)
    s.dffn[rows, :] = s.cotangent(rows).astype(BF)


def expand(per_expert):
    high, rest = split(per_expert)
    spread = one_where(
        jnp.bitwise_and(rows_of((256, 512)), 127) == jnp.right_shift(lanes((256, 512)), 6)
    )
    return nn(jnp.concatenate([high, rest], axis=1), spread)


def phase_ffn(s, c, r):
    rows = pl.ds(r * 512, 512)
    up = s.weight(CU + 512 * c, CU + 512 * c + 512)
    down = s.down(c)
    pre = nn(s.normed2[rows, :], up) + s.bias[:, 512 * c : 512 * c + 512]
    dhidden = nt(s.dffn[rows, :], down)
    value, slope = gelu_both(pre)
    dpre = dhidden * slope
    s.biasg[:, 512 * c : 512 * c + 512] += jnp.sum(dpre, axis=0, keepdims=True)
    hidden = value.astype(BF)
    dpre = dpre.astype(BF)
    s.hidden[rows, :] = hidden
    s.dpre[rows, :] = dpre
    s.x[rows, :] += nn(hidden, down)
    back = nt(dpre, up)
    if c == 0:
        s.dn2[rows, :] = back
    else:
        s.dn2[rows, :] += back


def phase_ffn_grads(s, c):
    s.put_down(c, tn(s.hidden[...], s.dffn[...]))
    s.put(CU + 512 * c, tn(s.normed2[...], s.dpre[...]))


def phase_norm2_back(s, r):
    rows = pl.ds(r * 512, 512)
    grad = s.dn2[rows, :]
    xhat = s.xh2[rows, :]
    s.gaing[1:2, :] += jnp.sum(grad * xhat, axis=0, keepdims=True)
    dresid = s.cotangent_row(r) + norm_back(grad, xhat, s.gates[rows, 9:10], s.g2[...])
    s.dn2[rows, :] = dresid
    dbranch = dresid.astype(BF)
    s.dbranch[rows, :] = dbranch


def phase_back(s, r, hook=lambda i: None):
    rows = pl.ds(r * 512, 512)
    dmixed = nt(s.dbranch[rows, :], s.weight(CO, CU))
    heads = s.heads[rows, :]
    gather = one_where(
        lanes((1024, 128)) == jnp.right_shift(jnp.bitwise_and(rows_of((1024, 128)), 511), 6)
    )
    dgate = nn(jnp.concatenate(split(dmixed * heads), axis=1), gather)
    gates = s.gates[rows, :]
    first8 = lanes((512, 128)) < 8
    mix = jnp.where(first8, gates, 0.0)
    prob = jnp.where(first8, pltpu.roll(gates, 64, 1), 0.0)
    weighted = dgate * mix
    dlogits = weighted - prob * jnp.sum(weighted, axis=-1, keepdims=True)
    s.dkr[rows, 128:256] = dlogits.astype(BF)
    dout = (dmixed * expand(mix) * s.pinv[rows, :]).astype(BF)
    s.dout[...] = dout
    within = dout.astype(F32) * heads
    high, rest = split(within)
    block = one_where(
        jnp.right_shift(jnp.bitwise_and(rows_of((256, 128)), 127), 6)
        == jnp.right_shift(lanes((256, 128)), 6)
    )
    place = jnp.bitwise_and(lanes((512, 128)), 63)
    for p in range(4):
        cols = slice(128 * p, 128 * p + 128)
        total = nn(jnp.concatenate([high[:, cols], rest[:, cols]], axis=1), block)
        first, second = split(total)
        s.delta[:, cols] = jnp.where(
            place == 0, first.astype(F32), jnp.where(place == 1, second.astype(F32), 0.0)
        ).astype(BF)
    s.dkv[...] = jnp.zeros_like(s.dkv)
    hook(0)
    for t, (start, width, at) in enumerate(TILES):
        here = pl.ds(128 * t, 128)
        at_rows = pl.ds(r * 512 + 128 * t, 128)
        win = pl.ds(r * 512 + start, width)
        do4 = stack_pairs(s.dout[here, :])
        de4 = stack_pairs(s.delta[here, :])
        lane = lanes((width, 128))
        neg_e = jnp.where(lane < 2, -1.0, 0.0).astype(BF)
        neg_o = jnp.where(jnp.bitwise_and(lane, 126) == 64, -1.0, 0.0).astype(BF)
        dprob = nt(jnp.concatenate([do4, de4], axis=1), values_of(s, win, neg_e, neg_o))
        weights = s.pu[pl.ds(r * 512, 512), at : at + 2 * width]
        dscore = (weights.astype(F32) * dprob).astype(BF)
        dq4 = nn(dscore, keys_of(s, win)).astype(BF)
        q4 = stack_pairs(s.q[at_rows, :])
        dk = tn(dscore, q4)
        dv = tn(weights, do4)
        for p in range(4):
            s.q[at_rows, 128 * p : 128 * p + 128] = dq4[128 * p : 128 * p + 128]
        s.dkv[pl.ds(start, width), :] += jnp.where(
            lane < 64,
            (dk[:width] + pltpu.roll(dk[width:], 64, 1)) * 0.125,
            dv[width:] + pltpu.roll(dv[:width], 64, 1),
        )
        if t < 3:
            hook(1 + t)
    s.dkr[rows, 0:128] = s.dkv[...].astype(BF)
    hook(4)


def phase_input(s, r):
    rows = pl.ds(r * 512, 512)
    dproj = jnp.concatenate([s.q[rows, :], s.dkr[rows, :]], axis=1)
    grad = nt(dproj, s.weight(CQ, CO))
    xhat = s.xh1[rows, :]
    s.gaing[0:1, :] += jnp.sum(grad * xhat, axis=0, keepdims=True)
    s.dn2[rows, :] += norm_back(grad, xhat, s.gates[rows, 8:9], s.g1[...])


def local_kernel(
    x_in, cot_in, segs, ids, over, g1, g2, bias, wa, wd,
    out_y, out_dx, out_ga, out_gd, out_small, out_bias,
    x, cot, xh1, xh2, heads, pinv, dn2, normed, q, mixed, normed2, dffn, hidden, dpre,
    kv, vk, gates, pu, block, small, gaing, biasg, sem,
):
    s = Plan()
    s.x, s.xh1, s.xh2, s.heads, s.pinv, s.dn2 = x, xh1, xh2, heads, pinv, dn2
    s.cotangent = lambda rows: cot[rows, :]
    s.cotangent_row = lambda r: cot[pl.ds(r * 512, 512), :]
    s.normed, s.q, s.mixed, s.normed2, s.dffn, s.hidden, s.dpre = normed, q, mixed, normed2, dffn, hidden, dpre
    s.kv, s.vk, s.gates, s.pu, s.dkv = kv, vk, gates, pu, block
    s.small, s.gaing, s.biasg, s.segs, s.ids, s.over = small, gaing, biasg, segs, ids, over
    s.g1, s.g2, s.bias = g1, g2, bias
    s.dbranch = s.dffn
    s.dkr = hidden.at[:, 0:256]
    s.dout, s.delta = dpre.at[0:512, :], dpre.at[512:1024, :]
    s.weight = lambda a, b: wa[:, a:b]
    s.down = lambda c: wd[512 * c : 512 * c + 512, :]

    def put(at, value):
        out_ga[:, at : at + value.shape[1]] = value.astype(BF)

    def put_down(c, value):
        out_gd[512 * c : 512 * c + 512, :] = value.astype(BF)

    s.put, s.put_down = put, put_down
    copies = [pltpu.make_async_copy(x_in, x, sem.at[0]), pltpu.make_async_copy(cot_in, cot, sem.at[1])]
    for copy in copies:
        copy.start()
    small[...] = jnp.zeros_like(small)
    gaing[...] = jnp.zeros_like(gaing)
    biasg[...] = jnp.zeros_like(biasg)
    for copy in copies:
        copy.wait()
    nrows = x.shape[0] // 512

    def each(phase):
        lax.fori_loop(0, nrows, lambda r, _: (phase(r), 0)[1], 0)

    each(lambda r: phase_norm1(s, r))
    each(lambda r: phase_forward(s, r))
    each(lambda r: phase_resid(s, r))
    for c in range(4):
        each(lambda r: phase_ffn(s, c, r))
        phase_ffn_grads(s, c)
    finish = pltpu.make_async_copy(x, out_y, sem.at[2])
    finish.start()
    each(lambda r: phase_norm2_back(s, r))
    each(lambda r: phase_back(s, r))
    put(CO, tn(mixed[...], s.dbranch[...]))
    put(CQ, tn(normed[...], q[...]))
    put(CKV, tn(normed[...], s.dkr[...]))
    each(lambda r: phase_input(s, r))
    last = pltpu.make_async_copy(dn2, out_dx, sem.at[3])
    last.start()
    out_small[...] = gaing[...]
    out_bias[...] = biasg[...]
    finish.wait()
    last.wait()


def scratch(tokens):
    f = lambda *shape: pltpu.VMEM(shape, F32)
    b = lambda *shape: pltpu.VMEM(shape, BF)
    t = tokens
    return (
        [f(t, 512)] * 7 + [b(t, 512)] * 7 + [b(t, 128)] * 2
        + [f(t, 128), b(t, 2048), f(512, 128)]
        + [f(8, 512), f(8, 512), f(1, 2048)]
    )


MESH = pl.DeviceIdType.MESH


class Ring:
    def __init__(self):
        self.d = lax.axis_index("dp")
        self.f = lax.axis_index("fsdp")
        self.x, self.c = jnp.right_shift(self.d, 1), jnp.bitwise_and(self.d, 1)
        self.z, self.y = jnp.right_shift(self.f, 1), jnp.bitwise_and(self.f, 1)
        self.ox, self.oc, self.oy = 1 - self.x, 1 - self.c, 1 - self.y
        self.core_peer = (2 * self.x + self.oc, self.f)
        self.x_peer = (2 * self.ox + self.c, self.f)
        self.y_peer = (self.d, 2 * self.z + self.oy)
        self.far_peer = (2 * self.ox + self.c, 2 * self.z + self.oy)
        self.later = [jnp.bitwise_and(self.z + k, 3) for k in (1, 2, 3)]
        self.earlier = [jnp.bitwise_and(self.z - k + 4, 3) for k in (1, 2, 3)]
        self.z_peers = [(self.d, 2 * z + self.y) for z in self.later]


def remote(src, dst, send, recv, peer):
    return pltpu.make_async_remote_copy(
        src_ref=src, dst_ref=dst, send_sem=send, recv_sem=recv, device_id=peer, device_id_type=MESH
    )


class Gather:
    def __init__(self, ring, buf, kinds, send, recv):
        self.ring, self.buf, self.kinds, self.send, self.recv = ring, buf, kinds, send, recv
        self.all = slice(kinds[0][0], kinds[-1][1])

    def copies(self, k, arriving):
        g, b = self.ring, self.buf
        if k == 0:
            at = lambda z: b.at[g.x, g.c, z, g.y, :, self.all]
            moves = [(n, at(g.earlier[n] if arriving else g.z), g.z_peers[n]) for n in range(3)]
        elif k == 3:
            moves = [(7, b.at[:, g.oc if arriving else g.c, :, :, :, self.all], g.core_peer)]
        else:
            moves = []
            x, y = (g.ox, g.oy) if arriving else (g.x, g.y)
            for kind, (lo, hi) in enumerate(self.kinds):
                cols = slice(lo, hi)
                if k == 1:
                    if kind == 0:
                        moves.append((3, b.at[x, g.c, :, g.y, :, cols], g.x_peer))
                    else:
                        moves.append((4, b.at[g.x, g.c, :, y, :, cols], g.y_peer))
                elif kind == 0:
                    moves.append((5, b.at[:, g.c, :, y, :, cols], g.y_peer))
                else:
                    moves.append((6, b.at[x, g.c, :, :, :, cols], g.x_peer))
        return [remote(ref, ref, self.send.at[n], self.recv.at[n], peer) for n, ref, peer in moves]

    def step(self, k):
        if k > 0:
            for copy in self.copies(k - 1, True):
                copy.wait_recv()
        if k < 4:
            for copy in self.copies(k, False):
                copy.start()

    def finish(self):
        for k in range(4):
            for copy in self.copies(k, False):
                copy.wait_send()


class Reduce:
    def __init__(self, ring, buf, kinds, send, recv, landing, write):
        self.ring, self.buf, self.kinds, self.send, self.recv = ring, buf, kinds, send, recv
        self.first, self.halves, self.quarters, self.last = landing
        self.all = slice(kinds[0][0], kinds[-1][1])
        self.write = write

    def copies(self, k):
        g, b = self.ring, self.buf
        if k == 0:
            moves = [(0, b.at[:, g.oc, :, :, :, self.all], self.first, g.core_peer)]
        elif k == 3:
            moves = [
                (5 + n, b.at[g.x, g.c, g.later[n], g.y, :, self.all], self.last.at[n], g.z_peers[n])
                for n in range(3)
            ]
        else:
            moves = []
            for kind, (lo, hi) in enumerate(self.kinds):
                cols = slice(lo, hi)
                if k == 1:
                    if kind == 0:
                        moves.append((1, b.at[:, g.c, :, g.oy, :, cols], self.halves[0], g.y_peer))
                    else:
                        moves.append((2, b.at[g.ox, g.c, :, :, :, cols], self.halves[1], g.x_peer))
                elif kind == 0:
                    moves.append((3, b.at[g.ox, g.c, :, g.y, :, cols], self.quarters[0], g.x_peer))
                else:
                    moves.append((4, b.at[g.x, g.c, :, g.oy, :, cols], self.quarters[1], g.y_peer))
        return [remote(src, dst, self.send.at[n], self.recv.at[n], peer) for n, src, dst, peer in moves]

    def add(self, k):
        g, b = self.ring, self.buf
        if k == 0:
            b[:, g.c, :, :, :, self.all] += self.first[...]
        elif k == 3:
            total = b[g.x, g.c, g.z, g.y, :, self.all].astype(F32)
            for n in range(3):
                total = total + self.last[n].astype(F32)
            self.write(total)
        else:
            for kind, (lo, hi) in enumerate(self.kinds):
                if k == 2:
                    b[g.x, g.c, :, g.y, :, lo:hi] += self.quarters[kind][...]
                elif kind == 0:
                    b[:, g.c, :, g.y, :, lo:hi] += self.halves[0][...]
                else:
                    b[g.x, g.c, :, :, :, lo:hi] += self.halves[1][...]

    def step(self, k):
        if k > 0:
            for copy in self.copies(k - 1):
                copy.wait_recv()
            self.add(k - 1)
        if k < 4:
            for copy in self.copies(k):
                copy.start()

    def finish(self):
        for k in range(4):
            for copy in self.copies(k):
                copy.wait_send()


class GatherShort(Gather):
    def copies(self, k, arriving):
        g, b = self.ring, self.buf
        if k == 0:
            return Gather.copies(self, 0, arriving)
        if k == 2:
            return Gather.copies(self, 3, arriving)
        moves = []
        for n, x, y, peer in ((3, g.ox, g.y, g.x_peer), (4, g.x, g.oy, g.y_peer), (5, g.ox, g.oy, g.far_peer)):
            at = (x, y) if arriving else (g.x, g.y)
            moves.append((n, b.at[at[0], g.c, :, at[1], :, self.all], peer))
        return [remote(ref, ref, self.send.at[n], self.recv.at[n], peer) for n, ref, peer in moves]

    def step(self, k):
        if k > 0:
            for copy in self.copies(k - 1, True):
                copy.wait_recv()
        if k < 3:
            for copy in self.copies(k, False):
                copy.start()

    def finish(self):
        for k in range(3):
            for copy in self.copies(k, False):
                copy.wait_send()


class GatherOne:
    def __init__(self, ring, buf, z, send, recv):
        self.ring, self.buf, self.z, self.send, self.recv = ring, buf, z, send, recv

    def spread(self):
        g, b = self.ring, self.buf.at[self.ring.x, self.ring.c, self.z, self.ring.y]
        return [remote(b, b, self.send.at[n], self.recv.at[0], g.z_peers[n]) for n in range(3)]

    def copies(self, k, arriving):
        g, b, z = self.ring, self.buf, self.z
        x, y, c = (g.ox, g.oy, g.oc) if arriving else (g.x, g.y, g.c)
        low, high = slice(0, 256), slice(256, 512)
        if k == 1:
            moves = [
                (3, b.at[x, g.c, z, g.y, :, low], g.x_peer), (4, b.at[g.x, g.c, z, y, :, high], g.y_peer),
            ]
        elif k == 2:
            moves = [
                (5, b.at[:, g.c, z, y, :, low], g.y_peer), (6, b.at[x, g.c, z, :, :, high], g.x_peer),
            ]
        else:
            moves = [(7, b.at[:, c, z], g.core_peer)]
        return [remote(ref, ref, self.send.at[n], self.recv.at[n], peer) for n, ref, peer in moves]

    def step(self, k):
        if k == 0:
            @pl.when(self.ring.z == self.z)
            def _():
                for copy in self.spread():
                    copy.start()
        if k == 1:
            @pl.when(self.ring.z != self.z)
            def _():
                self.spread()[0].wait_recv()
        if k > 1:
            for copy in self.copies(k - 1, True):
                copy.wait_recv()
        if 0 < k < 4:
            for copy in self.copies(k, False):
                copy.start()

    def finish(self):
        @pl.when(self.ring.z == self.z)
        def _():
            for copy in self.spread():
                copy.wait_send()

        for k in (1, 2, 3):
            for copy in self.copies(k, False):
                copy.wait_send()


class ReduceOne:
    def __init__(self, ring, buf, z, send, recv, landing, write):
        self.ring, self.buf, self.z, self.send, self.recv = ring, buf, z, send, recv
        self.first, self.halves, self.quarters, self.last = landing
        self.write = write

    def copies(self, k):
        g, b, z = self.ring, self.buf, self.z
        low, high = slice(0, 256), slice(256, 512)
        if k == 0:
            moves = [(0, b.at[:, g.oc, z], self.first, g.core_peer)]
        elif k == 1:
            moves = [
                (1, b.at[:, g.c, z, g.oy, :, low], self.halves[0], g.y_peer),
                (2, b.at[g.ox, g.c, z, :, :, high], self.halves[1], g.x_peer),
            ]
        else:
            moves = [
                (3, b.at[g.ox, g.c, z, g.y, :, low], self.quarters[0], g.x_peer),
                (4, b.at[g.x, g.c, z, g.oy, :, high], self.quarters[1], g.y_peer),
            ]
        return [remote(src, dst, self.send.at[n], self.recv.at[n], peer) for n, src, dst, peer in moves]

    def collect(self, sender):
        g = self.ring
        slot = jnp.bitwise_and(sender - self.z + 3, 3)
        return remote(
            self.buf.at[g.x, g.c, self.z, g.y], self.last.at[slot], self.send.at[5], self.recv.at[5 + slot],
            (g.d, 2 * self.z + g.y),
        )

    def step(self, k):
        g, b, z = self.ring, self.buf, self.z
        low, high = slice(0, 256), slice(256, 512)
        if 0 < k < 4:
            for copy in self.copies(k - 1):
                copy.wait_recv()
        if k == 1:
            b[:, g.c, z] += self.first[...]
        if k == 2:
            b[:, g.c, z, g.y, :, low] += self.halves[0][...]
            b[g.x, g.c, z, :, :, high] += self.halves[1][...]
        if k == 3:
            b[g.x, g.c, z, g.y, :, low] += self.quarters[0][...]
            b[g.x, g.c, z, g.y, :, high] += self.quarters[1][...]

            @pl.when(g.z != z)
            def _():
                self.collect(g.z).start()
        if k < 3:
            for copy in self.copies(k):
                copy.start()
        if k == 4:
            @pl.when(g.z == z)
            def _():
                total = b[g.x, g.c, z, g.y].astype(F32)
                for n in range(3):
                    self.collect((z + 1 + n) % 4).wait_recv()
                    total = total + self.last[n].astype(F32)
                self.write(total)

    def finish(self):
        for k in range(3):
            for copy in self.copies(k):
                copy.wait_send()

        @pl.when(self.ring.z != self.z)
        def _():
            self.collect(self.ring.z).wait_send()


class ReduceShort:
    def __init__(self, ring, buf, cols, send, recv, landing, write):
        self.ring, self.buf, self.all, self.send, self.recv = ring, buf, slice(*cols), send, recv
        self.first, self.last, self.plane = landing
        self.write = write

    def copies(self, k):
        g, b = self.ring, self.buf
        if k == 0:
            moves = [(0, b.at[:, g.oc, :, :, :, self.all], self.first, g.core_peer)]
        elif k == 1:
            moves = [
                (1, b.at[g.ox, g.c, :, g.y, :, self.all], self.plane.at[0], g.x_peer),
                (2, b.at[g.x, g.c, :, g.oy, :, self.all], self.plane.at[1], g.y_peer),
                (3, b.at[g.ox, g.c, :, g.oy, :, self.all], self.plane.at[2], g.far_peer),
            ]
        else:
            moves = [
                (5 + n, b.at[g.x, g.c, g.later[n], g.y, :, self.all], self.last.at[n], g.z_peers[n])
                for n in range(3)
            ]
        return [remote(src, dst, self.send.at[n], self.recv.at[n], peer) for n, src, dst, peer in moves]

    def step(self, k):
        g, b = self.ring, self.buf
        if k > 0:
            for copy in self.copies(k - 1):
                copy.wait_recv()
        if k == 1:
            b[:, g.c, :, :, :, self.all] += self.first[...]
        if k > 1:
            mine = (g.x, g.c, slice(None), g.y) if k == 2 else (g.x, g.c, g.z, g.y)
            total = b[(*mine, slice(None), self.all)].astype(F32)
            for n in range(3):
                total = total + (self.plane if k == 2 else self.last)[n].astype(F32)
            if k == 2:
                b[(*mine, slice(None), self.all)] = total.astype(BF)
            else:
                self.write(total)
        if k < 3:
            for copy in self.copies(k):
                copy.start()

    def finish(self):
        for k in range(3):
            for copy in self.copies(k):
                copy.wait_send()


def landing_shapes(rows, kinds):
    b = lambda *shape: pltpu.VMEM(shape, BF)
    if isinstance(kinds, int):
        return [
            b(2, 2, rows, 512), b(3, rows, 512), b(2, rows, 256), b(rows, 256), b(2, rows, 256), b(rows, 256),
        ]
    if isinstance(kinds[0], int):
        n = kinds[1] - kinds[0]
        return [b(2, 4, 2, rows, n), b(3, rows, n), b(3, 4, rows, n)]
    n = kinds[-1][1] - kinds[0][0]
    shapes = [b(2, 4, 2, rows, n), b(3, rows, n)]
    for kind, (lo, hi) in enumerate(kinds):
        shapes.append(b(2, 4, rows, hi - lo) if kind == 0 else b(4, 2, rows, hi - lo))
        shapes.append(b(4, rows, hi - lo))
    return shapes


def halves(lo, hi, cut=None):
    cut = (lo + hi) // 2 if cut is None else cut
    return ((lo, cut), (cut, hi))


GATHERS = (
    ("P0", halves(CQ, CO)), ("P1", halves(CO, CU)), ("U0", halves(CU, CU + 512)), ("D0", 0),
    ("U1", halves(CU + 512, CU + 1024)), ("D1", 1), ("U2", halves(CU + 1024, CW)), ("D2", 2), ("D3", 3),
)
REDUCES = (
    ("u0", halves(CU, CU + 512)), ("u1", halves(CU + 512, CU + 1024)),
    ("u2", halves(CU + 1024, CU + 1536)), ("u3", halves(CU + 1536, CW)),
    ("d0", 0), ("d1", 1), ("d2", 2), ("d3", 3), ("o", halves(CO, CU)),
    ("q", (CQ, CR)), ("r", (CR, CO)),
)
SHARED = {"d2": "d0", "d3": "d1"}
SCHEDULE = {
    "go": (("P0", 0),),
    "P0": (("P0", 1), ("P1", 0), ("U0", 0), ("D0", 0), ("P0", 2), ("U1", 0), ("D1", 0), ("P1", 1), ("U0", 1), ("P0", 3),),
    "fwd0.3": (("D0", 1), ("U2", 0), ("D2", 0), ("D3", 0),),
    "fwd0.4": (("P1", 2),),
    "fwd1.0": (("U0", 2), ("U1", 1),),
    "fwd1.4": (("D1", 1),),
    "fwd2.1": (("D0", 2),),
    "fwd2.4": (("P1", 3),),
    "P1": (("U2", 1), ("U0", 3), ("U1", 2), ("D1", 2), ("D2", 1), ("P1", 4),),
    "ffn0": (("D0", 3), ("U0", 4), ("U2", 2), ("D3", 1), ("D0", 4),),
    "ffn0.1": (("U1", 3),),
    "ffn0.2": (("D1", 3), ("D2", 2),),
    "grads0": (("d0", 0), ("u0", 0),),
    "ffn1": (("U1", 4), ("U2", 3), ("D3", 2), ("D1", 4),),
    "ffn1.1": (("d0", 1),),
    "ffn1.2": (("D2", 3),),
    "grads1": (("d1", 0), ("u1", 0), ("u0", 1), ("U2", 4), ("D3", 3),),
    "ffn2": (("D2", 4),),
    "ffn2.1": (("d0", 2), ("d1", 1), ("u1", 1),),
    "grads2": (("d2", 0), ("u2", 0), ("D3", 4), ("u0", 2), ("d0", 3),),
    "ffn3.1": (("d1", 2), ("d2", 1), ("u1", 2), ("u2", 1), ("u0", 3),),
    "grads3": (("d3", 0), ("u3", 0), ("d1", 3), ("d0", 4),),
    "back0.0": (("d2", 2), ("u0", 4), ("u1", 3), ("d3", 1),),
    "back0.4": (("u3", 1), ("u2", 2),),
    "og": (("o", 0), ("d2", 3), ("d1", 4), ("d3", 2), ("u1", 4),),
    "back1.4": (("u3", 2), ("u2", 3), ("o", 1),),
    "back2.0": (("d3", 3),),
    "back2.4": (("d2", 4), ("u3", 3),),
    "qg": (("q", 0), ("u2", 4), ("o", 2),),
    "inp.1": (("q", 1),),
    "end": (("r", 0), ("d3", 4), ("o", 3), ("u3", 4), ("r", 1), ("q", 2), ("o", 4), ("r", 2), ("q", 3), ("r", 3),),
}


def mega_kernel(
    x_in, cot_in, segs_in, ids_in, over_in, g1_in, g2_in, bias_in, router_in, q_in, kv_in, o_in, up_in, down_in,
    x, dn2, out_g1, out_router, out_q, out_kv, out_o, out_g2, out_up, out_bias, out_down,
    xh1, xh2, heads, pinv, normed, q, mixed, normed2, dffn, hidden, dpre,
    kv, vk, gates, pu, block, small, gaing, biasg,
    sem, cot_row, segs, ids, over, small_in, router_at, bias_at, wa, wd, ga, gd, g1, g2, bias, tiny, ag_send, ag_recv, rs_send, rs_recv, *landing,
):
    s = Plan()
    s.x, s.xh1, s.xh2, s.heads, s.pinv, s.dn2 = x, xh1, xh2, heads, pinv, dn2
    s.cotangent = lambda rows: dn2[rows, :]

    def fetch_row(r):
        return pltpu.make_async_copy(cot_in.at[512 * r : 512 * r + 512], cot_row, sem.at[17 + r])

    def cotangent_row(r):
        fetch_row(r).wait()
        return cot_row[...]

    s.cotangent_row = cotangent_row
    s.normed, s.q, s.mixed, s.normed2, s.dffn, s.hidden, s.dpre = normed, q, mixed, normed2, dffn, hidden, dpre
    s.kv, s.vk, s.gates, s.pu, s.dkv = kv, vk, gates, pu, block
    s.small, s.gaing, s.biasg, s.segs, s.ids, s.over = small, gaing, biasg, segs, ids, over
    s.g1, s.g2, s.bias = g1, g2, bias
    s.dbranch = s.dffn
    s.dkr = hidden.at[:, 0:256]
    s.dout, s.delta = dpre.at[0:512, :], dpre.at[512:1024, :]
    s.weight = lambda a, b: wa[:, :, :, :, :, a:b].reshape(512, b - a)
    s.down = lambda c: wd[:, :, c].reshape(512, 512)

    def put(at, value):
        n = value.shape[1]
        ga[:, :, :, :, :, at : at + n] = value.astype(BF).reshape(2, 2, 4, 2, 16, n)

    def put_down(c, value):
        gd[:, :, c] = value.astype(BF).reshape(2, 2, 2, 64, 512)

    s.put, s.put_down = put, put_down
    g = Ring()
    peers = [g.core_peer, g.x_peer, g.y_peer, g.far_peer] + g.z_peers
    barrier = pltpu.get_barrier_semaphore()
    for peer in peers:
        pl.semaphore_signal(barrier, inc=1, device_id=peer, device_id_type=MESH)
    moves = [
        (q_in, dn2.at[0:16]), (o_in, dn2.at[16:32]), (kv_in, dn2.at[32:48, 0:128]), (down_in, dn2.at[128:192]),
        (router_in, router_at), (g1_in, small_in.at[0:1]), (g2_in, small_in.at[8:9]), (bias_in, bias_at),
    ]
    moves += [
        (up_in.at[:, 512 * k : 512 * k + 512], dn2.at[48 + 16 * k : 64 + 16 * k]) for k in range(4)
    ]
    moves += [(x_in, x), (segs_in, segs), (ids_in, ids), (over_in, over), (cot_in, dn2)]
    copies = [pltpu.make_async_copy(src, dst, sem.at[n]) for n, (src, dst) in enumerate(moves)]
    for copy in copies[:16]:
        copy.start()
    for copy in copies[:12]:
        copy.wait()

    wa[g.x, g.c, g.z, g.y, :, CQ:CKV] = dn2[0:16, :].astype(BF)
    wa[g.x, g.c, g.z, g.y, :, CKV:CR] = dn2[32:48, 0:128].astype(BF)
    wa[g.x, g.c, g.z, g.y, :, CO:CU] = dn2[16:32, :].astype(BF)
    for k in range(16):
        at = CU + 512 * (k % 4) + 128 * (k // 4)
        wa[g.x, g.c, g.z, g.y, :, at : at + 128] = dn2[
            48 + 16 * (k // 4) : 64 + 16 * (k // 4), 128 * (k % 4) : 128 * (k % 4) + 128
        ].astype(BF)
    wd[g.x, g.c, g.z, g.y] = dn2[128:192, :].astype(BF)
    tiny[...] = jnp.zeros_like(tiny)
    tiny[0:8, 0:16] = router_at[...]
    tiny[8:9, 0:16] = small_in[0:1]
    tiny[9:10, 0:16] = small_in[8:9]
    tiny[16:17, 0:64] = bias_at[...]
    turned = tn(
        tiny[0:16, :].astype(BF), one_where(rows_of((16, 128)) == lanes((16, 128)))
    )[0:16]
    shifted = nn(tiny[16:32, :].astype(BF), one_where(rows_of((128, 128)) + 64 == lanes((128, 128))))
    wa[g.x, g.c, g.z, g.y, :, CR:CO] = (turned + shifted).astype(BF)

    copies[16].start()
    pl.semaphore_wait(barrier, len(peers))
    parts = {}
    for k, (name, kinds) in enumerate(GATHERS):
        make, buf = (GatherOne, wd) if name[0] == "D" else (GatherShort if name == "P0" else Gather, wa)
        parts[name] = make(g, buf, kinds, ag_send.at[k], ag_recv.at[k])

    def write_to(ref, at=0):
        def write(total):
            ref[:, at : at + total.shape[1]] = total

        return write

    def write_q(total):
        out_q[...] = total[:, :512]
        out_kv[...] = total[:, 512:]

    def write_small(total):
        turned = total.T
        out_router[...] = turned[0:8]
        out_g1[...] = turned[8:9]
        out_g2[...] = turned[9:10]
        out_bias[...] = pltpu.roll(total, 64, 1)[0:1, 0:64]

    def write_up(c):
        def write(total):
            for k in range(4):
                at = 512 * k + 128 * c
                out_up[:, at : at + 128] = total[:, 128 * k : 128 * k + 128]

        return write

    writes = [write_up(c) for c in range(4)] + [write_to(out_down)] * 4 + [write_to(out_o), write_q, write_small]
    spots = list(landing)
    for k, (name, kinds) in enumerate(REDUCES):
        first = parts[SHARED[name]].first if name in SHARED else spots.pop(0)
        last = spots.pop(0)
        if name in ("q", "r"):
            parts[name] = ReduceShort(
                g, ga, kinds, rs_send.at[k], rs_recv.at[k], (first, last, spots.pop(0)), writes[k]
            )
            continue
        halves_in, quarters_in = [], []
        for _ in range(2 if isinstance(kinds, int) else len(kinds)):
            halves_in.append(spots.pop(0))
            quarters_in.append(spots.pop(0))
        make, buf = (ReduceOne, gd) if name[0] == "d" else (Reduce, ga)
        parts[name] = make(
            g, buf, kinds, rs_send.at[k], rs_recv.at[k],
            (first, halves_in, quarters_in, last), writes[k],
        )

    def hook(name):
        for part, k in SCHEDULE.get(name, ()):
            parts[part].step(k)

    hook("go")
    small[...] = jnp.zeros_like(small)
    gaing[...] = jnp.zeros_like(gaing)
    biasg[...] = jnp.zeros_like(biasg)
    nrows = x.shape[0] // 512

    def each(phase, name):
        def body(r, _):
            phase(r)
            for k in range(nrows):
                if SCHEDULE.get(name + "." + str(k)):
                    pl.when(r == k)(lambda k=k: hook(name + "." + str(k)))
            return 0

        lax.fori_loop(0, nrows, body, 0)

    copies[12].wait()
    each(lambda r: phase_norm1(s, r), "norm")
    hook("P0")
    block[...] = s.weight(CR, CO).astype(F32)
    turned = block[...].T
    g1[...] = turned[8:9]
    g2[...] = turned[9:10]
    even = block[pl.ds(0, 16, stride=32), :]
    odd = block[pl.ds(16, 16, stride=32), :]
    both = jnp.where(lanes((16, 128)) < 64, pltpu.roll(even, 64, 1), odd)
    for k in range(16):
        at = 512 * (k % 4) + 128 * (k // 4)
        bias[:, at : at + 128] = both[k : k + 1]
    for copy in copies[13:]:
        copy.wait()
    for r in range(nrows):
        phase_forward(s, r, lambda i, r=r: hook("fwd" + str(r) + "." + str(i)))
    hook("P1")
    each(lambda r: phase_resid(s, r), "res")
    fetch_row(0).start()
    for c in range(4):
        hook("ffn" + str(c))
        each(lambda r, c=c: phase_ffn(s, c, r), "ffn" + str(c))
        phase_ffn_grads(s, c)
        hook("grads" + str(c))
    def norm2_back(r):
        phase_norm2_back(s, r)
        if r + 1 < nrows:
            fetch_row(r + 1).start()
        else:
            put(CO, tn(mixed[...], s.dbranch[...]))
            hook("og")

    def back_hook(r, i):
        if i == 0 and r > 0:
            for later in range(r + 1, nrows):
                if later > done[-1]:
                    done.append(later)
                    norm2_back(later)
        hook("back" + str(r) + "." + str(i))

    done = [0]
    norm2_back(0)
    for r in range(nrows):
        if r > done[-1]:
            done.append(r)
            norm2_back(r)
        phase_back(s, r, functools.partial(back_hook, r))
    put(CQ, tn(normed[...], q[...]))
    kvr = tn(normed[...], s.dkr[...])
    put(CKV, kvr[:, :128])
    block[...] = kvr[:, 128:]
    hook("qg")
    each(lambda r: phase_input(s, r), "inp")
    turned = gaing[...].T
    lane = lanes((512, 128))
    block[...] = jnp.where(
        lane == 8, turned[:, 0:1], jnp.where(lane == 9, turned[:, 1:2], block[...])
    )
    for k in range(16):
        at = 512 * (k % 4) + 128 * (k // 4)
        tiny[k : k + 1, :] = biasg[:, at : at + 128]
    pieces = tiny[0:16, :]
    low = lanes((16, 128)) < 64
    even = pl.ds(0, 16, stride=32)
    block[even, :] = jnp.where(low, block[even, :], pltpu.roll(pieces, 64, 1))
    odd = pl.ds(16, 16, stride=32)
    block[odd, :] = jnp.where(low, block[odd, :], pieces)
    put(CR, block[...])
    hook("end")
    for part in parts.values():
        part.finish()


def hand_on_kernel(*refs):
    n = len(refs) // 2
    copies = [pltpu.make_async_copy(refs[k], refs[n + k], refs[-1].at[k]) for k in range(n)]
    for copy in copies:
        copy.start()
    for copy in copies:
        copy.wait()


def shards_mega(inputs, cotangent, segment_ids, expert_ids, overflow, norm1_gain, router_weight,
                query_weight, key_value_weight, output_weight, norm2_gain, up_weight, up_bias, down_weight):
    nrows, length, width = inputs.shape
    tokens = nrows * length
    v = pl.BlockSpec(memory_space=pltpu.VMEM)
    h = pl.BlockSpec(memory_space=pl.ANY)
    sd = lambda *shape: jax.ShapeDtypeStruct(shape, F32)
    b = lambda *shape: pltpu.VMEM(shape, BF)
    f = lambda *shape: pltpu.VMEM(shape, F32)
    n = lambda *shape: pltpu.VMEM(shape, jnp.int32)
    landing = []
    for name, kinds in REDUCES:
        landing += landing_shapes(64 if name[0] == "d" else 16, kinds)[name in SHARED :]
    dma = pltpu.SemaphoreType.DMA
    out = pl.pallas_call(
        mega_kernel,
        out_shape=(
            f(tokens, width), f(tokens, width), f(1, 16), f(8, 16), f(16, 512), f(16, 128),
            f(16, 512), f(1, 16), f(16, 2048), f(1, 64), f(64, 512),
        ),
        in_specs=[h] * 14,
        out_specs=(v,) * 11,
        scratch_shapes=scratch(tokens)[2:6] + scratch(tokens)[7:] + [
            dma((20,)), f(512, 512), n(3, 512), n(3, 2, 512), n(3, 2, 512), f(16, 16), f(8, 16), f(1, 64), b(2, 2, 4, 2, 16, CW), b(2, 2, 4, 2, 64, 512), b(2, 2, 4, 2, 16, CW),
            b(2, 2, 4, 2, 64, 512), f(1, 512), f(1, 512), f(1, 2048), f(32, 128),
            dma((9, 8)), dma((9, 8)), dma((11, 8)), dma((11, 8)),
        ] + landing,
        compiler_params=pltpu.CompilerParams(
            collective_id=0, has_side_effects=True, vmem_limit_bytes=VLIM
        ),
    )(
        inputs.reshape(tokens, width), cotangent.reshape(tokens, width), segment_ids,
        jnp.swapaxes(expert_ids, 1, 2), jnp.swapaxes(overflow, 1, 2),
        norm1_gain[None], norm2_gain[None], up_bias[None], router_weight.T, query_weight, key_value_weight,
        output_weight, up_weight, down_weight,
    )
    y, dx, g1, router, query, pair, output, g2, up, bias, down = pl.pallas_call(
        hand_on_kernel,
        out_shape=tuple(sd(*o.shape) for o in out),
        in_specs=[h] * 11,
        out_specs=(h,) * 11,
        scratch_shapes=[dma((11,))],
        compiler_params=pltpu.CompilerParams(vmem_limit_bytes=32 * 1024),
    )(*out)
    return (
        y.reshape(inputs.shape), dx.reshape(inputs.shape), g1[0], router.T, query, pair, output, g2[0],
        up, bias[0], down,
    )


def shards_local(inputs, cotangent, segment_ids, expert_ids, overflow, norm1_gain, router_weight,
                 query_weight, key_value_weight, output_weight, norm2_gain, up_weight, up_bias, down_weight):
    nrows, length, width = inputs.shape
    tokens = nrows * length
    whole = lambda v: lax.all_gather(v.astype(BF), AXES, axis=0, tiled=True)
    g1, g2 = whole(norm1_gain), whole(norm2_gain)
    bias = whole(up_bias)
    router = whole(router_weight)
    parts = [whole(query_weight), whole(key_value_weight), jnp.pad(router, ((0, 0), (0, 120))),
             whole(output_weight), whole(up_weight)]
    wa = jnp.concatenate(parts, axis=1)
    wd = whole(down_weight)
    v = pl.BlockSpec(memory_space=pltpu.VMEM)
    h = pl.BlockSpec(memory_space=pl.ANY)
    sd = jax.ShapeDtypeStruct
    y, dx, ga, gd, small, biasg = pl.pallas_call(
        local_kernel,
        out_shape=(sd((tokens, width), F32), sd((tokens, width), F32), sd((512, CW), BF), sd((2048, 512), BF),
                   sd((8, 512), F32), sd((1, 2048), F32)),
        in_specs=[h, h] + [v] * 8,
        out_specs=(h, h, v, v, v, v),
        scratch_shapes=scratch(tokens) + [pltpu.SemaphoreType.DMA((4,))],
        compiler_params=pltpu.CompilerParams(vmem_limit_bytes=63 * 2**20),
    )(
        inputs.reshape(tokens, width), cotangent.reshape(tokens, width), segment_ids,
        jnp.swapaxes(expert_ids, 1, 2), jnp.swapaxes(overflow, 1, 2),
        g1.astype(F32)[None], g2.astype(F32)[None], bias.astype(F32)[None], wa, wd,
    )
    total = lambda v: lax.psum_scatter(v.astype(F32), AXES, scatter_dimension=0, tiled=True)
    return (
        y.reshape(inputs.shape), dx.reshape(inputs.shape),
        total(small[0]), total(ga[:, CR : CR + 8]), total(ga[:, CQ:CKV]), total(ga[:, CKV:CR]),
        total(ga[:, CO:CU]), total(small[1]), total(ga[:, CU:]), total(biasg[0]), total(gd),
    )


def solution(mesh):
    row3, row2, row1 = P(AXES, None, None), P(AXES, None), P(AXES)
    in_specs = (row3, row3, row2, row3, row3, row1, row2, row2, row2, row2, row1, row2, row1, row2)
    out_specs = (row3, row3, row1, row2, row2, row2, row2, row1, row2, row1, row2)
    small = mesh.shape['dp'] == 4 and mesh.shape['fsdp'] == 8
    shards = shards_mega if small else shards_local
    return jax.shard_map(shards, mesh=mesh, in_specs=in_specs, out_specs=out_specs, check_vma=False)
```

```python
import functools
import jax
import jax.numpy as jnp
from jax import lax
from jax.experimental import pallas as pl
from jax.experimental.pallas import tpu as pltpu
from jax.sharding import PartitionSpec as P

EPS = 1e-05
BIG = -1e30
GELU_C = 0.7978845608028654
GELU_K = 0.044715
BF = jnp.bfloat16
F32 = jnp.float32
AXES = ("dp", "fsdp")
VLIM = 60293120
CQ, CKV, CR, CO, CU, CW = 0, 512, 640, 768, 1280, 3328
TILES = ((0, 128, 0), (128, 256, 256), (128, 384, 768), (256, 256, 1536))


def nn(a, b):
    return lax.dot_general(a, b, (((1,), (0,)), ((), ())), preferred_element_type=F32)


def nt(a, b):
    return lax.dot_general(a, b, (((1,), (1,)), ((), ())), preferred_element_type=F32)


def tn(a, b):
    return lax.dot_general(a, b, (((0,), (0,)), ((), ())), preferred_element_type=F32)


def split(v):
    high = v.astype(BF)
    return high, (v - high.astype(F32)).astype(BF)


def lanes(shape):
    return lax.broadcasted_iota(jnp.int32, shape, len(shape) - 1)


def rows_of(shape):
    return lax.broadcasted_iota(jnp.int32, shape, len(shape) - 2)


def one_where(mask):
    return jnp.where(mask, 1.0, 0.0).astype(BF)


def norm(v):
    centred = v - jnp.mean(v, axis=-1, keepdims=True)
    inverse = lax.rsqrt(jnp.mean(centred * centred, axis=-1, keepdims=True) + EPS)
    return centred * inverse, inverse


def norm_back(grad, xhat, inverse, gain):
    scaled = grad * gain
    inner = (
        scaled
        - jnp.mean(scaled, axis=-1, keepdims=True)
        - xhat * jnp.mean(scaled * xhat, axis=-1, keepdims=True)
    )
    return inner * inverse


def gelu_both(x):
    square = x * x
    slope = (GELU_C * GELU_K) * square + GELU_C
    half = 0.5 * jnp.tanh(x * slope) + 0.5
    value = x * half
    return value, half + (value - value * half) * (6.0 * slope - 4.0 * GELU_C)


def stack_pairs(v):
    return jnp.concatenate([v[:, 128 * p : 128 * p + 128] for p in range(4)], axis=0)


class Plan:
    pass


def keys_of(s, win):
    kv, vk = s.kv[win, :], s.vk[win, :]
    low, zero = lanes(kv.shape) < 64, jnp.zeros_like(kv)
    return jnp.concatenate([jnp.where(low, kv, zero), jnp.where(low, zero, vk)], axis=0)


def values_of(s, win, extra_e, extra_o):
    kv, vk = s.kv[win, :], s.vk[win, :]
    low, zero = lanes(kv.shape) < 64, jnp.zeros_like(kv)
    even = jnp.concatenate([jnp.where(low, vk, zero), extra_e], axis=1)
    odd = jnp.concatenate([jnp.where(low, zero, kv), extra_o], axis=1)
    return jnp.concatenate([even, odd], axis=0)


def phase_norm1(s, r):
    rows = pl.ds(r * 512, 512)
    xhat, inverse = norm(s.x[rows, :])
    s.xh1[rows, :] = xhat
    s.gates[rows, :] = jnp.broadcast_to(inverse, (512, 128))


def phase_forward(s, r, hook=lambda i: None):
    rows = pl.ds(r * 512, 512)
    normed = (s.xh1[rows, :] * s.g1[...]).astype(BF)
    s.normed[rows, :] = normed
    proj = nn(normed, s.weight(CQ, CO))
    query = proj[:, :512].astype(BF)
    s.q[rows, :] = query
    pair = proj[:, CKV:CR].astype(BF).astype(F32)
    swapped = pltpu.roll(pair, 64, 1)
    low = lanes((512, 128)) < 64
    s.kv[rows, :] = jnp.where(low, pair * 0.125, pair).astype(BF)
    s.vk[rows, :] = jnp.where(low, swapped, swapped * 0.125).astype(BF)
    lane = lanes((512, 128))
    logits = jnp.where(lane < 8, proj[:, CR:CO], BIG)
    top = jnp.max(logits, axis=-1, keepdims=True)
    weights = jnp.exp(logits - top)
    prob = weights / jnp.sum(weights, axis=-1, keepdims=True)
    s.small[0:2, :] = jnp.where(s.over[r] == 0, s.ids[r], -1).astype(F32)
    s.small[2:3, :] = s.segs[pl.ds(r, 1), :].astype(F32)
    columns = s.small[...].T
    lane_f = lane.astype(F32)
    route = jnp.where(lane_f == columns[:, 0:1], 1.0, 0.0) + jnp.where(
        lane_f == columns[:, 1:2], 1.0, 0.0
    )
    mix = prob * route
    s.gates[rows, :] = jnp.where(lane == 8, s.gates[rows, :], mix + pltpu.roll(prob, 64, 1))
    seg_row = s.small[2:3, :]
    hook(0)
    for t, (start, width, at) in enumerate(TILES):
        q4 = stack_pairs(query[128 * t : 128 * t + 128])
        win = pl.ds(r * 512 + start, width)
        scores = nt(q4, keys_of(s, win))
        even, odd = scores[:, :width], scores[:, width:]
        if t:
            same = columns[128 * t : 128 * t + 128, 2:3] == seg_row[:, start : start + width]
            bias = jnp.where(same, 0.0, BIG)
            bias = jnp.concatenate([bias] * 4, axis=0)
            even, odd = even + bias, odd + bias
        even = jnp.exp(even - jnp.max(even, axis=-1, keepdims=True)).astype(BF)
        odd = jnp.exp(odd - jnp.max(odd, axis=-1, keepdims=True)).astype(BF)
        both = jnp.concatenate([even, odd], axis=1)
        s.pu[pl.ds(r * 512, 512), at : at + 2 * width] = both
        low_w = lanes((width, 128)) < 64
        one_e = jnp.where(low_w, 1.0, 0.0).astype(BF)
        one_o = jnp.where(low_w, 0.0, 1.0).astype(BF)
        out = nn(both, values_of(s, win, one_e, one_o))
        inverse = 1.0 / out[:, 128:]
        out = out[:, :128] * inverse
        for p in range(4):
            at_rows = pl.ds(r * 512 + 128 * t, 128)
            s.heads[at_rows, 128 * p : 128 * p + 128] = out[128 * p : 128 * p + 128]
            s.pinv[at_rows, 128 * p : 128 * p + 128] = inverse[128 * p : 128 * p + 128]
        hook(1 + t)
    mixed = (s.heads[rows, :] * expand(mix)).astype(BF)
    s.mixed[rows, :] = mixed
    hook(5)


def phase_resid(s, r):
    rows = pl.ds(r * 512, 512)
    resid = s.x[rows, :] + nn(s.mixed[rows, :], s.weight(CO, CU))
    s.x[rows, :] = resid
    xhat, inverse = norm(resid)
    s.xh2[rows, :] = xhat
    s.gates[rows, :] = jnp.where(lanes((512, 128)) == 9, inverse, s.gates[rows, :])
    s.normed2[rows, :] = (xhat * s.g2[...]).astype(BF)
    s.dffn[rows, :] = s.cotangent(rows).astype(BF)


def expand(per_expert):
    high, rest = split(per_expert)
    spread = one_where(
        jnp.bitwise_and(rows_of((256, 512)), 127) == jnp.right_shift(lanes((256, 512)), 6)
    )
    return nn(jnp.concatenate([high, rest], axis=1), spread)


def phase_ffn(s, c, r):
    rows = pl.ds(r * 512, 512)
    up = s.weight(CU + 512 * c, CU + 512 * c + 512)
    down = s.down(c)
    pre = nn(s.normed2[rows, :], up) + s.bias[:, 512 * c : 512 * c + 512]
    dhidden = nt(s.dffn[rows, :], down)
    value, slope = gelu_both(pre)
    dpre = dhidden * slope
    s.biasg[:, 512 * c : 512 * c + 512] += jnp.sum(dpre, axis=0, keepdims=True)
    hidden = value.astype(BF)
    dpre = dpre.astype(BF)
    s.hidden[rows, :] = hidden
    s.dpre[rows, :] = dpre
    s.x[rows, :] += nn(hidden, down)
    back = nt(dpre, up)
    if c == 0:
        s.dn2[rows, :] = back
    else:
        s.dn2[rows, :] += back


def phase_ffn_grads(s, c):
    s.put_down(c, tn(s.hidden[...], s.dffn[...]))
    s.put(CU + 512 * c, tn(s.normed2[...], s.dpre[...]))


def phase_norm2_back(s, r):
    rows = pl.ds(r * 512, 512)
    grad = s.dn2[rows, :]
    xhat = s.xh2[rows, :]
    s.gaing[1:2, :] += jnp.sum(grad * xhat, axis=0, keepdims=True)
    dresid = s.cotangent_row(r) + norm_back(grad, xhat, s.gates[rows, 9:10], s.g2[...])
    s.dn2[rows, :] = dresid
    dbranch = dresid.astype(BF)
    s.dbranch[rows, :] = dbranch


def phase_back(s, r, hook=lambda i: None):
    rows = pl.ds(r * 512, 512)
    dmixed = nt(s.dbranch[rows, :], s.weight(CO, CU))
    heads = s.heads[rows, :]
    gather = one_where(
        lanes((1024, 128)) == jnp.right_shift(jnp.bitwise_and(rows_of((1024, 128)), 511), 6)
    )
    dgate = nn(jnp.concatenate(split(dmixed * heads), axis=1), gather)
    gates = s.gates[rows, :]
    first8 = lanes((512, 128)) < 8
    mix = jnp.where(first8, gates, 0.0)
    prob = jnp.where(first8, pltpu.roll(gates, 64, 1), 0.0)
    weighted = dgate * mix
    dlogits = weighted - prob * jnp.sum(weighted, axis=-1, keepdims=True)
    s.dkr[rows, 128:256] = dlogits.astype(BF)
    dout = (dmixed * expand(mix) * s.pinv[rows, :]).astype(BF)
    s.dout[...] = dout
    within = dout.astype(F32) * heads
    high, rest = split(within)
    block = one_where(
        jnp.right_shift(jnp.bitwise_and(rows_of((256, 128)), 127), 6)
        == jnp.right_shift(lanes((256, 128)), 6)
    )
    place = jnp.bitwise_and(lanes((512, 128)), 63)
    for p in range(4):
        cols = slice(128 * p, 128 * p + 128)
        total = nn(jnp.concatenate([high[:, cols], rest[:, cols]], axis=1), block)
        first, second = split(total)
        s.delta[:, cols] = jnp.where(
            place == 0, first.astype(F32), jnp.where(place == 1, second.astype(F32), 0.0)
        ).astype(BF)
    s.dkv[...] = jnp.zeros_like(s.dkv)
    hook(0)
    for t, (start, width, at) in enumerate(TILES):
        here = pl.ds(128 * t, 128)
        at_rows = pl.ds(r * 512 + 128 * t, 128)
        win = pl.ds(r * 512 + start, width)
        do4 = stack_pairs(s.dout[here, :])
        de4 = stack_pairs(s.delta[here, :])
        lane = lanes((width, 128))
        neg_e = jnp.where(lane < 2, -1.0, 0.0).astype(BF)
        neg_o = jnp.where(jnp.bitwise_and(lane, 126) == 64, -1.0, 0.0).astype(BF)
        dprob = nt(jnp.concatenate([do4, de4], axis=1), values_of(s, win, neg_e, neg_o))
        weights = s.pu[pl.ds(r * 512, 512), at : at + 2 * width]
        dscore = (weights.astype(F32) * dprob).astype(BF)
        dq4 = nn(dscore, keys_of(s, win)).astype(BF)
        q4 = stack_pairs(s.q[at_rows, :])
        dk = tn(dscore, q4)
        dv = tn(weights, do4)
        for p in range(4):
            s.q[at_rows, 128 * p : 128 * p + 128] = dq4[128 * p : 128 * p + 128]
        s.dkv[pl.ds(start, width), :] += jnp.where(
            lane < 64,
            (dk[:width] + pltpu.roll(dk[width:], 64, 1)) * 0.125,
            dv[width:] + pltpu.roll(dv[:width], 64, 1),
        )
        if t < 3:
            hook(1 + t)
    s.dkr[rows, 0:128] = s.dkv[...].astype(BF)
    hook(4)


def phase_input(s, r):
    rows = pl.ds(r * 512, 512)
    dproj = jnp.concatenate([s.q[rows, :], s.dkr[rows, :]], axis=1)
    grad = nt(dproj, s.weight(CQ, CO))
    xhat = s.xh1[rows, :]
    s.gaing[0:1, :] += jnp.sum(grad * xhat, axis=0, keepdims=True)
    s.dn2[rows, :] += norm_back(grad, xhat, s.gates[rows, 8:9], s.g1[...])


def local_kernel(
    x_in, cot_in, segs, ids, over, g1, g2, bias, wa, wd,
    out_y, out_dx, out_ga, out_gd, out_small, out_bias,
    x, cot, xh1, xh2, heads, pinv, dn2, normed, q, mixed, normed2, dffn, hidden, dpre,
    kv, vk, gates, pu, block, small, gaing, biasg, sem,
):
    s = Plan()
    s.x, s.xh1, s.xh2, s.heads, s.pinv, s.dn2 = x, xh1, xh2, heads, pinv, dn2
    s.cotangent = lambda rows: cot[rows, :]
    s.cotangent_row = lambda r: cot[pl.ds(r * 512, 512), :]
    s.normed, s.q, s.mixed, s.normed2, s.dffn, s.hidden, s.dpre = normed, q, mixed, normed2, dffn, hidden, dpre
    s.kv, s.vk, s.gates, s.pu, s.dkv = kv, vk, gates, pu, block
    s.small, s.gaing, s.biasg, s.segs, s.ids, s.over = small, gaing, biasg, segs, ids, over
    s.g1, s.g2, s.bias = g1, g2, bias
    s.dbranch = s.dffn
    s.dkr = hidden.at[:, 0:256]
    s.dout, s.delta = dpre.at[0:512, :], dpre.at[512:1024, :]
    s.weight = lambda a, b: wa[:, a:b]
    s.down = lambda c: wd[512 * c : 512 * c + 512, :]

    def put(at, value):
        out_ga[:, at : at + value.shape[1]] = value.astype(BF)

    def put_down(c, value):
        out_gd[512 * c : 512 * c + 512, :] = value.astype(BF)

    s.put, s.put_down = put, put_down
    copies = [pltpu.make_async_copy(x_in, x, sem.at[0]), pltpu.make_async_copy(cot_in, cot, sem.at[1])]
    for copy in copies:
        copy.start()
    small[...] = jnp.zeros_like(small)
    gaing[...] = jnp.zeros_like(gaing)
    biasg[...] = jnp.zeros_like(biasg)
    for copy in copies:
        copy.wait()
    nrows = x.shape[0] // 512

    def each(phase):
        lax.fori_loop(0, nrows, lambda r, _: (phase(r), 0)[1], 0)

    each(lambda r: phase_norm1(s, r))
    each(lambda r: phase_forward(s, r))
    each(lambda r: phase_resid(s, r))
    for c in range(4):
        each(lambda r: phase_ffn(s, c, r))
        phase_ffn_grads(s, c)
    finish = pltpu.make_async_copy(x, out_y, sem.at[2])
    finish.start()
    each(lambda r: phase_norm2_back(s, r))
    each(lambda r: phase_back(s, r))
    put(CO, tn(mixed[...], s.dbranch[...]))
    put(CQ, tn(normed[...], q[...]))
    put(CKV, tn(normed[...], s.dkr[...]))
    each(lambda r: phase_input(s, r))
    last = pltpu.make_async_copy(dn2, out_dx, sem.at[3])
    last.start()
    out_small[...] = gaing[...]
    out_bias[...] = biasg[...]
    finish.wait()
    last.wait()


def scratch(tokens):
    f = lambda *shape: pltpu.VMEM(shape, F32)
    b = lambda *shape: pltpu.VMEM(shape, BF)
    t = tokens
    return (
        [f(t, 512)] * 7 + [b(t, 512)] * 7 + [b(t, 128)] * 2
        + [f(t, 128), b(t, 2048), f(512, 128)]
        + [f(8, 512), f(8, 512), f(1, 2048)]
    )


MESH = pl.DeviceIdType.MESH


class Ring:
    def __init__(self):
        self.d = lax.axis_index("dp")
        self.f = lax.axis_index("fsdp")
        self.x, self.c = jnp.right_shift(self.d, 1), jnp.bitwise_and(self.d, 1)
        self.z, self.y = jnp.right_shift(self.f, 1), jnp.bitwise_and(self.f, 1)
        self.ox, self.oc, self.oy = 1 - self.x, 1 - self.c, 1 - self.y
        self.core_peer = (2 * self.x + self.oc, self.f)
        self.x_peer = (2 * self.ox + self.c, self.f)
        self.y_peer = (self.d, 2 * self.z + self.oy)
        self.far_peer = (2 * self.ox + self.c, 2 * self.z + self.oy)
        self.later = [jnp.bitwise_and(self.z + k, 3) for k in (1, 2, 3)]
        self.earlier = [jnp.bitwise_and(self.z - k + 4, 3) for k in (1, 2, 3)]
        self.z_peers = [(self.d, 2 * z + self.y) for z in self.later]


def remote(src, dst, send, recv, peer):
    return pltpu.make_async_remote_copy(
        src_ref=src, dst_ref=dst, send_sem=send, recv_sem=recv, device_id=peer, device_id_type=MESH
    )


class Gather:
    def __init__(self, ring, buf, kinds, send, recv):
        self.ring, self.buf, self.kinds, self.send, self.recv = ring, buf, kinds, send, recv
        self.all = slice(kinds[0][0], kinds[-1][1])

    def copies(self, k, arriving):
        g, b = self.ring, self.buf
        if k == 0:
            at = lambda z: b.at[g.x, g.c, z, g.y, :, self.all]
            moves = [(n, at(g.earlier[n] if arriving else g.z), g.z_peers[n]) for n in range(3)]
        elif k == 3:
            moves = [(7, b.at[:, g.oc if arriving else g.c, :, :, :, self.all], g.core_peer)]
        else:
            moves = []
            x, y = (g.ox, g.oy) if arriving else (g.x, g.y)
            for kind, (lo, hi) in enumerate(self.kinds):
                cols = slice(lo, hi)
                if k == 1:
                    if kind == 0:
                        moves.append((3, b.at[x, g.c, :, g.y, :, cols], g.x_peer))
                    else:
                        moves.append((4, b.at[g.x, g.c, :, y, :, cols], g.y_peer))
                elif kind == 0:
                    moves.append((5, b.at[:, g.c, :, y, :, cols], g.y_peer))
                else:
                    moves.append((6, b.at[x, g.c, :, :, :, cols], g.x_peer))
        return [remote(ref, ref, self.send.at[n], self.recv.at[n], peer) for n, ref, peer in moves]

    def step(self, k):
        if k > 0:
            for copy in self.copies(k - 1, True):
                copy.wait_recv()
        if k < 4:
            for copy in self.copies(k, False):
                copy.start()

    def finish(self):
        for k in range(4):
            for copy in self.copies(k, False):
                copy.wait_send()


class Reduce:
    def __init__(self, ring, buf, kinds, send, recv, landing, write):
        self.ring, self.buf, self.kinds, self.send, self.recv = ring, buf, kinds, send, recv
        self.first, self.halves, self.quarters, self.last = landing
        self.all = slice(kinds[0][0], kinds[-1][1])
        self.write = write

    def copies(self, k):
        g, b = self.ring, self.buf
        if k == 0:
            moves = [(0, b.at[:, g.oc, :, :, :, self.all], self.first, g.core_peer)]
        elif k == 3:
            moves = [
                (5 + n, b.at[g.x, g.c, g.later[n], g.y, :, self.all], self.last.at[n], g.z_peers[n])
                for n in range(3)
            ]
        else:
            moves = []
            for kind, (lo, hi) in enumerate(self.kinds):
                cols = slice(lo, hi)
                if k == 1:
                    if kind == 0:
                        moves.append((1, b.at[:, g.c, :, g.oy, :, cols], self.halves[0], g.y_peer))
                    else:
                        moves.append((2, b.at[g.ox, g.c, :, :, :, cols], self.halves[1], g.x_peer))
                elif kind == 0:
                    moves.append((3, b.at[g.ox, g.c, :, g.y, :, cols], self.quarters[0], g.x_peer))
                else:
                    moves.append((4, b.at[g.x, g.c, :, g.oy, :, cols], self.quarters[1], g.y_peer))
        return [remote(src, dst, self.send.at[n], self.recv.at[n], peer) for n, src, dst, peer in moves]

    def add(self, k):
        g, b = self.ring, self.buf
        if k == 0:
            b[:, g.c, :, :, :, self.all] += self.first[...]
        elif k == 3:
            total = b[g.x, g.c, g.z, g.y, :, self.all].astype(F32)
            for n in range(3):
                total = total + self.last[n].astype(F32)
            self.write(total)
        else:
            for kind, (lo, hi) in enumerate(self.kinds):
                if k == 2:
                    b[g.x, g.c, :, g.y, :, lo:hi] += self.quarters[kind][...]
                elif kind == 0:
                    b[:, g.c, :, g.y, :, lo:hi] += self.halves[0][...]
                else:
                    b[g.x, g.c, :, :, :, lo:hi] += self.halves[1][...]

    def step(self, k):
        if k > 0:
            for copy in self.copies(k - 1):
                copy.wait_recv()
            self.add(k - 1)
        if k < 4:
            for copy in self.copies(k):
                copy.start()

    def finish(self):
        for k in range(4):
            for copy in self.copies(k):
                copy.wait_send()


class GatherShort(Gather):
    def copies(self, k, arriving):
        g, b = self.ring, self.buf
        if k == 0:
            return Gather.copies(self, 0, arriving)
        if k == 2:
            return Gather.copies(self, 3, arriving)
        moves = []
        for n, x, y, peer in ((3, g.ox, g.y, g.x_peer), (4, g.x, g.oy, g.y_peer), (5, g.ox, g.oy, g.far_peer)):
            at = (x, y) if arriving else (g.x, g.y)
            moves.append((n, b.at[at[0], g.c, :, at[1], :, self.all], peer))
        return [remote(ref, ref, self.send.at[n], self.recv.at[n], peer) for n, ref, peer in moves]

    def step(self, k):
        if k > 0:
            for copy in self.copies(k - 1, True):
                copy.wait_recv()
        if k < 3:
            for copy in self.copies(k, False):
                copy.start()

    def finish(self):
        for k in range(3):
            for copy in self.copies(k, False):
                copy.wait_send()


class GatherOne:
    def __init__(self, ring, buf, z, send, recv):
        self.ring, self.buf, self.z, self.send, self.recv = ring, buf, z, send, recv

    def spread(self):
        g, b = self.ring, self.buf.at[self.ring.x, self.ring.c, self.z, self.ring.y]
        return [remote(b, b, self.send.at[n], self.recv.at[0], g.z_peers[n]) for n in range(3)]

    def copies(self, k, arriving):
        g, b, z = self.ring, self.buf, self.z
        x, y, c = (g.ox, g.oy, g.oc) if arriving else (g.x, g.y, g.c)
        low, high = slice(0, 256), slice(256, 512)
        if k == 1:
            moves = [
                (3, b.at[x, g.c, z, g.y, :, low], g.x_peer), (4, b.at[g.x, g.c, z, y, :, high], g.y_peer),
            ]
        elif k == 2:
            moves = [
                (5, b.at[:, g.c, z, y, :, low], g.y_peer), (6, b.at[x, g.c, z, :, :, high], g.x_peer),
            ]
        else:
            moves = [(7, b.at[:, c, z], g.core_peer)]
        return [remote(ref, ref, self.send.at[n], self.recv.at[n], peer) for n, ref, peer in moves]

    def step(self, k):
        if k == 0:
            @pl.when(self.ring.z == self.z)
            def _():
                for copy in self.spread():
                    copy.start()
        if k == 1:
            @pl.when(self.ring.z != self.z)
            def _():
                self.spread()[0].wait_recv()
        if k > 1:
            for copy in self.copies(k - 1, True):
                copy.wait_recv()
        if 0 < k < 4:
            for copy in self.copies(k, False):
                copy.start()

    def finish(self):
        @pl.when(self.ring.z == self.z)
        def _():
            for copy in self.spread():
                copy.wait_send()

        for k in (1, 2, 3):
            for copy in self.copies(k, False):
                copy.wait_send()


class ReduceOne:
    def __init__(self, ring, buf, z, send, recv, landing, write):
        self.ring, self.buf, self.z, self.send, self.recv = ring, buf, z, send, recv
        self.first, self.halves, self.quarters, self.last = landing
        self.write = write

    def copies(self, k):
        g, b, z = self.ring, self.buf, self.z
        low, high = slice(0, 256), slice(256, 512)
        if k == 0:
            moves = [(0, b.at[:, g.oc, z], self.first, g.core_peer)]
        elif k == 1:
            moves = [
                (1, b.at[:, g.c, z, g.oy, :, low], self.halves[0], g.y_peer),
                (2, b.at[g.ox, g.c, z, :, :, high], self.halves[1], g.x_peer),
            ]
        else:
            moves = [
                (3, b.at[g.ox, g.c, z, g.y, :, low], self.quarters[0], g.x_peer),
                (4, b.at[g.x, g.c, z, g.oy, :, high], self.quarters[1], g.y_peer),
            ]
        return [remote(src, dst, self.send.at[n], self.recv.at[n], peer) for n, src, dst, peer in moves]

    def collect(self, sender):
        g = self.ring
        slot = jnp.bitwise_and(sender - self.z + 3, 3)
        return remote(
            self.buf.at[g.x, g.c, self.z, g.y], self.last.at[slot], self.send.at[5], self.recv.at[5 + slot],
            (g.d, 2 * self.z + g.y),
        )

    def step(self, k):
        g, b, z = self.ring, self.buf, self.z
        low, high = slice(0, 256), slice(256, 512)
        if 0 < k < 4:
            for copy in self.copies(k - 1):
                copy.wait_recv()
        if k == 1:
            b[:, g.c, z] += self.first[...]
        if k == 2:
            b[:, g.c, z, g.y, :, low] += self.halves[0][...]
            b[g.x, g.c, z, :, :, high] += self.halves[1][...]
        if k == 3:
            b[g.x, g.c, z, g.y, :, low] += self.quarters[0][...]
            b[g.x, g.c, z, g.y, :, high] += self.quarters[1][...]

            @pl.when(g.z != z)
            def _():
                self.collect(g.z).start()
        if k < 3:
            for copy in self.copies(k):
                copy.start()
        if k == 4:
            @pl.when(g.z == z)
            def _():
                total = b[g.x, g.c, z, g.y].astype(F32)
                for n in range(3):
                    self.collect((z + 1 + n) % 4).wait_recv()
                    total = total + self.last[n].astype(F32)
                self.write(total)

    def finish(self):
        for k in range(3):
            for copy in self.copies(k):
                copy.wait_send()

        @pl.when(self.ring.z != self.z)
        def _():
            self.collect(self.ring.z).wait_send()


class ReduceShort:
    def __init__(self, ring, buf, cols, send, recv, landing, write):
        self.ring, self.buf, self.all, self.send, self.recv = ring, buf, slice(*cols), send, recv
        self.first, self.last, self.plane = landing
        self.write = write

    def copies(self, k):
        g, b = self.ring, self.buf
        if k == 0:
            moves = [(0, b.at[:, g.oc, :, :, :, self.all], self.first, g.core_peer)]
        elif k == 1:
            moves = [
                (1, b.at[g.ox, g.c, :, g.y, :, self.all], self.plane.at[0], g.x_peer),
                (2, b.at[g.x, g.c, :, g.oy, :, self.all], self.plane.at[1], g.y_peer),
                (3, b.at[g.ox, g.c, :, g.oy, :, self.all], self.plane.at[2], g.far_peer),
            ]
        else:
            moves = [
                (5 + n, b.at[g.x, g.c, g.later[n], g.y, :, self.all], self.last.at[n], g.z_peers[n])
                for n in range(3)
            ]
        return [remote(src, dst, self.send.at[n], self.recv.at[n], peer) for n, src, dst, peer in moves]

    def step(self, k):
        g, b = self.ring, self.buf
        if k > 0:
            for copy in self.copies(k - 1):
                copy.wait_recv()
        if k == 1:
            b[:, g.c, :, :, :, self.all] += self.first[...]
        if k > 1:
            mine = (g.x, g.c, slice(None), g.y) if k == 2 else (g.x, g.c, g.z, g.y)
            total = b[(*mine, slice(None), self.all)].astype(F32)
            for n in range(3):
                total = total + (self.plane if k == 2 else self.last)[n].astype(F32)
            if k == 2:
                b[(*mine, slice(None), self.all)] = total.astype(BF)
            else:
                self.write(total)
        if k < 3:
            for copy in self.copies(k):
                copy.start()

    def finish(self):
        for k in range(3):
            for copy in self.copies(k):
                copy.wait_send()


def landing_shapes(rows, kinds):
    b = lambda *shape: pltpu.VMEM(shape, BF)
    if isinstance(kinds, int):
        return [
            b(2, 2, rows, 512), b(3, rows, 512), b(2, rows, 256), b(rows, 256), b(2, rows, 256), b(rows, 256),
        ]
    if isinstance(kinds[0], int):
        n = kinds[1] - kinds[0]
        return [b(2, 4, 2, rows, n), b(3, rows, n), b(3, 4, rows, n)]
    n = kinds[-1][1] - kinds[0][0]
    shapes = [b(2, 4, 2, rows, n), b(3, rows, n)]
    for kind, (lo, hi) in enumerate(kinds):
        shapes.append(b(2, 4, rows, hi - lo) if kind == 0 else b(4, 2, rows, hi - lo))
        shapes.append(b(4, rows, hi - lo))
    return shapes


def halves(lo, hi, cut=None):
    cut = (lo + hi) // 2 if cut is None else cut
    return ((lo, cut), (cut, hi))


GATHERS = (
    ("P0", halves(CQ, CO)), ("P1", halves(CO, CU)), ("U0", halves(CU, CU + 512)), ("D0", 0),
    ("U1", halves(CU + 512, CU + 1024)), ("D1", 1), ("U2", halves(CU + 1024, CW)), ("D2", 2), ("D3", 3),
)
REDUCES = (
    ("u0", halves(CU, CU + 512)), ("u1", halves(CU + 512, CU + 1024)),
    ("u2", halves(CU + 1024, CU + 1536)), ("u3", halves(CU + 1536, CW)),
    ("d0", 0), ("d1", 1), ("d2", 2), ("d3", 3), ("o", (CO, CU)),
    ("q", (CQ, CR)), ("r", (CR, CO)),
)
SHARED = {"d2": "d0", "d3": "d1"}
SCHEDULE = {
    "go": (("P0", 0),),
    "P0": (("P0", 1), ("P1", 0), ("U0", 0), ("D0", 0), ("P0", 2), ("U1", 0), ("D1", 0), ("P1", 1), ("U0", 1), ("P0", 3),),
    "fwd0.3": (("D0", 1), ("U2", 0), ("D2", 0), ("D3", 0),),
    "fwd1.0": (("U1", 1),),
    "fwd1.3": (("P1", 2), ("U0", 2),),
    "fwd1.4": (("D1", 1),),
    "fwd2.1": (("D0", 2),),
    "fwd2.4": (("P1", 3), ("U1", 2),),
    "res.0": (("U2", 1),),
    "ffn0": (("U0", 3), ("D2", 1), ("D1", 2), ("D0", 3), ("U0", 4), ("U1", 3), ("D3", 1), ("D0", 4),),
    "ffn0.1": (("U2", 2),),
    "ffn0.2": (("U1", 4), ("D2", 2),),
    "grads0": (("d0", 0), ("u0", 0), ("D1", 3), ("D3", 2),),
    "ffn1": (("d0", 1), ("U2", 3), ("u0", 1), ("D2", 3), ("D1", 4),),
    "ffn1.2": (("D3", 3), ("U2", 4), ("D2", 4),),
    "grads1": (("d1", 0), ("u1", 0), ("d0", 2), ("u0", 2),),
    "ffn2.0": (("D3", 4),),
    "ffn2.1": (("d1", 1), ("u1", 1),),
    "grads2": (("d2", 0), ("u2", 0), ("d0", 3), ("u0", 3),),
    "ffn3.1": (("d1", 2), ("d2", 1), ("u1", 2), ("u2", 1),),
    "grads3": (("d3", 0), ("u3", 0), ("d1", 3), ("d0", 4),),
    "back0.0": (("d2", 2), ("u0", 4), ("u1", 3), ("d3", 1),),
    "back0.4": (("u3", 1), ("u2", 2),),
    "og": (("o", 0), ("d2", 3), ("d1", 4), ("d3", 2), ("u1", 4),),
    "back1.4": (("u3", 2), ("u2", 3), ("o", 1),),
    "back2.0": (("d3", 3),),
    "back2.4": (("d2", 4), ("u3", 3),),
    "qg": (("q", 0), ("u2", 4),),
    "inp.0": (("o", 2),),
    "inp.1": (("q", 1),),
    "end": (("r", 0), ("d3", 4), ("u3", 4), ("r", 1), ("o", 3), ("q", 2), ("r", 2), ("q", 3), ("r", 3),),
}


def mega_kernel(
    x_in, cot_in, segs_in, ids_in, over_in, g1_in, g2_in, bias_in, router_in, q_in, kv_in, o_in, up_in, down_in,
    x, dn2, out_g1, out_router, out_q, out_kv, out_o, out_g2, out_up, out_bias, out_down,
    xh1, xh2, heads, pinv, normed, q, mixed, normed2, dffn, hidden, dpre,
    kv, vk, gates, pu, block, small, gaing, biasg,
    sem, cot_row, segs, ids, over, small_in, router_at, bias_at, wa, wd, ga, gd, g1, g2, bias, tiny, ag_send, ag_recv, rs_send, rs_recv, *landing,
):
    s = Plan()
    s.x, s.xh1, s.xh2, s.heads, s.pinv, s.dn2 = x, xh1, xh2, heads, pinv, dn2
    s.cotangent = lambda rows: dn2[rows, :]

    def fetch_row(r):
        return pltpu.make_async_copy(cot_in.at[512 * r : 512 * r + 512], cot_row, sem.at[17 + r])

    def cotangent_row(r):
        fetch_row(r).wait()
        return cot_row[...]

    s.cotangent_row = cotangent_row
    s.normed, s.q, s.mixed, s.normed2, s.dffn, s.hidden, s.dpre = normed, q, mixed, normed2, dffn, hidden, dpre
    s.kv, s.vk, s.gates, s.pu, s.dkv = kv, vk, gates, pu, block
    s.small, s.gaing, s.biasg, s.segs, s.ids, s.over = small, gaing, biasg, segs, ids, over
    s.g1, s.g2, s.bias = g1, g2, bias
    s.dbranch = s.dffn
    s.dkr = hidden.at[:, 0:256]
    s.dout, s.delta = dpre.at[0:512, :], dpre.at[512:1024, :]
    s.weight = lambda a, b: wa[:, :, :, :, :, a:b].reshape(512, b - a)
    s.down = lambda c: wd[:, :, c].reshape(512, 512)

    def put(at, value):
        n = value.shape[1]
        ga[:, :, :, :, :, at : at + n] = value.astype(BF).reshape(2, 2, 4, 2, 16, n)

    def put_down(c, value):
        gd[:, :, c] = value.astype(BF).reshape(2, 2, 2, 64, 512)

    s.put, s.put_down = put, put_down
    g = Ring()
    peers = [g.core_peer, g.x_peer, g.y_peer, g.far_peer] + g.z_peers
    barrier = pltpu.get_barrier_semaphore()
    for peer in peers:
        pl.semaphore_signal(barrier, inc=1, device_id=peer, device_id_type=MESH)
    moves = [
        (q_in, dn2.at[0:16]), (o_in, dn2.at[16:32]), (kv_in, dn2.at[32:48, 0:128]), (down_in, dn2.at[128:192]),
        (router_in, router_at), (g1_in, small_in.at[0:1]), (g2_in, small_in.at[8:9]), (bias_in, bias_at),
    ]
    moves += [
        (up_in.at[:, 512 * k : 512 * k + 512], dn2.at[48 + 16 * k : 64 + 16 * k]) for k in range(4)
    ]
    moves += [(x_in, x), (segs_in, segs), (ids_in, ids), (over_in, over), (cot_in, dn2)]
    copies = [pltpu.make_async_copy(src, dst, sem.at[n]) for n, (src, dst) in enumerate(moves)]
    for copy in copies[:16]:
        copy.start()
    for copy in copies[:12]:
        copy.wait()

    wa[g.x, g.c, g.z, g.y, :, CQ:CKV] = dn2[0:16, :].astype(BF)
    wa[g.x, g.c, g.z, g.y, :, CKV:CR] = dn2[32:48, 0:128].astype(BF)
    wa[g.x, g.c, g.z, g.y, :, CO:CU] = dn2[16:32, :].astype(BF)
    for k in range(16):
        at = CU + 512 * (k % 4) + 128 * (k // 4)
        wa[g.x, g.c, g.z, g.y, :, at : at + 128] = dn2[
            48 + 16 * (k // 4) : 64 + 16 * (k // 4), 128 * (k % 4) : 128 * (k % 4) + 128
        ].astype(BF)
    wd[g.x, g.c, g.z, g.y] = dn2[128:192, :].astype(BF)
    tiny[...] = jnp.zeros_like(tiny)
    tiny[0:8, 0:16] = router_at[...]
    tiny[8:9, 0:16] = small_in[0:1]
    tiny[9:10, 0:16] = small_in[8:9]
    tiny[16:17, 0:64] = bias_at[...]
    turned = tn(
        tiny[0:16, :].astype(BF), one_where(rows_of((16, 128)) == lanes((16, 128)))
    )[0:16]
    shifted = nn(tiny[16:32, :].astype(BF), one_where(rows_of((128, 128)) + 64 == lanes((128, 128))))
    wa[g.x, g.c, g.z, g.y, :, CR:CO] = (turned + shifted).astype(BF)

    copies[16].start()
    pl.semaphore_wait(barrier, len(peers))
    parts = {}
    for k, (name, kinds) in enumerate(GATHERS):
        make, buf = (GatherOne, wd) if name[0] == "D" else (GatherShort if name in ("P0", "P1") else Gather, wa)
        parts[name] = make(g, buf, kinds, ag_send.at[k], ag_recv.at[k])

    def write_to(ref, at=0):
        def write(total):
            ref[:, at : at + total.shape[1]] = total

        return write

    def write_q(total):
        out_q[...] = total[:, :512]
        out_kv[...] = total[:, 512:]

    def write_small(total):
        turned = total.T
        out_router[...] = turned[0:8]
        out_g1[...] = turned[8:9]
        out_g2[...] = turned[9:10]
        out_bias[...] = pltpu.roll(total, 64, 1)[0:1, 0:64]

    def write_up(c):
        def write(total):
            for k in range(4):
                at = 512 * k + 128 * c
                out_up[:, at : at + 128] = total[:, 128 * k : 128 * k + 128]

        return write

    writes = [write_up(c) for c in range(4)] + [write_to(out_down)] * 4 + [write_to(out_o), write_q, write_small]
    spots = list(landing)
    for k, (name, kinds) in enumerate(REDUCES):
        first = parts[SHARED[name]].first if name in SHARED else spots.pop(0)
        last = spots.pop(0)
        if name in ("o", "q", "r"):
            parts[name] = ReduceShort(
                g, ga, kinds, rs_send.at[k], rs_recv.at[k], (first, last, spots.pop(0)), writes[k]
            )
            continue
        halves_in, quarters_in = [], []
        for _ in range(2 if isinstance(kinds, int) else len(kinds)):
            halves_in.append(spots.pop(0))
            quarters_in.append(spots.pop(0))
        make, buf = (ReduceOne, gd) if name[0] == "d" else (Reduce, ga)
        parts[name] = make(
            g, buf, kinds, rs_send.at[k], rs_recv.at[k],
            (first, halves_in, quarters_in, last), writes[k],
        )

    def hook(name):
        for part, k in SCHEDULE.get(name, ()):
            parts[part].step(k)

    hook("go")
    small[...] = jnp.zeros_like(small)
    gaing[...] = jnp.zeros_like(gaing)
    biasg[...] = jnp.zeros_like(biasg)
    nrows = x.shape[0] // 512

    def each(phase, name):
        def body(r, _):
            phase(r)
            for k in range(nrows):
                if SCHEDULE.get(name + "." + str(k)):
                    pl.when(r == k)(lambda k=k: hook(name + "." + str(k)))
            return 0

        lax.fori_loop(0, nrows, body, 0)

    copies[12].wait()
    each(lambda r: phase_norm1(s, r), "norm")
    hook("P0")
    block[...] = s.weight(CR, CO).astype(F32)
    turned = block[...].T
    g1[...] = turned[8:9]
    g2[...] = turned[9:10]
    even = block[pl.ds(0, 16, stride=32), :]
    odd = block[pl.ds(16, 16, stride=32), :]
    both = jnp.where(lanes((16, 128)) < 64, pltpu.roll(even, 64, 1), odd)
    for k in range(16):
        at = 512 * (k % 4) + 128 * (k // 4)
        bias[:, at : at + 128] = both[k : k + 1]
    for copy in copies[13:]:
        copy.wait()
    for r in range(nrows):
        phase_forward(s, r, lambda i, r=r: hook("fwd" + str(r) + "." + str(i)))
    hook("P1")
    each(lambda r: phase_resid(s, r), "res")
    fetch_row(0).start()
    for c in range(4):
        hook("ffn" + str(c))
        each(lambda r, c=c: phase_ffn(s, c, r), "ffn" + str(c))
        phase_ffn_grads(s, c)
        hook("grads" + str(c))
    def norm2_back(r):
        phase_norm2_back(s, r)
        if r + 1 < nrows:
            fetch_row(r + 1).start()
        else:
            put(CO, tn(mixed[...], s.dbranch[...]))
            hook("og")

    def back_hook(r, i):
        if i == 0 and r > 0:
            for later in range(r + 1, nrows):
                if later > done[-1]:
                    done.append(later)
                    norm2_back(later)
        hook("back" + str(r) + "." + str(i))

    done = [0]
    norm2_back(0)
    for r in range(nrows):
        if r > done[-1]:
            done.append(r)
            norm2_back(r)
        phase_back(s, r, functools.partial(back_hook, r))
    put(CQ, tn(normed[...], q[...]))
    kvr = tn(normed[...], s.dkr[...])
    put(CKV, kvr[:, :128])
    block[...] = kvr[:, 128:]
    hook("qg")
    each(lambda r: phase_input(s, r), "inp")
    turned = gaing[...].T
    lane = lanes((512, 128))
    block[...] = jnp.where(
        lane == 8, turned[:, 0:1], jnp.where(lane == 9, turned[:, 1:2], block[...])
    )
    for k in range(16):
        at = 512 * (k % 4) + 128 * (k // 4)
        tiny[k : k + 1, :] = biasg[:, at : at + 128]
    pieces = tiny[0:16, :]
    low = lanes((16, 128)) < 64
    even = pl.ds(0, 16, stride=32)
    block[even, :] = jnp.where(low, block[even, :], pltpu.roll(pieces, 64, 1))
    odd = pl.ds(16, 16, stride=32)
    block[odd, :] = jnp.where(low, block[odd, :], pieces)
    put(CR, block[...])
    hook("end")
    for part in parts.values():
        part.finish()


def hand_on_kernel(*refs):
    n = len(refs) // 2
    copies = [pltpu.make_async_copy(refs[k], refs[n + k], refs[-1].at[k]) for k in range(n)]
    for copy in copies:
        copy.start()
    for copy in copies:
        copy.wait()


def shards_mega(inputs, cotangent, segment_ids, expert_ids, overflow, norm1_gain, router_weight,
                query_weight, key_value_weight, output_weight, norm2_gain, up_weight, up_bias, down_weight):
    nrows, length, width = inputs.shape
    tokens = nrows * length
    v = pl.BlockSpec(memory_space=pltpu.VMEM)
    h = pl.BlockSpec(memory_space=pl.ANY)
    sd = lambda *shape: jax.ShapeDtypeStruct(shape, F32)
    b = lambda *shape: pltpu.VMEM(shape, BF)
    f = lambda *shape: pltpu.VMEM(shape, F32)
    n = lambda *shape: pltpu.VMEM(shape, jnp.int32)
    landing = []
    for name, kinds in REDUCES:
        landing += landing_shapes(64 if name[0] == "d" else 16, kinds)[name in SHARED :]
    dma = pltpu.SemaphoreType.DMA
    out = pl.pallas_call(
        mega_kernel,
        out_shape=(
            f(tokens, width), f(tokens, width), f(1, 16), f(8, 16), f(16, 512), f(16, 128),
            f(16, 512), f(1, 16), f(16, 2048), f(1, 64), f(64, 512),
        ),
        in_specs=[h] * 14,
        out_specs=(v,) * 11,
        scratch_shapes=scratch(tokens)[2:6] + scratch(tokens)[7:] + [
            dma((20,)), f(512, 512), n(3, 512), n(3, 2, 512), n(3, 2, 512), f(16, 16), f(8, 16), f(1, 64), b(2, 2, 4, 2, 16, CW), b(2, 2, 4, 2, 64, 512), b(2, 2, 4, 2, 16, CW),
            b(2, 2, 4, 2, 64, 512), f(1, 512), f(1, 512), f(1, 2048), f(32, 128),
            dma((9, 8)), dma((9, 8)), dma((11, 8)), dma((11, 8)),
        ] + landing,
        compiler_params=pltpu.CompilerParams(
            collective_id=0, has_side_effects=True, vmem_limit_bytes=VLIM
        ),
    )(
        inputs.reshape(tokens, width), cotangent.reshape(tokens, width), segment_ids,
        jnp.swapaxes(expert_ids, 1, 2), jnp.swapaxes(overflow, 1, 2),
        norm1_gain[None], norm2_gain[None], up_bias[None], router_weight.T, query_weight, key_value_weight,
        output_weight, up_weight, down_weight,
    )
    y, dx, g1, router, query, pair, output, g2, up, bias, down = pl.pallas_call(
        hand_on_kernel,
        out_shape=tuple(sd(*o.shape) for o in out),
        in_specs=[h] * 11,
        out_specs=(h,) * 11,
        scratch_shapes=[dma((11,))],
        compiler_params=pltpu.CompilerParams(vmem_limit_bytes=32 * 1024),
    )(*out)
    return (
        y.reshape(inputs.shape), dx.reshape(inputs.shape), g1[0], router.T, query, pair, output, g2[0],
        up, bias[0], down,
    )


def shards_local(inputs, cotangent, segment_ids, expert_ids, overflow, norm1_gain, router_weight,
                 query_weight, key_value_weight, output_weight, norm2_gain, up_weight, up_bias, down_weight):
    nrows, length, width = inputs.shape
    tokens = nrows * length
    whole = lambda v: lax.all_gather(v.astype(BF), AXES, axis=0, tiled=True)
    g1, g2 = whole(norm1_gain), whole(norm2_gain)
    bias = whole(up_bias)
    router = whole(router_weight)
    parts = [whole(query_weight), whole(key_value_weight), jnp.pad(router, ((0, 0), (0, 120))),
             whole(output_weight), whole(up_weight)]
    wa = jnp.concatenate(parts, axis=1)
    wd = whole(down_weight)
    v = pl.BlockSpec(memory_space=pltpu.VMEM)
    h = pl.BlockSpec(memory_space=pl.ANY)
    sd = jax.ShapeDtypeStruct
    y, dx, ga, gd, small, biasg = pl.pallas_call(
        local_kernel,
        out_shape=(sd((tokens, width), F32), sd((tokens, width), F32), sd((512, CW), BF), sd((2048, 512), BF),
                   sd((8, 512), F32), sd((1, 2048), F32)),
        in_specs=[h, h] + [v] * 8,
        out_specs=(h, h, v, v, v, v),
        scratch_shapes=scratch(tokens) + [pltpu.SemaphoreType.DMA((4,))],
        compiler_params=pltpu.CompilerParams(vmem_limit_bytes=63 * 2**20),
    )(
        inputs.reshape(tokens, width), cotangent.reshape(tokens, width), segment_ids,
        jnp.swapaxes(expert_ids, 1, 2), jnp.swapaxes(overflow, 1, 2),
        g1.astype(F32)[None], g2.astype(F32)[None], bias.astype(F32)[None], wa, wd,
    )
    total = lambda v: lax.psum_scatter(v.astype(F32), AXES, scatter_dimension=0, tiled=True)
    return (
        y.reshape(inputs.shape), dx.reshape(inputs.shape),
        total(small[0]), total(ga[:, CR : CR + 8]), total(ga[:, CQ:CKV]), total(ga[:, CKV:CR]),
        total(ga[:, CO:CU]), total(small[1]), total(ga[:, CU:]), total(biasg[0]), total(gd),
    )


def solution(mesh):
    row3, row2, row1 = P(AXES, None, None), P(AXES, None), P(AXES)
    in_specs = (row3, row3, row2, row3, row3, row1, row2, row2, row2, row2, row1, row2, row1, row2)
    out_specs = (row3, row3, row1, row2, row2, row2, row2, row1, row2, row1, row2)
    small = mesh.shape['dp'] == 4 and mesh.shape['fsdp'] == 8
    shards = shards_mega if small else shards_local
    return jax.shard_map(shards, mesh=mesh, in_specs=in_specs, out_specs=out_specs, check_vma=False)
```
